128 devices in a mesh: dp: 32 (over y_hi, z, x), pipe: 4 (over y_lo, core).
Axes of the slice: x: 4, y: 4 (y_hi: 2, y_lo: 2; y = y_hi * 2 + y_lo), z: 4, core: 2. Of those that a mesh axis runs over, the one named last changes fastest.
Arguments:
- tokens: bfloat16 [8192, 768], P('dp'), may hold values from -6 to 6
- doc_ids: int32 [64, 128], P('dp'), may hold values from 0 to 3, never falling along the last dimension, each value on 1 to 80 neighbouring positions
- region_ids: int32 [64, 128], P('dp'), may hold values from 0 to 127, as said below
- proj: bfloat16 [4, 768, 3072], P('pipe', 'dp')
- down: bfloat16 [4, 1536, 768], P('pipe', 'dp'), may hold values from -0.15625 to 0.15625
- ln_gain: float32 [4, 768], P('pipe'), may hold values from 0.25 to 1.75
- ln_bias: float32 [4, 768], P('pipe'), may hold values from -3 to 3
- bn_gain: float32 [4, 768], P('pipe'), may hold values from 0.25 to 1.75
- bn_bias: float32 [4, 768], P('pipe'), may hold values from -3 to 3
- region_table: bfloat16 [4, 256, 768], P('pipe')
- out_cot: bfloat16 [8192, 768], P('dp'), may hold values from -6 to 6
Outputs:
- activations: bfloat16 [4, 8192, 768], P('pipe', 'dp')
- input_grads: bfloat16 [4, 8192, 768], P('pipe', 'dp')
- proj_grad: float32 [4, 768, 3072], P('pipe', 'dp')
- down_grad: float32 [4, 1536, 768], P('pipe', 'dp')
- ln_gain_grad: float32 [4, 768], P('pipe', 'dp')
- ln_bias_grad: float32 [4, 768], P('pipe', 'dp')
- bn_gain_grad: float32 [4, 768], P('pipe', 'dp')
- bn_bias_grad: float32 [4, 768], P('pipe', 'dp')
- region_table_grad: float32 [4, 256, 768], P('pipe', 'dp')
The draws below stay inside these ranges and needn't reach their ends.
Inputs may be any that keep to these rules, and one draw needn't show every extreme that they name: `doc_ids`: within each packed row the entries never fall; a document is a run of equal entries. `region_ids`: within each packed row the first entry is 0 and each next entry is the same or one more.
All inputs are finite; a program needn't handle non-finite values.
Results may differ from the reference program's by a relative error of at most 0.033.
Values may be sent and summed in bfloat16 or wider, within the bound.
A program may use at most 448 MiB of HBM per device.

```python
import math
import jax
import jax.numpy as jnp
import numpy as np
from jax import lax

D = 768
HEADS = 12
HEAD = 64
FF = 3072
SEQ = 128
NREG = 256
ROWS = 64
TOKENS = 8192
N_PIPE = 4


def draw_region_ids(key, part):
    key = jax.random.fold_in(key, 37)
    row_rank = jnp.arange(ROWS, dtype=jnp.int32)[:, None]
    start_level = 2 + 62 * row_rank // max(ROWS - 1, 1)
    coin_draws = jax.random.randint(key, (ROWS, SEQ), 0, 64, dtype=jnp.int32)
    starts = (coin_draws < start_level).astype(jnp.int32)
    position = jnp.arange(SEQ, dtype=jnp.int32)[None, :]
    starts = jnp.where(position == 0, 1, starts)
    return (jnp.cumsum(starts, axis=1) - 1).astype(jnp.int32)


def draw_proj(key, part):
    key = jax.random.fold_in(key, 11)
    base_draw = jax.random.normal(key, (N_PIPE, D, FF), jnp.float32)
    section_rank = jnp.arange(N_PIPE)[:, None, None]
    column = jnp.arange(FF)[None, None, :]
    boost_factor = jnp.where((section_rank % 2 == 0) & (column >= 3 * D), 6.0, 1.0)
    return (base_draw * boost_factor * float(D) ** (-0.5)).astype(jnp.bfloat16)


def draw_region_table(key, part):
    key = jax.random.fold_in(key, 23)
    row_rank = jnp.arange(NREG, dtype=jnp.float32)[None, :, None]
    base_draw = jax.random.normal(key, (N_PIPE, NREG, D), jnp.float32)
    row_scale = jnp.sqrt(1.0 + 12.0 * row_rank / NREG)
    return (base_draw * row_scale).astype(jnp.bfloat16)


def steps_of(rng, extent, pieces, least, high):
    def one(dim, shards_of):
        heights = jax.random.uniform(jax.random.fold_in(jax.random.fold_in(rng, 6), dim), (shards_of,), jnp.float32, least / len(pieces), high / len(pieces))
        return jnp.repeat(jnp.exp(heights), extent[dim] // shards_of).reshape((-1,) + (1,) * (len(extent) - dim - 1))

    loudness = one(*pieces[0])
    for cut in pieces[1:]:
        loudness = loudness * one(*cut)
    return loudness


def split_up(count, total, most, skew):
    weights = [(1 << 20) // math.isqrt(rank ** skew) + 1 for rank in range(2, count + 1)]
    surplus, holding = total - most - (count - 1), [1] * (count - 1)
    while surplus > 0:
        movable = [i for i in range(count - 1) if holding[i] < most]
        whole, left = sum([weights[i] for i in movable]), surplus
        for i in movable:
            more = min(most - holding[i], max(1, left * weights[i] // whole), surplus)
            holding[i] = holding[i] + more
            surplus = surplus - more
    return np.array([most] + holding)


def ragged_sizes(stream_key, count, total, reach, skew):
    if count == 2:
        one = jax.random.randint(stream_key, (), max(1, total - reach), min(reach, total - 1) + 1)
        return jnp.stack([one, total - one])
    sizes = jnp.asarray(split_up(count, total, reach, skew), jnp.int32)
    pairs = (count - 1) // 2
    source_of, receiver = sizes[1:1 + 2 * pairs:2], sizes[2:2 + 2 * pairs:2]
    room = jnp.minimum(source_of - 1, reach - receiver)
    shifted = jax.random.randint(jax.random.fold_in(stream_key, 1), (pairs,), 0, 1 << 20) % (room + 1)
    sizes = sizes.at[1:1 + 2 * pairs:2].set(source_of - shifted).at[2:2 + 2 * pairs:2].set(receiver + shifted)
    return sizes[jax.random.permutation(jax.random.fold_in(stream_key, 2), count)]


def bell_draw(rng, shape, width, limit, shards=(), kind=jnp.bfloat16):
    level = steps_of(rng, shape, shards, -0.22, 0.18) if shards else 1.0
    array = jax.random.normal(rng, shape, jnp.float32) * width * level
    return jnp.minimum(jnp.maximum(array, -limit), limit).astype(kind)


def setup_inputs(seed: int = 0) -> dict:
    streams_of = jax.random.split(jax.random.key(seed), 12)
    tokens = bell_draw(streams_of[0], (TOKENS, D), 1.0, 6.0, ((0, 32),))
    doc_ids = jax.vmap(lambda own: jnp.searchsorted(jnp.cumsum(ragged_sizes(own, 4, SEQ, SEQ * 5 // 8, 1)), jnp.arange(SEQ), side="right"))(jax.random.split(streams_of[1], ROWS)).reshape((ROWS, SEQ)).astype(jnp.int32)
    region_ids = draw_region_ids(jax.random.fold_in(streams_of[11], 71), 0)
    proj = draw_proj(jax.random.fold_in(streams_of[11], 71), 0)
    down = bell_draw(streams_of[4], (N_PIPE, FF // 2, D), (FF // 2) ** -0.5, 0.15625, ((0, 4), (1, 32)))
    ln_gain = jnp.clip(1.0 + 0.15 * jax.random.normal(streams_of[5], (N_PIPE, D), jnp.float32), 0.25, 1.75)
    ln_bias = bell_draw(streams_of[6], (N_PIPE, D), 0.3, 3.0, ((0, 4),), jnp.float32)
    bn_gain = jnp.clip(1.0 + 0.15 * jax.random.normal(streams_of[7], (N_PIPE, D), jnp.float32), 0.25, 1.75)
    bn_bias = bell_draw(streams_of[8], (N_PIPE, D), 0.5, 3.0, ((0, 4),), jnp.float32)
    region_table = draw_region_table(jax.random.fold_in(streams_of[11], 71), 0)
    out_cot = bell_draw(streams_of[10], (TOKENS, D), 1.0, 6.0, ((0, 32),))
    return {"tokens": tokens, "doc_ids": doc_ids, "region_ids": region_ids, "proj": proj, "down": down, "ln_gain": ln_gain, "ln_bias": ln_bias, "bn_gain": bn_gain, "bn_bias": bn_bias, "region_table": region_table, "out_cot": out_cot}


EPSILON = 1e-05
HIGH = lax.Precision.HIGHEST

@jax.custom_vjp
def low(v):
    return lax.optimization_barrier(v.astype(jnp.bfloat16)).astype(jnp.float32)

@jax.custom_vjp
def low_back(v):
    return v

def low_keep(v):
    return (low(v), None)

def low_pass(kept, grad):
    return (grad,)

def back_keep(v):
    return (v, None)

def back_low(kept, grad):
    return (low(grad),)
low.defvjp(low_keep, low_pass)
low_back.defvjp(back_keep, back_low)

def product(left, right):
    return jnp.dot(left, right, precision=HIGH, preferred_element_type=jnp.float32)

def layer_norm(residual, norm_gain, norm_shift):
    row_mean = lax.optimization_barrier(jnp.mean(residual, -1, keepdims=True))
    centered = residual - row_mean
    spread = lax.optimization_barrier(jnp.mean(centered * centered, -1, keepdims=True))
    return centered * lax.rsqrt(spread + EPSILON) * norm_gain + norm_shift

def attend_row(row_item):
    queries, key_rows, value_rows, doc_row = row_item
    scores = jnp.einsum('qhd,khd->hqk', queries, key_rows, precision=HIGH) * 0.125
    scores = low_back(scores)
    same_doc = doc_row[:, None] == doc_row[None, :]
    scores = jnp.where(same_doc[None], scores, -1e+30)
    attn_probs = low(jax.nn.softmax(scores, axis=-1))
    return jnp.einsum('hqk,khd->qhd', attn_probs, value_rows, precision=HIGH)

def attention_branch(lowered, weights, doc_ids):
    packed = low_back(low(product(lowered, weights[:, :3 * D])))
    row_shape = (ROWS, SEQ, HEADS, HEAD)
    queries = packed[:, :D].reshape(row_shape)
    key_rows = packed[:, D:2 * D].reshape(row_shape)
    value_rows = packed[:, 2 * D:].reshape(row_shape)
    mixed_heads = lax.map(jax.checkpoint(attend_row), (queries, key_rows, value_rows, doc_ids))
    mixed_heads = low_back(low(mixed_heads.reshape(TOKENS, D)))
    return low_back(product(mixed_heads, weights[:, 3 * D:]))

def feed_forward_branch(lowered, weights, down_rows):
    hidden = low_back(product(lowered, weights))
    activated = low(jax.nn.gelu(hidden, approximate=False))
    return low_back(product(activated, down_rows))

def run_section(section_rank, act_in, extra, proj, down, ln_gain, ln_bias, bn_gain, bn_bias, region_table, regions, doc_ids):
    embedded = region_table[section_rank][regions]
    region_mean = lax.optimization_barrier(jnp.mean(embedded, 0))
    second = lax.optimization_barrier(jnp.mean(embedded * embedded, 0))
    normed_region = (embedded - region_mean) * lax.rsqrt(second - region_mean * region_mean + EPSILON)
    summed = low_back(act_in + extra) + normed_region * bn_gain[section_rank] + bn_bias[section_rank]
    lowered = low(summed)
    if section_rank % 2 == 0:
        branch = attention_branch(lowered, proj[section_rank], doc_ids)
    else:
        down_rows = jnp.concatenate([down[section_rank - 1], down[section_rank]], 0)
        branch = feed_forward_branch(lowered, proj[section_rank], down_rows)
    return low(layer_norm(summed + branch, ln_gain[section_rank], ln_bias[section_rank]))

def reference(tokens, doc_ids, region_ids, proj, down, ln_gain, ln_bias, bn_gain, bn_bias, region_table, out_cot):
    regions = region_ids.reshape(-1)
    first_input = tokens.astype(jnp.float32)
    extras = jnp.zeros((N_PIPE, TOKENS, D), jnp.float32)
    section_fn = jax.checkpoint(run_section, static_argnums=(0,))

    def forward(proj_f, down_f, gain_f, shift_f, bn_gain_f, bn_bias_f, table_f, extra_all):
        activation = first_input
        kept_list = []
        for section_rank in range(N_PIPE):
            activation = section_fn(section_rank, activation, extra_all[section_rank], proj_f, down_f, gain_f, shift_f, bn_gain_f, bn_bias_f, table_f, regions, doc_ids)
            kept_list.append(activation)
        return (activation, jnp.stack(kept_list))
    final_out, pullback, kept_all = jax.vjp(forward, proj.astype(jnp.float32), down.astype(jnp.float32), ln_gain, ln_bias, bn_gain, bn_bias, region_table.astype(jnp.float32), extras, has_aux=True)
    gradients = pullback(out_cot.astype(jnp.float32))
    return (kept_all.astype(jnp.bfloat16), gradients[7].astype(jnp.bfloat16), gradients[0], gradients[1], gradients[2], gradients[3], gradients[4], gradients[5], gradients[6])
```

```python
from functools import partial

import jax
import jax.numpy as jnp
from jax import lax
from jax.experimental import pallas as pl
from jax.experimental.pallas import tpu as pltpu
from jax.sharding import PartitionSpec as P

HEADS = 12
FF = 3072
MICRO = 2
EPSILON = 1e-05
LOW = jnp.bfloat16
WIDE = jnp.float32
MESH = pl.DeviceIdType.MESH
DMA = pltpu.SemaphoreType.DMA
BLOCKS = 4
ROWS = 48
WIDTH = 768


def place():
    group = lax.axis_index("dp")
    pipe = lax.axis_index("pipe")
    half = lax.div(group, 16)
    rest = lax.rem(group, 16)
    return group, pipe, half, lax.div(rest, 4), lax.rem(rest, 4)


def around(position, distance):
    return lax.rem(position + distance + 4, 4)


def group_of(half, depth, column):
    return half * 16 + depth * 4 + column


def along(route, first, second):
    return (second, first) if route == 0 else (first, second)


def to_group(src, dst, send, recv, group):
    return pltpu.make_async_remote_copy(
        src_ref=src,
        dst_ref=dst,
        send_sem=send,
        recv_sem=recv,
        device_id={"dp": group},
        device_id_type=MESH,
    )


def arrived(dst, recv):
    pltpu.make_async_copy(dst, dst, recv).wait()


def narrow(ref, route, block, half, first, second):
    depth, column = along(route, first, second)
    return ref.at[block, half, depth, column]


def wide(ref, route, block, half, second):
    if route == 0:
        return ref.at[block, half, second]
    return ref.at[block, half, :, second]


def greet(others):
    barrier = pltpu.get_barrier_semaphore()
    for device in others:
        pl.semaphore_signal(barrier, inc=1, device_id=device, device_id_type=MESH)
    pl.semaphore_wait(barrier, len(others))


def ring_devices():
    group, pipe, half, depth, column = place()
    return [
        {"dp": group_of(1 - half, depth, column)},
        {"dp": group_of(half, around(depth, 1), column)},
        {"dp": group_of(half, around(depth, -1), column)},
        {"dp": group_of(half, depth, around(column, 1))},
        {"dp": group_of(half, depth, around(column, -1))},
    ]


def gather_sems():
    return [DMA((BLOCKS,)), DMA((BLOCKS, 2, 2)), DMA((BLOCKS, 2)), DMA((BLOCKS, 2, 2)), DMA((BLOCKS, 2))]


class Gather:
    def __init__(self, ref, sends, recvs):
        self.ref, self.sends, self.recvs = ref, sends, recvs
        self.group, self.pipe, self.half, self.depth, self.column = place()

    def axes(self, route):
        return (self.column, self.depth) if route == 0 else (self.depth, self.column)

    def small_peer(self, route, distance):
        if route == 0:
            return group_of(self.half, self.depth, around(self.column, distance))
        return group_of(self.half, around(self.depth, distance), self.column)

    def large_peer(self, route, distance):
        return self.small_peer(1 - route, distance)

    def own(self, block):
        return self.ref.at[block, self.half, self.depth, self.column]

    def swap(self, block):
        slot = self.own(block)
        return to_group(
            slot, slot, self.sends[0].at[block], self.recvs[0].at[block],
            group_of(1 - self.half, self.depth, self.column),
        )

    def small(self, route, block, half, way):
        first, second = self.axes(route)
        slot = narrow(self.ref, route, block, half, first, second)
        return to_group(
            slot, slot, self.sends[1].at[block, half, way], self.recvs[1].at[block, half, way],
            self.small_peer(route, 1 - 2 * way),
        )

    def small_relay(self, route, block, way):
        first, second = self.axes(route)
        distance = 1 - 2 * way
        slot = narrow(self.ref, route, block, way, around(first, -distance), second)
        return to_group(
            slot, slot, self.sends[2].at[block, way], self.recvs[2].at[block, way],
            self.small_peer(route, distance),
        )

    def large(self, route, block, half, way):
        second = self.axes(route)[1]
        slot = wide(self.ref, route, block, half, second)
        return to_group(
            slot, slot, self.sends[3].at[block, half, way], self.recvs[3].at[block, half, way],
            self.large_peer(route, 1 - 2 * way),
        )

    def large_relay(self, route, block, way):
        second = self.axes(route)[1]
        distance = 1 - 2 * way
        slot = wide(self.ref, route, block, way, around(second, -distance))
        return to_group(
            slot, slot, self.sends[4].at[block, way], self.recvs[4].at[block, way],
            self.large_peer(route, distance),
        )

    def start(self, route, block):
        self.swap(block).start()
        for way in range(2):
            self.small(route, block, self.half, way).start()

    def second(self, route, block):
        self.swap(block).wait_recv()
        for way in range(2):
            self.small(route, block, 1 - self.half, way).start()

    def third(self, route, block):
        for way in range(2):
            self.small(route, block, way, way).wait_recv()
            self.small_relay(route, block, way).start()

    def fourth(self, route, block):
        for half in range(2):
            self.small(route, block, half, 1 - half).wait_recv()
            self.small_relay(route, block, half).wait_recv()
            for way in range(2):
                self.large(route, block, half, way).start()

    def fifth(self, route, block):
        for way in range(2):
            self.large(route, block, way, way).wait_recv()
            self.large_relay(route, block, way).start()

    def last(self, route, block):
        for way in range(2):
            self.large(route, block, way, 1 - way).wait_recv()
            self.large_relay(route, block, way).wait_recv()

    def finish(self, route, block):
        self.swap(block).wait_send()
        for way in range(2):
            for half in range(2):
                self.small(route, block, half, way).wait_send()
                self.large(route, block, half, way).wait_send()
            self.small_relay(route, block, way).wait_send()
            self.large_relay(route, block, way).wait_send()


def scatter_buffers(blocks, rows, width, dtype):
    return [
        pltpu.VMEM((blocks, 2, 4, rows, width), dtype),
        pltpu.VMEM((blocks, 2, 2, 4, rows, width), dtype),
        pltpu.VMEM((blocks, 2, rows, width), dtype),
        pltpu.VMEM((blocks, 2, 2, rows, width), dtype),
        pltpu.VMEM((blocks, rows, width), dtype),
    ]


def scatter_sems(blocks):
    return [DMA((blocks, 2)), DMA((blocks, 2, 2)), DMA((blocks, 2)), DMA((blocks, 2, 2)), DMA((blocks,))]


def accumulate(target, others):
    total = target[...].astype(WIDE)
    for other in others:
        total = total + other[...].astype(WIDE)
    target[...] = total.astype(target.dtype)


class Scatter(Gather):
    def __init__(self, ref, buffers, sends, recvs):
        super().__init__(ref, sends, recvs)
        self.buffers = buffers

    def large_early(self, route, block, way):
        second = self.axes(route)[1]
        return to_group(
            wide(self.ref, route, block, way, around(second, 2)), self.buffers[0].at[block, way],
            self.sends[0].at[block, way], self.recvs[0].at[block, way],
            self.large_peer(route, 1 - 2 * way),
        )

    def large(self, route, block, half, way):
        second = self.axes(route)[1]
        distance = 1 - 2 * way
        return to_group(
            wide(self.ref, route, block, half, around(second, distance)),
            self.buffers[1].at[block, way, half],
            self.sends[1].at[block, way, half], self.recvs[1].at[block, way, half],
            self.large_peer(route, distance),
        )

    def small_early(self, route, block, way):
        first, second = self.axes(route)
        return to_group(
            narrow(self.ref, route, block, way, around(first, 2), second),
            self.buffers[2].at[block, way],
            self.sends[2].at[block, way], self.recvs[2].at[block, way],
            self.small_peer(route, 1 - 2 * way),
        )

    def small(self, route, block, half, way):
        first, second = self.axes(route)
        distance = 1 - 2 * way
        return to_group(
            narrow(self.ref, route, block, half, around(first, distance), second),
            self.buffers[3].at[block, way, half],
            self.sends[3].at[block, way, half], self.recvs[3].at[block, way, half],
            self.small_peer(route, distance),
        )

    def swap(self, block):
        return to_group(
            self.ref.at[block, 1 - self.half, self.depth, self.column], self.buffers[4].at[block],
            self.sends[4].at[block], self.recvs[4].at[block],
            group_of(1 - self.half, self.depth, self.column),
        )

    def start(self, route, block):
        for way in range(2):
            self.large_early(route, block, way).start()
            self.large(route, block, 1 - way, way).start()

    def second(self, route, block):
        second = self.axes(route)[1]
        for way in range(2):
            self.large_early(route, block, way).wait_recv()
            accumulate(
                wide(self.ref, route, block, way, around(second, 1 - 2 * way)),
                [self.buffers[0].at[block, way]],
            )
            self.large(route, block, way, way).start()

    def third(self, route, block):
        first, second = self.axes(route)
        for half in range(2):
            for way in range(2):
                self.large(route, block, half, way).wait_recv()
            accumulate(
                wide(self.ref, route, block, half, second),
                [self.buffers[1].at[block, way, half] for way in range(2)],
            )
        for way in range(2):
            self.small_early(route, block, way).start()
            self.small(route, block, 1 - way, way).start()

    def fourth(self, route, block):
        first, second = self.axes(route)
        for way in range(2):
            self.small_early(route, block, way).wait_recv()
            accumulate(
                narrow(self.ref, route, block, way, around(first, 1 - 2 * way), second),
                [self.buffers[2].at[block, way]],
            )
            self.small(route, block, way, way).start()

    def fifth(self, route, block):
        for half in range(2):
            for way in range(2):
                self.small(route, block, half, way).wait_recv()
            accumulate(
                self.ref.at[block, half, self.depth, self.column],
                [self.buffers[3].at[block, way, half] for way in range(2)],
            )
        self.swap(block).start()

    def last(self, route, block):
        self.swap(block).wait_recv()
        accumulate(self.own(block), [self.buffers[4].at[block]])

    def finish(self, route, block):
        self.swap(block).wait_send()
        for way in range(2):
            self.large_early(route, block, way).wait_send()
            self.small_early(route, block, way).wait_send()
            for half in range(2):
                self.large(route, block, half, way).wait_send()
                self.small(route, block, half, way).wait_send()


STEPS = ("second", "third", "fourth", "fifth", "last", "finish")


class Total:
    def __init__(self, first, second, third, sends, recvs):
        self.stages, self.sends, self.recvs = (first, second, third), sends, recvs
        self.group, self.pipe, self.half, self.depth, self.column = place()
        self.where = (self.column, self.depth, self.half)

    def copy(self, stage, distance):
        here, buffer = self.where[stage], self.stages[stage]
        if stage == 0:
            peer = group_of(self.half, self.depth, around(here, distance))
        elif stage == 1:
            peer = group_of(self.half, around(here, distance), self.column)
        else:
            peer = group_of(1 - here, self.depth, self.column)
        return to_group(
            buffer.at[here], buffer.at[here],
            self.sends.at[stage, distance - 1], self.recvs.at[stage, distance - 1], peer,
        )

    def distances(self, stage):
        return range(1, 4) if stage < 2 else range(1, 2)

    def send(self, stage, value):
        self.stages[stage][self.where[stage]] = value
        for distance in self.distances(stage):
            self.copy(stage, distance).start()

    def receive(self, stage):
        for distance in self.distances(stage):
            self.copy(stage, distance).wait_recv()
        total = self.stages[stage][0]
        for index in range(1, 4 if stage < 2 else 2):
            total = total + self.stages[stage][index]
        return total

    def finish(self):
        for stage in range(3):
            for distance in self.distances(stage):
                self.copy(stage, distance).wait_send()


def total_scratch(shape):
    return [
        pltpu.VMEM((4,) + shape, WIDE),
        pltpu.VMEM((4,) + shape, WIDE),
        pltpu.VMEM((2,) + shape, WIDE),
        DMA((3, 3)),
        DMA((3, 3)),
    ]


def all_dp_devices():
    group, pipe, half, depth, column = place()
    return ring_devices() + [
        {"dp": group_of(half, around(depth, 2), column)},
        {"dp": group_of(half, depth, around(column, 2))},
    ]


def gather_kernel(proj_ref, down_ref, counts_ref, full_ref, counted_ref, *scratch):
    sends, recvs = scratch[0:5], scratch[5:10]
    total = Total(*scratch[10:15])
    local_sem, cross_send, cross_recv = scratch[15:18]
    gather = Gather(full_ref, sends, recvs)
    sibling = lax.rem(gather.pipe, 2) * -2 + 1 + gather.pipe
    ffn = lax.rem(gather.pipe, 2) == 1
    pairs = lax.rem(gather.pipe, 2) + 1
    greet(all_dp_devices() + [{"pipe": sibling}])
    cross = pltpu.make_async_remote_copy(
        src_ref=down_ref, dst_ref=gather.own(2), send_sem=cross_send, recv_sem=cross_recv,
        device_id={"pipe": sibling}, device_id_type=MESH,
    )
    locals_ = [
        pltpu.make_async_copy(proj_ref.at[block], gather.own(block), local_sem.at[block])
        for block in range(2)
    ]
    for item in locals_:
        item.start()

    @pl.when(jnp.logical_not(ffn))
    def _():
        cross.start()

    for item in locals_:
        item.wait()
    for route in range(2):
        gather.start(route, route)
    total.send(0, counts_ref[...])

    @pl.when(ffn)
    def _():
        mine = pltpu.make_async_copy(down_ref, gather.own(3), local_sem.at[2])
        mine.start()
        mine.wait()
        gather.start(1, 3)
        cross.wait_recv()
        gather.start(0, 2)

    for index, step in enumerate(STEPS):
        def run(pair, _, step=step):
            for route in range(2):
                getattr(gather, step)(route, 2 * pair + route)
            return 0

        lax.fori_loop(0, pairs, run, 0)
        if index < 2:
            total.send(index + 1, total.receive(index))
        elif index == 2:
            counted_ref[...] = total.receive(2)
    total.finish()

    @pl.when(jnp.logical_not(ffn))
    def _():
        cross.wait_send()


def gather_weights(proj_blocks, down_rows, counts):
    shape = (BLOCKS, 2, 4, 4, ROWS, WIDTH)
    return pl.pallas_call(
        gather_kernel,
        out_shape=(jax.ShapeDtypeStruct(shape, LOW), jax.ShapeDtypeStruct(counts.shape, WIDE)),
        in_specs=[pl.BlockSpec(memory_space=pltpu.VMEM)] * 3,
        out_specs=(pl.BlockSpec(memory_space=pltpu.VMEM),) * 2,
        scratch_shapes=gather_sems() + gather_sems() + total_scratch(counts.shape) + [DMA((3,)), DMA, DMA],
        compiler_params=pltpu.CompilerParams(
            collective_id=0, has_side_effects=True, vmem_limit_bytes=40 * 2**20
        ),
    )(proj_blocks, down_rows, counts)


def scatter_kernel(grad_ref, region_ref, stats_ref, proj_ref, down_ref, table_ref, summed_ref, *scratch):
    held, region_held = scratch[0:2]
    main = Scatter(held, scratch[2:7], scratch[7:12], scratch[12:17])
    region = Scatter(region_held, scratch[17:22], scratch[22:27], scratch[27:32])
    total = Total(*scratch[32:37])
    local_sem, cross_send, cross_recv = scratch[37:40]
    sibling = lax.rem(main.pipe, 2) * -2 + 1 + main.pipe
    ffn = lax.rem(main.pipe, 2) == 1
    pairs = lax.rem(main.pipe, 2) + 1
    greet(all_dp_devices() + [{"pipe": sibling}])

    def load(block):
        return pltpu.make_async_copy(grad_ref.at[block], held.at[block], local_sem.at[block])

    load_region = pltpu.make_async_copy(region_ref, region_held.at[0], local_sem.at[BLOCKS])

    def each(action):
        def run(pair, _):
            for route in range(2):
                action(route, 2 * pair + route)
            return 0

        lax.fori_loop(0, pairs, run, 0)

    each(lambda route, block: load(block).start())
    load_region.start()

    def begin(route, block):
        load(block).wait()
        main.start(route, block)

    each(begin)
    load_region.wait()
    region.start(0, 0)
    total.send(0, stats_ref[...])
    for index, step in enumerate(STEPS):
        each(getattr(main, step))
        getattr(region, step)(0, 0)
        if index < 2:
            total.send(index + 1, total.receive(index))
        elif index == 2:
            summed_ref[...] = total.receive(2)
    total.finish()
    cross = pltpu.make_async_remote_copy(
        src_ref=main.own(2), dst_ref=down_ref, send_sem=cross_send, recv_sem=cross_recv,
        device_id={"pipe": sibling}, device_id_type=MESH,
    )
    for block in range(2):
        proj_ref[block] = main.own(block)[...]
    table_ref[...] = region.own(0)[...]

    @pl.when(ffn)
    def _():
        cross.start()
        down_ref[...] = main.own(3)[...]
        cross.wait_send()

    @pl.when(jnp.logical_not(ffn))
    def _():
        cross.wait_recv()


def scatter_gradients(grads, region, stats):
    any_space, vmem = pl.BlockSpec(memory_space=pl.ANY), pl.BlockSpec(memory_space=pltpu.VMEM)
    return pl.pallas_call(
        scatter_kernel,
        out_shape=(
            jax.ShapeDtypeStruct((2, ROWS, WIDTH), LOW),
            jax.ShapeDtypeStruct((ROWS, WIDTH), LOW),
            jax.ShapeDtypeStruct((8, WIDTH), WIDE),
            jax.ShapeDtypeStruct(stats.shape, WIDE),
        ),
        in_specs=[any_space, any_space, vmem],
        out_specs=(vmem,) * 4,
        scratch_shapes=[pltpu.VMEM((BLOCKS, 2, 4, 4, ROWS, WIDTH), LOW), pltpu.VMEM((1, 2, 4, 4, 8, WIDTH), WIDE)]
        + scatter_buffers(BLOCKS, ROWS, WIDTH, LOW) + scatter_sems(BLOCKS) + scatter_sems(BLOCKS)
        + scatter_buffers(1, 8, WIDTH, WIDE) + scatter_sems(1) + scatter_sems(1)
        + total_scratch(stats.shape) + [DMA((BLOCKS + 1,)), DMA, DMA],
        compiler_params=pltpu.CompilerParams(
            collective_id=1, has_side_effects=True, vmem_limit_bytes=48 * 2**20
        ),
    )(grads, region, stats)


def shifted(block, axis, distance):
    devices = range(lax.axis_size(axis))
    route = [(i - distance, i) for i in devices if i - distance in devices]
    return lax.ppermute(block, axis, route)


def norm_forward(residual, norm_gain, norm_shift):
    row_mean = jnp.mean(residual, -1, keepdims=True)
    centered = residual - row_mean
    spread = jnp.mean(centered * centered, -1, keepdims=True)
    inv_scale = lax.rsqrt(spread + EPSILON)
    normed = centered * inv_scale
    return (normed * norm_gain + norm_shift, normed, inv_scale)


def norm_backward(grad_out, normed, inv_scale, norm_gain):
    dnormed = grad_out * norm_gain
    row_inner = jnp.mean(dnormed, -1, keepdims=True)
    row_twist = jnp.mean(dnormed * normed, -1, keepdims=True)
    residual_grad = inv_scale * (dnormed - row_inner - normed * row_twist)
    return (residual_grad, jnp.sum(grad_out * normed, 0), jnp.sum(grad_out, 0))


def row_probs(queries, key_rows, doc_row):
    scores = jnp.einsum("qhd,khd->hqk", queries, key_rows, preferred_element_type=WIDE) * 0.125
    same_doc = doc_row[:, None] == doc_row[None, :]
    return jax.nn.softmax(jnp.where(same_doc[None], scores, -1e30), axis=-1)


def attend_rows(stacked, doc_rows):

    def one_row(row_item):
        packed_row, doc_row = row_item
        attn_probs = row_probs(packed_row[:, 0], packed_row[:, 1], doc_row).astype(LOW)
        mixed_row = jnp.einsum(
            "hqk,khd->qhd", attn_probs, packed_row[:, 2], preferred_element_type=WIDE
        )
        return mixed_row.astype(LOW)

    return lax.map(one_row, (stacked, doc_rows))


def attend_rows_back(stacked, doc_rows, mixed_grad):

    def one_row(row_item):
        packed_row, doc_row, mixed_row_grad = row_item
        queries = packed_row[:, 0]
        key_rows = packed_row[:, 1]
        value_rows = packed_row[:, 2]
        attn_probs = row_probs(queries, key_rows, doc_row)
        value_grad = jnp.einsum(
            "hqk,qhd->khd", attn_probs.astype(LOW), mixed_row_grad, preferred_element_type=WIDE
        )
        probs_grad = jnp.einsum(
            "qhd,khd->hqk", mixed_row_grad, value_rows, preferred_element_type=WIDE
        )
        row_inner = jnp.sum(probs_grad * attn_probs, -1, keepdims=True)
        score_grad = (attn_probs * (probs_grad - row_inner)).astype(LOW)
        query_grad = (
            jnp.einsum("hqk,khd->qhd", score_grad, key_rows, preferred_element_type=WIDE) * 0.125
        )
        key_grad = (
            jnp.einsum("hqk,qhd->khd", score_grad, queries, preferred_element_type=WIDE) * 0.125
        )
        return jnp.stack([query_grad, key_grad, value_grad], 1).astype(LOW)

    return lax.map(one_row, (stacked, doc_rows, mixed_grad))


def attention_parts(summed, weights, doc_rows):
    proj_full = weights[0]
    model_width = summed.shape[1]
    lowered = summed.astype(LOW)
    packed = jnp.dot(lowered, proj_full[:, : 3 * model_width], preferred_element_type=WIDE).astype(
        LOW
    )
    stacked = packed.reshape(doc_rows.shape[0], doc_rows.shape[1], 3, HEADS, model_width // HEADS)
    mixed_heads = attend_rows(stacked, doc_rows).reshape(-1, model_width)
    branch = jnp.dot(mixed_heads, proj_full[:, 3 * model_width :], preferred_element_type=WIDE)
    return (lowered, stacked, mixed_heads, branch)


def attention_section(summed, weights, doc_rows):
    parts_list = attention_parts(summed, weights, doc_rows)
    return norm_forward(summed + parts_list[3], weights[2], weights[3])[0]


def attention_back(summed, grad_out, weights, doc_rows):
    proj_full, down_full, norm_gain, norm_shift = weights
    model_width = summed.shape[1]
    lowered, stacked, mixed_heads, branch = attention_parts(summed, weights, doc_rows)
    outcome = norm_forward(summed + branch, norm_gain, norm_shift)
    residual_grad, gain_grad, shift_grad = norm_backward(
        grad_out, outcome[1], outcome[2], norm_gain
    )
    branch_grad = residual_grad.astype(LOW)
    out_weights = proj_full[:, 3 * model_width :]
    out_proj_grad = jnp.einsum("td,te->de", mixed_heads, branch_grad, preferred_element_type=WIDE)
    mixed_grad = jnp.einsum(
        "te,de->td", branch_grad, out_weights, preferred_element_type=WIDE
    ).astype(LOW)
    mixed_grad = mixed_grad.reshape(
        doc_rows.shape[0], doc_rows.shape[1], HEADS, model_width // HEADS
    )
    packed_grad = attend_rows_back(stacked, doc_rows, mixed_grad).reshape(-1, 3 * model_width)
    in_weights = proj_full[:, : 3 * model_width]
    in_proj_grad = jnp.einsum("td,te->de", lowered, packed_grad, preferred_element_type=WIDE)
    input_grad = (
        jnp.einsum("te,de->td", packed_grad, in_weights, preferred_element_type=WIDE)
        + residual_grad
    )
    proj_grad = jnp.concatenate([in_proj_grad, out_proj_grad], 1)
    return (input_grad, proj_grad, jnp.zeros(down_full.shape, WIDE), gain_grad, shift_grad)


def forward_mlp(summed, weights, doc_rows):
    proj_full, down_full, norm_gain, norm_shift = weights
    lowered = summed.astype(LOW)
    hidden = jnp.dot(lowered, proj_full, preferred_element_type=WIDE)
    activated = jax.nn.gelu(hidden, approximate=False).astype(LOW)
    branch = jnp.dot(activated, down_full, preferred_element_type=WIDE)
    return norm_forward(summed + branch, norm_gain, norm_shift)[0]


def feed_forward_back(summed, grad_out, weights, doc_rows):
    proj_full, down_full, norm_gain, norm_shift = weights
    lowered = summed.astype(LOW)
    hidden = jnp.dot(lowered, proj_full, preferred_element_type=WIDE)
    activated, gelu_pull = jax.vjp(partial(jax.nn.gelu, approximate=False), hidden)
    activated_low = activated.astype(LOW)
    branch = jnp.dot(activated_low, down_full, preferred_element_type=WIDE)
    outcome = norm_forward(summed + branch, norm_gain, norm_shift)
    residual_grad, gain_grad, shift_grad = norm_backward(
        grad_out, outcome[1], outcome[2], norm_gain
    )
    branch_grad = residual_grad.astype(LOW)
    down_grad = jnp.einsum("tf,td->fd", activated_low, branch_grad, preferred_element_type=WIDE)
    activated_grad = jnp.einsum("td,fd->tf", branch_grad, down_full, preferred_element_type=WIDE)
    hidden_grad = gelu_pull(activated_grad)[0].astype(LOW)
    proj_grad = jnp.einsum("td,tf->df", lowered, hidden_grad, preferred_element_type=WIDE)
    input_grad = (
        jnp.einsum("tf,df->td", hidden_grad, proj_full, preferred_element_type=WIDE) + residual_grad
    )
    return (input_grad, proj_grad, down_grad, gain_grad, shift_grad)


def body(
    tokens,
    doc_ids,
    region_ids,
    proj,
    down,
    ln_gain,
    ln_bias,
    bn_gain,
    bn_bias,
    region_table,
    out_cot,
):
    sections = lax.axis_size("pipe")
    groups = lax.axis_size("dp")
    section_rank = lax.axis_index("pipe")
    group_rank = lax.axis_index("dp")
    attn_section = section_rank % 2 == 0
    model_width = tokens.shape[1]
    region_total = region_table.shape[1]
    row_count = doc_ids.shape[0] // MICRO
    micro_tokens = row_count * doc_ids.shape[1]
    token_total = tokens.shape[0] * groups
    region_flat = region_ids.reshape(-1)
    onehot = region_flat[:, None] == jnp.arange(region_total, dtype=jnp.int32)[None, :]
    local_counts = jnp.sum(onehot.astype(WIDE), 0)
    proj_blocks = proj[0].reshape(3, 8, 2, 1536).transpose(0, 2, 1, 3).reshape(ROWS, 2, WIDTH).transpose(1, 0, 2)
    gathered, counted = gather_weights(
        proj_blocks, down[0], jnp.broadcast_to(local_counts[None], (8, region_total))
    )
    counts = counted[0]
    proj_full = gathered[:2].reshape(2, 32, ROWS, WIDTH).transpose(1, 2, 0, 3)
    proj_full = proj_full.reshape(96, 2, 8, 1536).transpose(0, 2, 1, 3).reshape(model_width, FF)
    weights = (proj_full, gathered[2:].reshape(FF, model_width), ln_gain[0], ln_bias[0])
    region_rows = region_table[0]
    region_wide = region_rows.astype(WIDE)
    region_mean = (
        jnp.dot(counts, region_wide, precision=lax.Precision.HIGHEST, preferred_element_type=WIDE)
        / token_total
    )
    second = (
        jnp.dot(
            counts,
            region_wide * region_wide,
            precision=lax.Precision.HIGHEST,
            preferred_element_type=WIDE,
        )
        / token_total
    )
    inv_spread = lax.rsqrt(second - region_mean * region_mean + EPSILON)
    normed_rows = (region_wide - region_mean) * inv_spread
    embedded = jnp.dot(onehot.astype(LOW), region_rows, preferred_element_type=WIDE)
    region_add = (embedded - region_mean) * inv_spread * bn_gain[0] + bn_bias[0]

    def section_run(summed, weight_set, doc_rows):
        return lax.cond(attn_section, attention_section, forward_mlp, summed, weight_set, doc_rows)

    def section_skip(summed, weight_set, doc_rows):
        return jnp.zeros_like(summed)

    inputs_kept = jnp.zeros((MICRO, micro_tokens, model_width), LOW)
    outputs_kept = jnp.zeros((MICRO, micro_tokens, model_width), LOW)
    incoming = jnp.zeros((micro_tokens, model_width), LOW)
    tick_total = MICRO + sections - 1
    for tick_index in range(tick_total):
        micro_slot = tick_index - section_rank
        active = (micro_slot >= 0) & (micro_slot < MICRO)
        micro_index = jnp.clip(micro_slot, 0, MICRO - 1)
        first_rows = lax.dynamic_slice_in_dim(tokens, micro_index * micro_tokens, micro_tokens, 0)
        section_input = jnp.where(section_rank == 0, first_rows, incoming)
        doc_rows = lax.dynamic_slice_in_dim(doc_ids, micro_index * row_count, row_count, 0)
        region_slice = lax.dynamic_slice_in_dim(
            region_add, micro_index * micro_tokens, micro_tokens, 0
        )
        summed = section_input.astype(WIDE) + region_slice
        section_out = lax.cond(active, section_run, section_skip, summed, weights, doc_rows).astype(
            LOW
        )
        inputs_kept = inputs_kept.at[micro_index].set(
            jnp.where(active, section_input, inputs_kept[micro_index])
        )
        outputs_kept = outputs_kept.at[micro_index].set(
            jnp.where(active, section_out, outputs_kept[micro_index])
        )
        if tick_index + 1 < tick_total:
            incoming = shifted(section_out, "pipe", 1)
    back_weights = weights

    def back_run(summed, grad_out, weight_set, doc_rows):
        return lax.cond(
            attn_section, attention_back, feed_forward_back, summed, grad_out, weight_set, doc_rows
        )

    def back_skip(summed, grad_out, weight_set, doc_rows):
        return (
            jnp.zeros_like(summed),
            jnp.zeros(weight_set[0].shape, WIDE),
            jnp.zeros(weight_set[1].shape, WIDE),
            jnp.zeros((model_width,), WIDE),
            jnp.zeros((model_width,), WIDE),
        )

    proj_grad = jnp.zeros(back_weights[0].shape, WIDE)
    down_grad = jnp.zeros(back_weights[1].shape, WIDE)
    gain_grad = jnp.zeros((model_width,), WIDE)
    shift_grad = jnp.zeros((model_width,), WIDE)
    region_grad = jnp.zeros((region_total, model_width), WIDE)
    input_grads = jnp.zeros((MICRO, micro_tokens, model_width), LOW)
    arriving = jnp.zeros((micro_tokens, model_width), LOW)
    for tick_index in range(tick_total):
        micro_slot = tick_index - (sections - 1 - section_rank)
        active = (micro_slot >= 0) & (micro_slot < MICRO)
        micro_index = jnp.clip(micro_slot, 0, MICRO - 1)
        last_grad = lax.dynamic_slice_in_dim(out_cot, micro_index * micro_tokens, micro_tokens, 0)
        grad_out = jnp.where(section_rank == sections - 1, last_grad, arriving).astype(WIDE)
        doc_rows = lax.dynamic_slice_in_dim(doc_ids, micro_index * row_count, row_count, 0)
        region_slice = lax.dynamic_slice_in_dim(
            region_add, micro_index * micro_tokens, micro_tokens, 0
        )
        summed = inputs_kept[micro_index].astype(WIDE) + region_slice
        step_grads = lax.cond(active, back_run, back_skip, summed, grad_out, back_weights, doc_rows)
        proj_grad = proj_grad + step_grads[1]
        down_grad = down_grad + step_grads[2]
        gain_grad = gain_grad + step_grads[3]
        shift_grad = shift_grad + step_grads[4]
        micro_regions = lax.dynamic_slice_in_dim(
            region_flat, micro_index * micro_tokens, micro_tokens, 0
        )
        region_grad = region_grad + jax.ops.segment_sum(step_grads[0], micro_regions, region_total)
        input_low = step_grads[0].astype(LOW)
        input_grads = input_grads.at[micro_index].set(
            jnp.where(active, input_low, input_grads[micro_index])
        )
        if tick_index + 1 < tick_total:
            arriving = shifted(input_low, "pipe", -1)
    proj_parts = proj_grad.astype(LOW).reshape(96, 8, 2, 1536).transpose(0, 2, 1, 3)
    proj_parts = proj_parts.reshape(32, ROWS, 2, WIDTH).transpose(2, 0, 1, 3)
    down_parts = down_grad.astype(LOW).reshape(2, 32, ROWS, WIDTH)
    parts = jnp.concatenate([proj_parts, down_parts], 0).reshape(BLOCKS, 2, 4, 4, ROWS, WIDTH)
    stats = jnp.stack([jnp.sum(region_grad, 0), jnp.sum(region_grad * normed_rows, 0), gain_grad, shift_grad])
    proj_sum, down_sum, table_sum, summed_stats = scatter_gradients(
        parts, region_grad.reshape(2, 4, 4, 8, model_width), jnp.concatenate([stats, stats], 0)
    )
    bias_sum, gain_sum = summed_stats[0], summed_stats[1]
    region_scale = bn_gain[0] * inv_spread
    own_counts = lax.dynamic_slice_in_dim(counts, group_rank * 8, 8, 0)
    own_normed = lax.dynamic_slice_in_dim(normed_rows, group_rank * 8, 8, 0)
    table_grad = region_scale * (
        table_sum - own_counts[:, None] * (bias_sum / token_total + own_normed * (gain_sum / token_total))
    )
    proj_out = proj_sum.transpose(1, 0, 2).reshape(3, 2, 8, 1536).transpose(0, 2, 1, 3).reshape(24, FF)
    feature_share = model_width // groups
    shares = lax.dynamic_slice_in_dim(summed_stats, group_rank * feature_share, feature_share, 1)
    return (
        outputs_kept.reshape(1, -1, model_width),
        input_grads.reshape(1, -1, model_width),
        proj_out.astype(WIDE)[None],
        down_sum.astype(WIDE)[None],
        shares[2][None],
        shares[3][None],
        shares[1][None],
        shares[0][None],
        table_grad[None],
    )


def solution(mesh):
    in_specs = (
        P("dp", None),
        P("dp", None),
        P("dp", None),
        P("pipe", "dp", None),
        P("pipe", "dp", None),
        P("pipe", None),
        P("pipe", None),
        P("pipe", None),
        P("pipe", None),
        P("pipe", None, None),
        P("dp", None),
    )
    out_specs = (
        P("pipe", "dp", None),
        P("pipe", "dp", None),
        P("pipe", "dp", None),
        P("pipe", "dp", None),
        P("pipe", "dp"),
        P("pipe", "dp"),
        P("pipe", "dp"),
        P("pipe", "dp"),
        P("pipe", "dp", None),
    )
    return jax.shard_map(body, mesh=mesh, in_specs=in_specs, out_specs=out_specs, check_vma=False)
```

```python
from functools import partial

import jax
import jax.numpy as jnp
from jax import lax
from jax.experimental import pallas as pl
from jax.experimental.pallas import tpu as pltpu
from jax.sharding import PartitionSpec as P

HEADS = 12
FF = 3072
EPSILON = 1e-05
LOW = jnp.bfloat16
WIDE = jnp.float32
MESH = pl.DeviceIdType.MESH
DMA = pltpu.SemaphoreType.DMA
BLOCKS = 4
ROWS = 48
WIDTH = 768


def place():
    group = lax.axis_index("dp")
    pipe = lax.axis_index("pipe")
    half = lax.div(group, 16)
    rest = lax.rem(group, 16)
    return group, pipe, half, lax.div(rest, 4), lax.rem(rest, 4)


def around(position, distance):
    return lax.rem(position + distance + 4, 4)


def group_of(half, depth, column):
    return half * 16 + depth * 4 + column


def along(route, first, second):
    return (second, first) if route == 0 else (first, second)


def to_group(src, dst, send, recv, group):
    return pltpu.make_async_remote_copy(
        src_ref=src,
        dst_ref=dst,
        send_sem=send,
        recv_sem=recv,
        device_id={"dp": group},
        device_id_type=MESH,
    )


def arrived(dst, recv):
    pltpu.make_async_copy(dst, dst, recv).wait()


def narrow(ref, route, block, half, first, second):
    depth, column = along(route, first, second)
    return ref.at[block, half, depth, column]


def wide(ref, route, block, half, second):
    if route == 0:
        return ref.at[block, half, second]
    return ref.at[block, half, :, second]


def greet(others):
    barrier = pltpu.get_barrier_semaphore()
    for device in others:
        pl.semaphore_signal(barrier, inc=1, device_id=device, device_id_type=MESH)
    pl.semaphore_wait(barrier, len(others))


def ring_devices():
    group, pipe, half, depth, column = place()
    return [
        {"dp": group_of(1 - half, depth, column)},
        {"dp": group_of(half, around(depth, 1), column)},
        {"dp": group_of(half, around(depth, -1), column)},
        {"dp": group_of(half, depth, around(column, 1))},
        {"dp": group_of(half, depth, around(column, -1))},
    ]


def gather_sems():
    return [DMA((BLOCKS,)), DMA((BLOCKS, 2, 2)), DMA((BLOCKS, 2)), DMA((BLOCKS, 2, 2)), DMA((BLOCKS, 2))]


class Gather:
    def __init__(self, ref, sends, recvs):
        self.ref, self.sends, self.recvs = ref, sends, recvs
        self.group, self.pipe, self.half, self.depth, self.column = place()

    def axes(self, route):
        return (self.column, self.depth) if route == 0 else (self.depth, self.column)

    def small_peer(self, route, distance):
        if route == 0:
            return group_of(self.half, self.depth, around(self.column, distance))
        return group_of(self.half, around(self.depth, distance), self.column)

    def large_peer(self, route, distance):
        return self.small_peer(1 - route, distance)

    def own(self, block):
        return self.ref.at[block, self.half, self.depth, self.column]

    def swap(self, block):
        slot = self.own(block)
        return to_group(
            slot, slot, self.sends[0].at[block], self.recvs[0].at[block],
            group_of(1 - self.half, self.depth, self.column),
        )

    def small(self, route, block, half, way):
        first, second = self.axes(route)
        slot = narrow(self.ref, route, block, half, first, second)
        return to_group(
            slot, slot, self.sends[1].at[block, half, way], self.recvs[1].at[block, half, way],
            self.small_peer(route, 1 - 2 * way),
        )

    def small_relay(self, route, block, way):
        first, second = self.axes(route)
        distance = 1 - 2 * way
        slot = narrow(self.ref, route, block, way, around(first, -distance), second)
        return to_group(
            slot, slot, self.sends[2].at[block, way], self.recvs[2].at[block, way],
            self.small_peer(route, distance),
        )

    def large(self, route, block, half, way):
        second = self.axes(route)[1]
        slot = wide(self.ref, route, block, half, second)
        return to_group(
            slot, slot, self.sends[3].at[block, half, way], self.recvs[3].at[block, half, way],
            self.large_peer(route, 1 - 2 * way),
        )

    def large_relay(self, route, block, way):
        second = self.axes(route)[1]
        distance = 1 - 2 * way
        slot = wide(self.ref, route, block, way, around(second, -distance))
        return to_group(
            slot, slot, self.sends[4].at[block, way], self.recvs[4].at[block, way],
            self.large_peer(route, distance),
        )

    def start(self, route, block):
        self.swap(block).start()
        for way in range(2):
            self.small(route, block, self.half, way).start()

    def second(self, route, block):
        self.swap(block).wait_recv()
        for way in range(2):
            self.small(route, block, 1 - self.half, way).start()

    def third(self, route, block):
        for way in range(2):
            self.small(route, block, way, way).wait_recv()
            self.small_relay(route, block, way).start()

    def fourth(self, route, block):
        for half in range(2):
            self.small(route, block, half, 1 - half).wait_recv()
            self.small_relay(route, block, half).wait_recv()
            for way in range(2):
                self.large(route, block, half, way).start()

    def fifth(self, route, block):
        for way in range(2):
            self.large(route, block, way, way).wait_recv()
            self.large_relay(route, block, way).start()

    def last(self, route, block):
        for way in range(2):
            self.large(route, block, way, 1 - way).wait_recv()
            self.large_relay(route, block, way).wait_recv()

    def finish(self, route, block):
        self.swap(block).wait_send()
        for way in range(2):
            for half in range(2):
                self.small(route, block, half, way).wait_send()
                self.large(route, block, half, way).wait_send()
            self.small_relay(route, block, way).wait_send()
            self.large_relay(route, block, way).wait_send()


def scatter_buffers(blocks, rows, width, dtype):
    return [
        pltpu.VMEM((blocks, 2, 4, rows, width), dtype),
        pltpu.VMEM((blocks, 2, 2, 4, rows, width), dtype),
        pltpu.VMEM((blocks, 2, rows, width), dtype),
        pltpu.VMEM((blocks, 2, 2, rows, width), dtype),
        pltpu.VMEM((blocks, rows, width), dtype),
    ]


def scatter_sems(blocks):
    return [DMA((blocks, 2)), DMA((blocks, 2, 2)), DMA((blocks, 2)), DMA((blocks, 2, 2)), DMA((blocks,))]


def accumulate(target, others):
    total = target[...].astype(WIDE)
    for other in others:
        total = total + other[...].astype(WIDE)
    target[...] = total.astype(target.dtype)


class Scatter(Gather):
    def __init__(self, ref, buffers, sends, recvs):
        super().__init__(ref, sends, recvs)
        self.buffers = buffers

    def large_early(self, route, block, way):
        second = self.axes(route)[1]
        return to_group(
            wide(self.ref, route, block, way, around(second, 2)), self.buffers[0].at[block, way],
            self.sends[0].at[block, way], self.recvs[0].at[block, way],
            self.large_peer(route, 1 - 2 * way),
        )

    def large(self, route, block, half, way):
        second = self.axes(route)[1]
        distance = 1 - 2 * way
        return to_group(
            wide(self.ref, route, block, half, around(second, distance)),
            self.buffers[1].at[block, way, half],
            self.sends[1].at[block, way, half], self.recvs[1].at[block, way, half],
            self.large_peer(route, distance),
        )

    def small_early(self, route, block, way):
        first, second = self.axes(route)
        return to_group(
            narrow(self.ref, route, block, way, around(first, 2), second),
            self.buffers[2].at[block, way],
            self.sends[2].at[block, way], self.recvs[2].at[block, way],
            self.small_peer(route, 1 - 2 * way),
        )

    def small(self, route, block, half, way):
        first, second = self.axes(route)
        distance = 1 - 2 * way
        return to_group(
            narrow(self.ref, route, block, half, around(first, distance), second),
            self.buffers[3].at[block, way, half],
            self.sends[3].at[block, way, half], self.recvs[3].at[block, way, half],
            self.small_peer(route, distance),
        )

    def swap(self, block):
        return to_group(
            self.ref.at[block, 1 - self.half, self.depth, self.column], self.buffers[4].at[block],
            self.sends[4].at[block], self.recvs[4].at[block],
            group_of(1 - self.half, self.depth, self.column),
        )

    def start(self, route, block):
        for way in range(2):
            self.large_early(route, block, way).start()
            self.large(route, block, 1 - way, way).start()

    def second(self, route, block):
        second = self.axes(route)[1]
        for way in range(2):
            self.large_early(route, block, way).wait_recv()
            accumulate(
                wide(self.ref, route, block, way, around(second, 1 - 2 * way)),
                [self.buffers[0].at[block, way]],
            )
            self.large(route, block, way, way).start()

    def third(self, route, block):
        first, second = self.axes(route)
        for half in range(2):
            for way in range(2):
                self.large(route, block, half, way).wait_recv()
            accumulate(
                wide(self.ref, route, block, half, second),
                [self.buffers[1].at[block, way, half] for way in range(2)],
            )
        for way in range(2):
            self.small_early(route, block, way).start()
            self.small(route, block, 1 - way, way).start()

    def fourth(self, route, block):
        first, second = self.axes(route)
        for way in range(2):
            self.small_early(route, block, way).wait_recv()
            accumulate(
                narrow(self.ref, route, block, way, around(first, 1 - 2 * way), second),
                [self.buffers[2].at[block, way]],
            )
            self.small(route, block, way, way).start()

    def fifth(self, route, block):
        for half in range(2):
            for way in range(2):
                self.small(route, block, half, way).wait_recv()
            accumulate(
                self.ref.at[block, half, self.depth, self.column],
                [self.buffers[3].at[block, way, half] for way in range(2)],
            )
        self.swap(block).start()

    def last(self, route, block):
        self.swap(block).wait_recv()
        accumulate(self.own(block), [self.buffers[4].at[block]])

    def finish(self, route, block):
        self.swap(block).wait_send()
        for way in range(2):
            self.large_early(route, block, way).wait_send()
            self.small_early(route, block, way).wait_send()
            for half in range(2):
                self.large(route, block, half, way).wait_send()
                self.small(route, block, half, way).wait_send()


STEPS = ("second", "third", "fourth", "fifth", "last", "finish")


class Total:
    def __init__(self, first, second, third, sends, recvs):
        self.stages, self.sends, self.recvs = (first, second, third), sends, recvs
        self.group, self.pipe, self.half, self.depth, self.column = place()
        self.where = (self.column, self.depth, self.half)

    def copy(self, stage, distance):
        here, buffer = self.where[stage], self.stages[stage]
        if stage == 0:
            peer = group_of(self.half, self.depth, around(here, distance))
        elif stage == 1:
            peer = group_of(self.half, around(here, distance), self.column)
        else:
            peer = group_of(1 - here, self.depth, self.column)
        return to_group(
            buffer.at[here], buffer.at[here],
            self.sends.at[stage, distance - 1], self.recvs.at[stage, distance - 1], peer,
        )

    def distances(self, stage):
        return range(1, 4) if stage < 2 else range(1, 2)

    def send(self, stage, value):
        self.stages[stage][self.where[stage]] = value
        for distance in self.distances(stage):
            self.copy(stage, distance).start()

    def receive(self, stage):
        for distance in self.distances(stage):
            self.copy(stage, distance).wait_recv()
        total = self.stages[stage][0]
        for index in range(1, 4 if stage < 2 else 2):
            total = total + self.stages[stage][index]
        return total

    def finish(self):
        for stage in range(3):
            for distance in self.distances(stage):
                self.copy(stage, distance).wait_send()


def total_scratch(shape):
    return [
        pltpu.VMEM((4,) + shape, WIDE),
        pltpu.VMEM((4,) + shape, WIDE),
        pltpu.VMEM((2,) + shape, WIDE),
        DMA((3, 3)),
        DMA((3, 3)),
    ]


def all_dp_devices():
    group, pipe, half, depth, column = place()
    return ring_devices() + [
        {"dp": group_of(half, around(depth, 2), column)},
        {"dp": group_of(half, depth, around(column, 2))},
    ]


def gather_kernel(proj_ref, down_ref, counts_ref, full_ref, counted_ref, *scratch):
    sends, recvs = scratch[0:5], scratch[5:10]
    total = Total(*scratch[10:15])
    local_sem, cross_send, cross_recv = scratch[15:18]
    gather = Gather(full_ref, sends, recvs)
    sibling = lax.rem(gather.pipe, 2) * -2 + 1 + gather.pipe
    ffn = lax.rem(gather.pipe, 2) == 1
    pairs = lax.rem(gather.pipe, 2) + 1
    greet(all_dp_devices() + [{"pipe": sibling}])
    cross = pltpu.make_async_remote_copy(
        src_ref=down_ref, dst_ref=gather.own(2), send_sem=cross_send, recv_sem=cross_recv,
        device_id={"pipe": sibling}, device_id_type=MESH,
    )
    locals_ = [
        pltpu.make_async_copy(proj_ref.at[block], gather.own(block), local_sem.at[block])
        for block in range(2)
    ]
    for item in locals_:
        item.start()

    @pl.when(jnp.logical_not(ffn))
    def _():
        cross.start()

    for item in locals_:
        item.wait()
    for route in range(2):
        gather.start(route, route)
    total.send(0, counts_ref[...])

    @pl.when(ffn)
    def _():
        mine = pltpu.make_async_copy(down_ref, gather.own(3), local_sem.at[2])
        mine.start()
        mine.wait()
        gather.start(1, 3)
        cross.wait_recv()
        gather.start(0, 2)

    for index, step in enumerate(STEPS):
        def run(pair, _, step=step):
            for route in range(2):
                getattr(gather, step)(route, 2 * pair + route)
            return 0

        lax.fori_loop(0, pairs, run, 0)
        if index < 2:
            total.send(index + 1, total.receive(index))
        elif index == 2:
            counted_ref[...] = total.receive(2)
    total.finish()

    @pl.when(jnp.logical_not(ffn))
    def _():
        cross.wait_send()


def gather_weights(proj_blocks, down_rows, counts):
    shape = (BLOCKS, 2, 4, 4, ROWS, WIDTH)
    return pl.pallas_call(
        gather_kernel,
        out_shape=(jax.ShapeDtypeStruct(shape, LOW), jax.ShapeDtypeStruct(counts.shape, WIDE)),
        in_specs=[pl.BlockSpec(memory_space=pltpu.VMEM)] * 3,
        out_specs=(pl.BlockSpec(memory_space=pltpu.VMEM),) * 2,
        scratch_shapes=gather_sems() + gather_sems() + total_scratch(counts.shape) + [DMA((3,)), DMA, DMA],
        compiler_params=pltpu.CompilerParams(
            collective_id=0, has_side_effects=True, vmem_limit_bytes=40 * 2**20
        ),
    )(proj_blocks, down_rows, counts)


def scatter_kernel(grad_ref, region_ref, stats_ref, proj_ref, down_ref, table_ref, summed_ref, *scratch):
    held, region_held = scratch[0:2]
    main = Scatter(held, scratch[2:7], scratch[7:12], scratch[12:17])
    region = Scatter(region_held, scratch[17:22], scratch[22:27], scratch[27:32])
    total = Total(*scratch[32:37])
    local_sem, cross_send, cross_recv = scratch[37:40]
    sibling = lax.rem(main.pipe, 2) * -2 + 1 + main.pipe
    ffn = lax.rem(main.pipe, 2) == 1
    pairs = lax.rem(main.pipe, 2) + 1
    greet(all_dp_devices() + [{"pipe": sibling}])

    def load(block):
        return pltpu.make_async_copy(grad_ref.at[block], held.at[block], local_sem.at[block])

    load_region = pltpu.make_async_copy(region_ref, region_held.at[0], local_sem.at[BLOCKS])

    def each(action):
        def run(pair, _):
            for route in range(2):
                action(route, 2 * pair + route)
            return 0

        lax.fori_loop(0, pairs, run, 0)

    each(lambda route, block: load(block).start())
    load_region.start()

    def begin(route, block):
        load(block).wait()
        main.start(route, block)

    each(begin)
    load_region.wait()
    region.start(0, 0)
    total.send(0, stats_ref[...])
    for index, step in enumerate(STEPS):
        each(getattr(main, step))
        getattr(region, step)(0, 0)
        if index < 2:
            total.send(index + 1, total.receive(index))
        elif index == 2:
            summed_ref[...] = total.receive(2)
    total.finish()
    cross = pltpu.make_async_remote_copy(
        src_ref=main.own(2), dst_ref=down_ref, send_sem=cross_send, recv_sem=cross_recv,
        device_id={"pipe": sibling}, device_id_type=MESH,
    )
    for block in range(2):
        proj_ref[block] = main.own(block)[...]
    table_ref[...] = region.own(0)[...]

    @pl.when(ffn)
    def _():
        cross.start()
        down_ref[...] = main.own(3)[...]
        cross.wait_send()

    @pl.when(jnp.logical_not(ffn))
    def _():
        cross.wait_recv()


def scatter_gradients(grads, region, stats):
    any_space, vmem = pl.BlockSpec(memory_space=pl.ANY), pl.BlockSpec(memory_space=pltpu.VMEM)
    return pl.pallas_call(
        scatter_kernel,
        out_shape=(
            jax.ShapeDtypeStruct((2, ROWS, WIDTH), LOW),
            jax.ShapeDtypeStruct((ROWS, WIDTH), LOW),
            jax.ShapeDtypeStruct((8, WIDTH), WIDE),
            jax.ShapeDtypeStruct(stats.shape, WIDE),
        ),
        in_specs=[any_space, any_space, vmem],
        out_specs=(vmem,) * 4,
        scratch_shapes=[pltpu.VMEM((BLOCKS, 2, 4, 4, ROWS, WIDTH), LOW), pltpu.VMEM((1, 2, 4, 4, 8, WIDTH), WIDE)]
        + scatter_buffers(BLOCKS, ROWS, WIDTH, LOW) + scatter_sems(BLOCKS) + scatter_sems(BLOCKS)
        + scatter_buffers(1, 8, WIDTH, WIDE) + scatter_sems(1) + scatter_sems(1)
        + total_scratch(stats.shape) + [DMA((BLOCKS + 1,)), DMA, DMA],
        compiler_params=pltpu.CompilerParams(
            collective_id=1, has_side_effects=True, vmem_limit_bytes=48 * 2**20
        ),
    )(grads, region, stats)


PAIRS = HEADS // 2
SEQ = 128
REGIONS = 256
TOKENS = 8192
CHUNKS = 4


def dot(left, right):
    return lax.dot_general(left, right, (((1,), (0,)), ((), ())), preferred_element_type=WIDE)


def dot_nt(left, right):
    return lax.dot_general(left, right, (((1,), (1,)), ((), ())), preferred_element_type=WIDE)


def dot_tn(left, right):
    return lax.dot_general(left, right, (((0,), (0,)), ((), ())), preferred_element_type=WIDE)


def cols(index, width=WIDTH):
    return slice(index * width, (index + 1) * width)


def two_heads(pair):
    lane = lax.broadcasted_iota(jnp.int32, pair.shape, 1)
    zero = jnp.zeros_like(pair)
    return jnp.concatenate([jnp.where(lane < 64, pair, zero), jnp.where(lane < 64, zero, pair)], 0)


def side_by_side(stacked):
    return jnp.concatenate([stacked[:SEQ], stacked[SEQ:]], 1)


def row_mean(value):
    return jnp.mean(value, -1, keepdims=True)


def chain_scratch():
    return dict(
        proj=pltpu.VMEM((CHUNKS, WIDTH, WIDTH), LOW),
        fin=pltpu.VMEM((2, SEQ, WIDTH), LOW),
        bin=pltpu.VMEM((2, SEQ, WIDTH), LOW),
        lowered=pltpu.VMEM((2, SEQ, WIDTH), LOW),
        normed=pltpu.VMEM((2, SEQ, WIDTH), WIDE),
        inverse=pltpu.VMEM((2, SEQ, 128), WIDE),
        normed_rows=pltpu.VMEM((REGIONS, WIDTH), WIDE),
        region_info=pltpu.VMEM((8, WIDTH), WIDE),
        qkv=pltpu.VMEM((2, SEQ, 3 * WIDTH), LOW),
        probs=pltpu.VMEM((2, PAIRS, 2 * SEQ, SEQ), WIDE),
        mixed=pltpu.VMEM((2, SEQ, WIDTH), LOW),
        dbranch=pltpu.VMEM((2, SEQ, WIDTH), LOW),
        dwide=pltpu.VMEM((2, SEQ, FF), LOW),
        act=pltpu.VMEM((2, SEQ, FF), LOW),
        slope=pltpu.VMEM((2, SEQ, FF), WIDE),
        dweight=pltpu.VMEM((2, WIDTH, WIDTH), WIDE),
        send=DMA((2, 2)),
        recv=DMA((2, 2)),
    )


def unpack_proj(full_ref, proj_ref):
    def run(index, _):
        half, depth = lax.div(index, 4), lax.rem(index, 4)
        rows = pl.ds(pl.multiple_of(index * 96, 96), 96)
        for block in range(2):
            value = full_ref[block, half, depth].astype(WIDE).reshape(12, 2, 8, WIDTH)
            for side in range(2):
                proj_ref[2 * side + block, rows] = value[:, side].reshape(96, WIDTH).astype(LOW)
        return 0

    lax.fori_loop(0, 8, run, 0)


class Chain:
    def __init__(self, args, full_ref, counts, outs, grads, s):
        self.args, self.full, self.outs, self.grads, self.s = args, full_ref, outs, grads, s
        self.pipe = lax.axis_index("pipe")
        self.attention = lax.rem(self.pipe, 2) == 0
        self.region_statistics(counts)

    def region_statistics(self, counts):
        table_ref, s = self.args["table"], self.s
        column = jnp.transpose(jnp.broadcast_to(counts[0:1], (SEQ, REGIONS)))
        for index in range(WIDTH // 128):
            lanes = cols(index, 128)
            table = table_ref[:, lanes].astype(WIDE)
            mean = jnp.sum(table * column, 0, keepdims=True) / TOKENS
            second = jnp.sum(table * table * column, 0, keepdims=True) / TOKENS
            inverse = lax.rsqrt(second - mean * mean + EPSILON)
            s["normed_rows"][:, lanes] = (table - mean) * inverse
            s["region_info"][0:1, lanes] = mean
            s["region_info"][1:2, lanes] = inverse
            s["region_info"][2:3, lanes] = inverse * self.args["bn_gain"][0:1, lanes]

    def marks(self, micro):
        ids = self.args["region_ids"][pl.ds(micro, 1), :]
        rank = lax.broadcasted_iota(jnp.int32, (REGIONS, SEQ), 0)
        return jnp.where(rank == ids, 1.0, 0.0).astype(LOW)

    def same_document(self, micro):
        ids = jnp.broadcast_to(self.args["doc_ids"][pl.ds(micro, 1), :].astype(WIDE), (SEQ, SEQ))
        same = jnp.where(ids == jnp.transpose(ids), 1.0, 0.0)
        return jnp.concatenate([same, same], 0) > 0.5

    def down(self, index):
        return self.full[2 + index // 2, index % 2].reshape(WIDTH, WIDTH)

    def hop(self, direction, micro):
        source, target = (self.outs["acts"], self.s["fin"]) if direction == 0 else (self.outs["dins"], self.s["bin"])
        return pltpu.make_async_remote_copy(
            src_ref=source.at[micro], dst_ref=target.at[micro],
            send_sem=self.s["send"].at[direction, micro], recv_sem=self.s["recv"].at[direction, micro],
            device_id={"pipe": lax.rem(self.pipe + 1 + 2 * direction, 4)}, device_id_type=MESH,
        )

    def forward(self, micro):
        s, args = self.s, self.args

        @pl.when(self.pipe == 0)
        def _():
            s["fin"][micro] = args["tokens"][micro]

        @pl.when(self.pipe > 0)
        def _():
            self.hop(0, micro).wait_recv()

        embedded = dot_tn(self.marks(micro), args["table"][...])
        info = s["region_info"]
        summed = (
            s["fin"][micro].astype(WIDE)
            + (embedded - info[0:1]) * info[2:3] + args["bn_bias"][...]
        )
        lowered = summed.astype(LOW)
        s["lowered"][micro] = lowered
        s["normed"][micro] = summed

        @pl.when(self.attention)
        def _():
            self.attention_forward(micro, lowered)

        @pl.when(jnp.logical_not(self.attention))
        def _():
            self.feed_forward(micro, lowered)

        residual = s["normed"][micro]
        centered = residual - row_mean(residual)
        inverse = lax.rsqrt(row_mean(centered * centered) + EPSILON)
        normed = centered * inverse
        s["normed"][micro] = normed
        s["inverse"][micro] = jnp.broadcast_to(inverse, (SEQ, 128))
        self.outs["acts"][micro] = (normed * args["ln_gain"][...] + args["ln_bias"][...]).astype(LOW)

        @pl.when(self.pipe < 3)
        def _():
            self.hop(0, micro).start()

    def attention_forward(self, micro, lowered):
        s = self.s
        for index in range(3):
            s["qkv"][micro, :, cols(index)] = dot(lowered, s["proj"][index]).astype(LOW)
        same = self.same_document(micro)
        for pair in range(PAIRS):
            queries = two_heads(s["qkv"][micro, :, cols(pair, 128)])
            keys = s["qkv"][micro, :, cols(PAIRS + pair, 128)]
            values = two_heads(s["qkv"][micro, :, cols(2 * PAIRS + pair, 128)])
            scores = jnp.where(same, dot_nt(queries, keys) * 0.125, -1e30)
            powers = jnp.exp(scores - jnp.max(scores, -1, keepdims=True))
            probs = powers / jnp.sum(powers, -1, keepdims=True)
            s["probs"][micro, pair] = probs
            s["mixed"][micro, :, cols(pair, 128)] = dot(side_by_side(probs.astype(LOW)), values).astype(LOW)
        s["normed"][micro] = s["normed"][micro] + dot(s["mixed"][micro], s["proj"][3])

    def feed_forward(self, micro, lowered):
        s = self.s
        branch = s["normed"][micro]
        for index in range(CHUNKS):
            hidden = dot(lowered, s["proj"][index])
            cumulative = 0.5 * (1.0 + lax.erf(hidden * (0.5 ** 0.5)))
            density = jnp.exp(hidden * hidden * -0.5) * 0.3989422804014327
            act = (hidden * cumulative).astype(LOW)
            s["act"][micro, :, cols(index)] = act
            s["slope"][micro, :, cols(index)] = cumulative + hidden * density
            branch = branch + dot(act, self.down(index))
        s["normed"][micro] = branch

    def backward(self, micro):
        s, args = self.s, self.args

        @pl.when(self.pipe == 3)
        def _():
            s["bin"][micro] = args["out_cot"][micro]

        @pl.when(self.pipe < 3)
        def _():
            self.hop(1, micro).wait_recv()

        gout = s["bin"][micro].astype(WIDE)
        normed = s["normed"][micro]
        stats = self.outs["stats"]
        stats[2:3] = stats[2:3] + jnp.sum(gout * normed, 0, keepdims=True)
        stats[3:4] = stats[3:4] + jnp.sum(gout, 0, keepdims=True)
        dnormed = gout * args["ln_gain"][...]
        dres = s["inverse"][micro][:, 0:1] * (
            dnormed - row_mean(dnormed) - normed * row_mean(dnormed * normed)
        )
        s["normed"][micro] = dres
        s["dbranch"][micro] = dres.astype(LOW)

        @pl.when(self.attention)
        def _():
            self.attention_backward(micro)

        @pl.when(jnp.logical_not(self.attention))
        def _():
            self.feed_backward(micro)

        dsum = s["normed"][micro]
        high = dsum.astype(LOW)
        self.outs["dins"][micro] = high

        @pl.when(self.pipe > 0)
        def _():
            self.hop(1, micro).start()

        marks = self.marks(micro)
        rest = (dsum - high.astype(WIDE)).astype(LOW)
        region = self.outs["region"]
        region[...] = region[...] + dot(marks, high) + dot(marks, rest)

    def attention_backward(self, micro):
        s = self.s
        dmixed = dot_nt(s["dbranch"][micro], s["proj"][3]).astype(LOW)
        for pair in range(PAIRS):
            pieces = [s["qkv"][micro, :, cols(part * PAIRS + pair, 128)] for part in range(3)]
            queries, keys = two_heads(pieces[0]), two_heads(pieces[1])
            grads = two_heads(dmixed[:, cols(pair, 128)])
            probs = s["probs"][micro, pair]
            dprobs = dot_nt(grads, pieces[2])
            dscores = (probs * (dprobs - jnp.sum(dprobs * probs, -1, keepdims=True))).astype(LOW)
            dqueries = dot(side_by_side(dscores), keys) * 0.125
            dkeys = dot_tn(dscores, queries) * 0.125
            dvalues = dot_tn(probs.astype(LOW), grads)
            for part, value in enumerate((dqueries, dkeys, dvalues)):
                s["dwide"][micro, :, cols(part * PAIRS + pair, 128)] = value.astype(LOW)
        total = s["normed"][micro]
        for index in range(3):
            total = total + dot_nt(s["dwide"][micro, :, cols(index)], s["proj"][index])
        s["normed"][micro] = total

    def feed_backward(self, micro):
        s = self.s
        total = s["normed"][micro]
        dbranch = s["dbranch"][micro]
        for index in range(CHUNKS):
            dact = dot_nt(dbranch, self.down(index))
            dhidden = (dact * s["slope"][micro, :, cols(index)]).astype(LOW)
            s["dwide"][micro, :, cols(index)] = dhidden
            total = total + dot_nt(dhidden, s["proj"][index])
        s["normed"][micro] = total

    def weight_gradients(self, block):
        s = self.s
        lowered = s["lowered"][...].reshape(2 * SEQ, WIDTH)
        for side in range(2):
            quarter = 2 * side + block
            if quarter == 3:
                @pl.when(self.attention)
                def _():
                    left = s["mixed"][...].reshape(2 * SEQ, WIDTH)
                    s["dweight"][1] = dot_tn(left, s["dbranch"][...].reshape(2 * SEQ, WIDTH))

                @pl.when(jnp.logical_not(self.attention))
                def _():
                    right = s["dwide"][:, :, cols(3)].reshape(2 * SEQ, WIDTH)
                    s["dweight"][1] = dot_tn(lowered, right)
            else:
                right = s["dwide"][:, :, cols(quarter)].reshape(2 * SEQ, WIDTH)
                s["dweight"][side] = dot_tn(lowered, right)

        def run(index, _):
            half, depth = lax.div(index, 4), lax.rem(index, 4)
            rows = pl.ds(pl.multiple_of(index * 96, 96), 96)
            sides = [s["dweight"][side, rows].reshape(12, 1, 8, WIDTH) for side in range(2)]
            value = jnp.concatenate(sides, 1).reshape(4, ROWS, WIDTH)
            self.grads[block, half, depth] = value.astype(LOW)
            return 0

        lax.fori_loop(0, 8, run, 0)

    def down_gradients(self, block):
        s = self.s
        dbranch = s["dbranch"][...].reshape(2 * SEQ, WIDTH)
        for half in range(2):
            act = s["act"][:, :, cols(2 * (block - 2) + half)].reshape(2 * SEQ, WIDTH)
            self.grads[block, half] = dot_tn(act, dbranch).astype(LOW).reshape(4, 4, ROWS, WIDTH)

    def start_stats(self):
        self.outs["stats"][...] = jnp.zeros((8, WIDTH), WIDE)
        self.outs["region"][...] = jnp.zeros((REGIONS, WIDTH), WIDE)

    def end_stats(self):
        region, stats = self.outs["region"][...], self.outs["stats"]
        stats[0:1] = jnp.sum(region, 0, keepdims=True)
        stats[1:2] = jnp.sum(region * self.s["normed_rows"][...], 0, keepdims=True)

    def each(self, action):
        lax.fori_loop(0, 2, lambda micro, _: (action(micro), 0)[1], 0)

    def finish(self):
        def run(micro):
            @pl.when(self.pipe < 3)
            def _():
                self.hop(0, micro).wait_send()

            @pl.when(self.pipe > 0)
            def _():
                self.hop(1, micro).wait_send()

        self.each(run)


ARGS = ("tokens", "doc_ids", "region_ids", "ln_gain", "ln_bias", "bn_gain", "bn_bias", "table", "out_cot")
OUTS = ("acts", "dins", "stats", "region")


def chain_kernel(*refs):
    names = list(chain_scratch())
    args = dict(zip(ARGS, refs))
    refs = refs[len(ARGS):]
    full_ref, counts_ref = refs[:2]
    outs = dict(zip(OUTS, refs[2:]))
    grads = refs[2 + len(OUTS)]
    s = dict(zip(names, refs[3 + len(OUTS):]))
    pipe = lax.axis_index("pipe")
    greet([{"pipe": lax.rem(pipe + 1, 4)}, {"pipe": lax.rem(pipe + 3, 4)}])
    unpack_proj(full_ref, s["proj"])
    chain = Chain(args, full_ref, counts_ref[...], outs, grads, s)
    chain.start_stats()
    chain.each(chain.forward)
    chain.each(chain.backward)
    chain.end_stats()
    for block in range(2):
        chain.weight_gradients(block)

    @pl.when(jnp.logical_not(chain.attention))
    def _():
        for block in range(2, 4):
            chain.down_gradients(block)

    chain.finish()


def run_chain(args, gathered, counted):
    micro = (2, SEQ, WIDTH)
    vmem = pl.BlockSpec(memory_space=pltpu.VMEM)
    out_shape = [
        jax.ShapeDtypeStruct(micro, LOW),
        jax.ShapeDtypeStruct(micro, LOW),
        jax.ShapeDtypeStruct((8, WIDTH), WIDE),
        jax.ShapeDtypeStruct((REGIONS, WIDTH), WIDE),
        jax.ShapeDtypeStruct((BLOCKS, 2, 4, 4, ROWS, WIDTH), LOW),
    ]
    return pl.pallas_call(
        chain_kernel,
        out_shape=out_shape,
        in_specs=[vmem] * (len(ARGS) + 2),
        out_specs=[vmem] * len(out_shape),
        scratch_shapes=list(chain_scratch().values()),
        compiler_params=pltpu.CompilerParams(
            collective_id=2, has_side_effects=True, vmem_limit_bytes=60 * 2**20
        ),
    )(*[args[name] for name in ARGS], gathered, counted)


def body(
    tokens, doc_ids, region_ids, proj, down, ln_gain, ln_bias, bn_gain, bn_bias, region_table, out_cot
):
    group = lax.axis_index("dp")
    local_counts = jnp.sum(
        (region_ids.reshape(-1)[:, None] == jnp.arange(REGIONS, dtype=jnp.int32)[None, :]).astype(WIDE), 0
    )
    proj_blocks = proj[0].reshape(3, 8, 2, 1536).transpose(0, 2, 1, 3).reshape(ROWS, 2, WIDTH).transpose(1, 0, 2)
    gathered, counted = gather_weights(
        proj_blocks, down[0], jnp.broadcast_to(local_counts[None], (8, REGIONS))
    )
    args = dict(
        tokens=tokens.reshape(2, SEQ, WIDTH), doc_ids=doc_ids, region_ids=region_ids, ln_gain=ln_gain,
        ln_bias=ln_bias, bn_gain=bn_gain, bn_bias=bn_bias, table=region_table[0],
        out_cot=out_cot.reshape(2, SEQ, WIDTH),
    )
    acts, dins, stats, region, grads = run_chain(args, gathered, counted)
    proj_sum, down_sum, table_sum, summed_stats = scatter_gradients(
        grads, region.reshape(2, 4, 4, 8, WIDTH), stats
    )
    counts = counted[0]
    wide_table = region_table[0].astype(WIDE)
    mean = jnp.sum(counts[:, None] * wide_table, 0) / TOKENS
    second = jnp.sum(counts[:, None] * wide_table * wide_table, 0) / TOKENS
    inverse = lax.rsqrt(second - mean * mean + EPSILON)
    bias_sum, gain_sum = summed_stats[0], summed_stats[1]
    own_counts = lax.dynamic_slice_in_dim(counts, group * 8, 8, 0)
    own_normed = (lax.dynamic_slice_in_dim(wide_table, group * 8, 8, 0) - mean) * inverse
    table_grad = bn_gain[0] * inverse * (
        table_sum - own_counts[:, None] * (bias_sum / TOKENS + own_normed * (gain_sum / TOKENS))
    )
    proj_out = proj_sum.transpose(1, 0, 2).reshape(3, 2, 8, 1536).transpose(0, 2, 1, 3).reshape(24, FF)
    shares = lax.dynamic_slice_in_dim(summed_stats, group * 24, 24, 1)
    return (
        acts.reshape(1, 2 * SEQ, WIDTH),
        dins.reshape(1, 2 * SEQ, WIDTH),
        proj_out.astype(WIDE)[None],
        down_sum.astype(WIDE)[None],
        shares[2][None],
        shares[3][None],
        shares[1][None],
        shares[0][None],
        table_grad[None],
    )


def solution(mesh):
    in_specs = (
        P("dp", None),
        P("dp", None),
        P("dp", None),
        P("pipe", "dp", None),
        P("pipe", "dp", None),
        P("pipe", None),
        P("pipe", None),
        P("pipe", None),
        P("pipe", None),
        P("pipe", None, None),
        P("dp", None),
    )
    out_specs = (
        P("pipe", "dp", None),
        P("pipe", "dp", None),
        P("pipe", "dp", None),
        P("pipe", "dp", None),
        P("pipe", "dp"),
        P("pipe", "dp"),
        P("pipe", "dp"),
        P("pipe", "dp"),
        P("pipe", "dp", None),
    )
    return jax.shard_map(body, mesh=mesh, in_specs=in_specs, out_specs=out_specs, check_vma=False)
```

```python
from functools import partial

import jax
import jax.numpy as jnp
from jax import lax
from jax.experimental import pallas as pl
from jax.experimental.pallas import tpu as pltpu
from jax.sharding import PartitionSpec as P

HEADS = 12
FF = 3072
EPSILON = 1e-05
LOW = jnp.bfloat16
WIDE = jnp.float32
MESH = pl.DeviceIdType.MESH
DMA = pltpu.SemaphoreType.DMA
BLOCKS = 4
ROWS = 48
WIDTH = 768


def place():
    group = lax.axis_index("dp")
    pipe = lax.axis_index("pipe")
    half = lax.div(group, 16)
    rest = lax.rem(group, 16)
    return group, pipe, half, lax.div(rest, 4), lax.rem(rest, 4)


def around(position, distance):
    return lax.rem(position + distance + 4, 4)


def group_of(half, depth, column):
    return half * 16 + depth * 4 + column


def along(route, first, second):
    return (second, first) if route == 0 else (first, second)


def to_group(src, dst, send, recv, group):
    return pltpu.make_async_remote_copy(
        src_ref=src,
        dst_ref=dst,
        send_sem=send,
        recv_sem=recv,
        device_id={"dp": group},
        device_id_type=MESH,
    )


def arrived(dst, recv):
    pltpu.make_async_copy(dst, dst, recv).wait()


def narrow(ref, route, block, half, first, second):
    depth, column = along(route, first, second)
    return ref.at[block, half, depth, column]


def wide(ref, route, block, half, second):
    if route == 0:
        return ref.at[block, half, second]
    return ref.at[block, half, :, second]


def greet(others):
    barrier = pltpu.get_barrier_semaphore()
    for device in others:
        pl.semaphore_signal(barrier, inc=1, device_id=device, device_id_type=MESH)
    pl.semaphore_wait(barrier, len(others))


def ring_devices():
    group, pipe, half, depth, column = place()
    return [
        {"dp": group_of(1 - half, depth, column)},
        {"dp": group_of(half, around(depth, 1), column)},
        {"dp": group_of(half, around(depth, -1), column)},
        {"dp": group_of(half, depth, around(column, 1))},
        {"dp": group_of(half, depth, around(column, -1))},
    ]


def gather_sems():
    return [DMA((BLOCKS,)), DMA((BLOCKS, 2, 2)), DMA((BLOCKS, 2)), DMA((BLOCKS, 2, 2)), DMA((BLOCKS, 2))]


class Gather:
    def __init__(self, ref, sends, recvs):
        self.ref, self.sends, self.recvs = ref, sends, recvs
        self.group, self.pipe, self.half, self.depth, self.column = place()

    def axes(self, route):
        return (self.column, self.depth) if route == 0 else (self.depth, self.column)

    def small_peer(self, route, distance):
        if route == 0:
            return group_of(self.half, self.depth, around(self.column, distance))
        return group_of(self.half, around(self.depth, distance), self.column)

    def large_peer(self, route, distance):
        return self.small_peer(1 - route, distance)

    def own(self, block):
        return self.ref.at[block, self.half, self.depth, self.column]

    def swap(self, block):
        slot = self.own(block)
        return to_group(
            slot, slot, self.sends[0].at[block], self.recvs[0].at[block],
            group_of(1 - self.half, self.depth, self.column),
        )

    def small(self, route, block, half, way):
        first, second = self.axes(route)
        slot = narrow(self.ref, route, block, half, first, second)
        return to_group(
            slot, slot, self.sends[1].at[block, half, way], self.recvs[1].at[block, half, way],
            self.small_peer(route, 1 - 2 * way),
        )

    def small_relay(self, route, block, way):
        first, second = self.axes(route)
        distance = 1 - 2 * way
        slot = narrow(self.ref, route, block, way, around(first, -distance), second)
        return to_group(
            slot, slot, self.sends[2].at[block, way], self.recvs[2].at[block, way],
            self.small_peer(route, distance),
        )

    def large(self, route, block, half, way):
        second = self.axes(route)[1]
        slot = wide(self.ref, route, block, half, second)
        return to_group(
            slot, slot, self.sends[3].at[block, half, way], self.recvs[3].at[block, half, way],
            self.large_peer(route, 1 - 2 * way),
        )

    def large_relay(self, route, block, way):
        second = self.axes(route)[1]
        distance = 1 - 2 * way
        slot = wide(self.ref, route, block, way, around(second, -distance))
        return to_group(
            slot, slot, self.sends[4].at[block, way], self.recvs[4].at[block, way],
            self.large_peer(route, distance),
        )

    def start(self, route, block):
        self.swap(block).start()
        for way in range(2):
            self.small(route, block, self.half, way).start()

    def second(self, route, block):
        self.swap(block).wait_recv()
        for way in range(2):
            self.small(route, block, 1 - self.half, way).start()

    def third(self, route, block):
        for way in range(2):
            self.small(route, block, way, way).wait_recv()
            self.small_relay(route, block, way).start()

    def fourth(self, route, block):
        for half in range(2):
            self.small(route, block, half, 1 - half).wait_recv()
            self.small_relay(route, block, half).wait_recv()
            for way in range(2):
                self.large(route, block, half, way).start()

    def fifth(self, route, block):
        for way in range(2):
            self.large(route, block, way, way).wait_recv()
            self.large_relay(route, block, way).start()

    def last(self, route, block):
        for way in range(2):
            self.large(route, block, way, 1 - way).wait_recv()
            self.large_relay(route, block, way).wait_recv()

    def finish(self, route, block):
        self.swap(block).wait_send()
        for way in range(2):
            for half in range(2):
                self.small(route, block, half, way).wait_send()
                self.large(route, block, half, way).wait_send()
            self.small_relay(route, block, way).wait_send()
            self.large_relay(route, block, way).wait_send()


def scatter_buffers(blocks, rows, width, dtype):
    return [
        pltpu.VMEM((blocks, 2, 4, rows, width), dtype),
        pltpu.VMEM((blocks, 2, 2, 4, rows, width), dtype),
        pltpu.VMEM((blocks, 2, rows, width), dtype),
        pltpu.VMEM((blocks, 2, 2, rows, width), dtype),
        pltpu.VMEM((blocks, rows, width), dtype),
    ]


def scatter_sems(blocks):
    return [DMA((blocks, 2)), DMA((blocks, 2, 2)), DMA((blocks, 2)), DMA((blocks, 2, 2)), DMA((blocks,))]


def accumulate(target, others):
    total = target[...].astype(WIDE)
    for other in others:
        total = total + other[...].astype(WIDE)
    target[...] = total.astype(target.dtype)


class Scatter(Gather):
    def __init__(self, ref, buffers, sends, recvs):
        super().__init__(ref, sends, recvs)
        self.buffers = buffers

    def large_early(self, route, block, way):
        second = self.axes(route)[1]
        return to_group(
            wide(self.ref, route, block, way, around(second, 2)), self.buffers[0].at[block, way],
            self.sends[0].at[block, way], self.recvs[0].at[block, way],
            self.large_peer(route, 1 - 2 * way),
        )

    def large(self, route, block, half, way):
        second = self.axes(route)[1]
        distance = 1 - 2 * way
        return to_group(
            wide(self.ref, route, block, half, around(second, distance)),
            self.buffers[1].at[block, way, half],
            self.sends[1].at[block, way, half], self.recvs[1].at[block, way, half],
            self.large_peer(route, distance),
        )

    def small_early(self, route, block, way):
        first, second = self.axes(route)
        return to_group(
            narrow(self.ref, route, block, way, around(first, 2), second),
            self.buffers[2].at[block, way],
            self.sends[2].at[block, way], self.recvs[2].at[block, way],
            self.small_peer(route, 1 - 2 * way),
        )

    def small(self, route, block, half, way):
        first, second = self.axes(route)
        distance = 1 - 2 * way
        return to_group(
            narrow(self.ref, route, block, half, around(first, distance), second),
            self.buffers[3].at[block, way, half],
            self.sends[3].at[block, way, half], self.recvs[3].at[block, way, half],
            self.small_peer(route, distance),
        )

    def swap(self, block):
        return to_group(
            self.ref.at[block, 1 - self.half, self.depth, self.column], self.buffers[4].at[block],
            self.sends[4].at[block], self.recvs[4].at[block],
            group_of(1 - self.half, self.depth, self.column),
        )

    def start(self, route, block):
        for way in range(2):
            self.large_early(route, block, way).start()
            self.large(route, block, 1 - way, way).start()

    def second(self, route, block):
        second = self.axes(route)[1]
        for way in range(2):
            self.large_early(route, block, way).wait_recv()
            accumulate(
                wide(self.ref, route, block, way, around(second, 1 - 2 * way)),
                [self.buffers[0].at[block, way]],
            )
            self.large(route, block, way, way).start()

    def third(self, route, block):
        first, second = self.axes(route)
        for half in range(2):
            for way in range(2):
                self.large(route, block, half, way).wait_recv()
            accumulate(
                wide(self.ref, route, block, half, second),
                [self.buffers[1].at[block, way, half] for way in range(2)],
            )
        for way in range(2):
            self.small_early(route, block, way).start()
            self.small(route, block, 1 - way, way).start()

    def fourth(self, route, block):
        first, second = self.axes(route)
        for way in range(2):
            self.small_early(route, block, way).wait_recv()
            accumulate(
                narrow(self.ref, route, block, way, around(first, 1 - 2 * way), second),
                [self.buffers[2].at[block, way]],
            )
            self.small(route, block, way, way).start()

    def fifth(self, route, block):
        for half in range(2):
            for way in range(2):
                self.small(route, block, half, way).wait_recv()
            accumulate(
                self.ref.at[block, half, self.depth, self.column],
                [self.buffers[3].at[block, way, half] for way in range(2)],
            )
        self.swap(block).start()

    def last(self, route, block):
        self.swap(block).wait_recv()
        accumulate(self.own(block), [self.buffers[4].at[block]])

    def finish(self, route, block):
        self.swap(block).wait_send()
        for way in range(2):
            self.large_early(route, block, way).wait_send()
            self.small_early(route, block, way).wait_send()
            for half in range(2):
                self.large(route, block, half, way).wait_send()
                self.small(route, block, half, way).wait_send()


STEPS = ("second", "third", "fourth", "fifth", "last", "finish")


class Total:
    def __init__(self, first, second, third, sends, recvs):
        self.stages, self.sends, self.recvs = (first, second, third), sends, recvs
        self.group, self.pipe, self.half, self.depth, self.column = place()
        self.where = (self.column, self.depth, self.half)

    def copy(self, stage, distance):
        here, buffer = self.where[stage], self.stages[stage]
        if stage == 0:
            peer = group_of(self.half, self.depth, around(here, distance))
        elif stage == 1:
            peer = group_of(self.half, around(here, distance), self.column)
        else:
            peer = group_of(1 - here, self.depth, self.column)
        return to_group(
            buffer.at[here], buffer.at[here],
            self.sends.at[stage, distance - 1], self.recvs.at[stage, distance - 1], peer,
        )

    def distances(self, stage):
        return range(1, 4) if stage < 2 else range(1, 2)

    def send(self, stage, value):
        self.stages[stage][self.where[stage]] = value
        for distance in self.distances(stage):
            self.copy(stage, distance).start()

    def receive(self, stage):
        for distance in self.distances(stage):
            self.copy(stage, distance).wait_recv()
        total = self.stages[stage][0]
        for index in range(1, 4 if stage < 2 else 2):
            total = total + self.stages[stage][index]
        return total

    def finish(self):
        for stage in range(3):
            for distance in self.distances(stage):
                self.copy(stage, distance).wait_send()


def total_scratch(shape):
    return [
        pltpu.VMEM((4,) + shape, WIDE),
        pltpu.VMEM((4,) + shape, WIDE),
        pltpu.VMEM((2,) + shape, WIDE),
        DMA((3, 3)),
        DMA((3, 3)),
    ]


def all_dp_devices():
    group, pipe, half, depth, column = place()
    return ring_devices() + [
        {"dp": group_of(half, around(depth, 2), column)},
        {"dp": group_of(half, depth, around(column, 2))},
    ]


PAIRS = HEADS // 2
SEQ = 128
REGIONS = 256
TOKENS = 8192
CHUNKS = 4


def dot(left, right):
    return lax.dot_general(left, right, (((1,), (0,)), ((), ())), preferred_element_type=WIDE)


def dot_nt(left, right):
    return lax.dot_general(left, right, (((1,), (1,)), ((), ())), preferred_element_type=WIDE)


def dot_tn(left, right):
    return lax.dot_general(left, right, (((0,), (0,)), ((), ())), preferred_element_type=WIDE)


def cols(index, width=WIDTH):
    return slice(index * width, (index + 1) * width)


def two_heads(pair):
    lane = lax.broadcasted_iota(jnp.int32, pair.shape, 1)
    zero = jnp.zeros_like(pair)
    return jnp.concatenate([jnp.where(lane < 64, pair, zero), jnp.where(lane < 64, zero, pair)], 0)


def side_by_side(stacked):
    return jnp.concatenate([stacked[:SEQ], stacked[SEQ:]], 1)


def row_mean(value):
    return jnp.mean(value, -1, keepdims=True)


def chain_scratch():
    return dict(
        proj=pltpu.VMEM((CHUNKS, WIDTH, WIDTH), LOW),
        fin=pltpu.VMEM((2, SEQ, WIDTH), LOW),
        bin=pltpu.VMEM((2, SEQ, WIDTH), LOW),
        lowered=pltpu.VMEM((2, SEQ, WIDTH), LOW),
        normed=pltpu.VMEM((2, SEQ, WIDTH), WIDE),
        inverse=pltpu.VMEM((2, SEQ, 128), WIDE),
        normed_rows=pltpu.VMEM((REGIONS, WIDTH), WIDE),
        region_info=pltpu.VMEM((8, WIDTH), WIDE),
        qkv=pltpu.VMEM((2, SEQ, 3 * WIDTH), LOW),
        probs=pltpu.VMEM((2, PAIRS, 2 * SEQ, SEQ), WIDE),
        mixed=pltpu.VMEM((2, SEQ, WIDTH), LOW),
        dbranch=pltpu.VMEM((2, SEQ, WIDTH), LOW),
        dwide=pltpu.VMEM((2, SEQ, FF), LOW),
        act=pltpu.VMEM((2, SEQ, FF), LOW),
        slope=pltpu.VMEM((2, SEQ, FF), WIDE),
        dweight=pltpu.VMEM((2, WIDTH, WIDTH), WIDE),
        send=DMA((2, 2)),
        recv=DMA((2, 2)),
    )


def unpack_proj(full_ref, proj_ref):
    def run(index, _):
        half, depth = lax.div(index, 4), lax.rem(index, 4)
        rows = pl.ds(pl.multiple_of(index * 96, 96), 96)
        for block in range(2):
            value = full_ref[block, half, depth].astype(WIDE).reshape(12, 2, 8, WIDTH)
            for side in range(2):
                proj_ref[2 * side + block, rows] = value[:, side].reshape(96, WIDTH).astype(LOW)
        return 0

    lax.fori_loop(0, 8, run, 0)


class Chain:
    def __init__(self, args, full_ref, counts, outs, grads, s):
        self.args, self.full, self.outs, self.grads, self.s = args, full_ref, outs, grads, s
        self.pipe = lax.axis_index("pipe")
        self.attention = lax.rem(self.pipe, 2) == 0
        self.region_statistics(counts)

    def region_statistics(self, counts):
        table_ref, s = self.args["table"], self.s
        column = jnp.transpose(jnp.broadcast_to(counts[0:1], (SEQ, REGIONS)))
        for index in range(WIDTH // 128):
            lanes = cols(index, 128)
            table = table_ref[:, lanes].astype(WIDE)
            mean = jnp.sum(table * column, 0, keepdims=True) / TOKENS
            second = jnp.sum(table * table * column, 0, keepdims=True) / TOKENS
            inverse = lax.rsqrt(second - mean * mean + EPSILON)
            s["normed_rows"][:, lanes] = (table - mean) * inverse
            s["region_info"][0:1, lanes] = mean
            s["region_info"][1:2, lanes] = inverse
            s["region_info"][2:3, lanes] = inverse * self.args["bn_gain"][0:1, lanes]

    def marks(self, micro):
        ids = self.args["region_ids"][pl.ds(micro, 1), :]
        rank = lax.broadcasted_iota(jnp.int32, (REGIONS, SEQ), 0)
        return jnp.where(rank == ids, 1.0, 0.0).astype(LOW)

    def same_document(self, micro):
        ids = jnp.broadcast_to(self.args["doc_ids"][pl.ds(micro, 1), :].astype(WIDE), (SEQ, SEQ))
        same = jnp.where(ids == jnp.transpose(ids), 1.0, 0.0)
        return jnp.concatenate([same, same], 0) > 0.5

    def down(self, index):
        return self.full[2 + index // 2, index % 2].reshape(WIDTH, WIDTH)

    def hop(self, direction, micro):
        source, target = (self.outs["acts"], self.s["fin"]) if direction == 0 else (self.outs["dins"], self.s["bin"])
        return pltpu.make_async_remote_copy(
            src_ref=source.at[micro], dst_ref=target.at[micro],
            send_sem=self.s["send"].at[direction, micro], recv_sem=self.s["recv"].at[direction, micro],
            device_id={"pipe": lax.rem(self.pipe + 1 + 2 * direction, 4)}, device_id_type=MESH,
        )

    def forward(self, micro):
        s, args = self.s, self.args

        @pl.when(self.pipe == 0)
        def _():
            s["fin"][micro] = args["tokens"][micro]

        @pl.when(self.pipe > 0)
        def _():
            self.hop(0, micro).wait_recv()

        embedded = dot_tn(self.marks(micro), args["table"][...])
        info = s["region_info"]
        summed = (
            s["fin"][micro].astype(WIDE)
            + (embedded - info[0:1]) * info[2:3] + args["bn_bias"][...]
        )
        lowered = summed.astype(LOW)
        s["lowered"][micro] = lowered
        s["normed"][micro] = summed

        @pl.when(self.attention)
        def _():
            self.attention_forward(micro, lowered)

        @pl.when(jnp.logical_not(self.attention))
        def _():
            self.feed_forward(micro, lowered)

        residual = s["normed"][micro]
        centered = residual - row_mean(residual)
        inverse = lax.rsqrt(row_mean(centered * centered) + EPSILON)
        normed = centered * inverse
        s["normed"][micro] = normed
        s["inverse"][micro] = jnp.broadcast_to(inverse, (SEQ, 128))
        self.outs["acts"][micro] = (normed * args["ln_gain"][...] + args["ln_bias"][...]).astype(LOW)

        @pl.when(self.pipe < 3)
        def _():
            self.hop(0, micro).start()

    def attention_forward(self, micro, lowered):
        s = self.s
        for index in range(3):
            s["qkv"][micro, :, cols(index)] = dot(lowered, s["proj"][index]).astype(LOW)
        same = self.same_document(micro)
        for pair in range(PAIRS):
            queries = two_heads(s["qkv"][micro, :, cols(pair, 128)])
            keys = s["qkv"][micro, :, cols(PAIRS + pair, 128)]
            values = two_heads(s["qkv"][micro, :, cols(2 * PAIRS + pair, 128)])
            scores = jnp.where(same, dot_nt(queries, keys) * 0.125, -1e30)
            powers = jnp.exp(scores - jnp.max(scores, -1, keepdims=True))
            probs = powers / jnp.sum(powers, -1, keepdims=True)
            s["probs"][micro, pair] = probs
            s["mixed"][micro, :, cols(pair, 128)] = dot(side_by_side(probs.astype(LOW)), values).astype(LOW)
        s["normed"][micro] = s["normed"][micro] + dot(s["mixed"][micro], s["proj"][3])

    def feed_forward(self, micro, lowered):
        s = self.s
        branch = s["normed"][micro]
        for index in range(CHUNKS):
            hidden = dot(lowered, s["proj"][index])
            cumulative = 0.5 * (1.0 + lax.erf(hidden * (0.5 ** 0.5)))
            density = jnp.exp(hidden * hidden * -0.5) * 0.3989422804014327
            act = (hidden * cumulative).astype(LOW)
            s["act"][micro, :, cols(index)] = act
            s["slope"][micro, :, cols(index)] = cumulative + hidden * density
            branch = branch + dot(act, self.down(index))
        s["normed"][micro] = branch

    def backward(self, micro):
        s, args = self.s, self.args

        @pl.when(self.pipe == 3)
        def _():
            s["bin"][micro] = args["out_cot"][micro]

        @pl.when(self.pipe < 3)
        def _():
            self.hop(1, micro).wait_recv()

        gout = s["bin"][micro].astype(WIDE)
        normed = s["normed"][micro]
        stats = self.outs["stats"]
        stats[2:3] = stats[2:3] + jnp.sum(gout * normed, 0, keepdims=True)
        stats[3:4] = stats[3:4] + jnp.sum(gout, 0, keepdims=True)
        dnormed = gout * args["ln_gain"][...]
        dres = s["inverse"][micro][:, 0:1] * (
            dnormed - row_mean(dnormed) - normed * row_mean(dnormed * normed)
        )
        s["normed"][micro] = dres
        s["dbranch"][micro] = dres.astype(LOW)

        @pl.when(self.attention)
        def _():
            self.attention_backward(micro)

        @pl.when(jnp.logical_not(self.attention))
        def _():
            self.feed_backward(micro)

        dsum = s["normed"][micro]
        high = dsum.astype(LOW)
        self.outs["dins"][micro] = high

        @pl.when(self.pipe > 0)
        def _():
            self.hop(1, micro).start()

        marks = self.marks(micro)
        rest = (dsum - high.astype(WIDE)).astype(LOW)
        region = self.outs["region"]
        added = dot(marks, high) + dot(marks, rest)
        region[0] = region[0] + added.reshape(2, 4, 4, 8, WIDTH)

    def attention_backward(self, micro):
        s = self.s
        dmixed = dot_nt(s["dbranch"][micro], s["proj"][3]).astype(LOW)
        for pair in range(PAIRS):
            pieces = [s["qkv"][micro, :, cols(part * PAIRS + pair, 128)] for part in range(3)]
            queries, keys = two_heads(pieces[0]), two_heads(pieces[1])
            grads = two_heads(dmixed[:, cols(pair, 128)])
            probs = s["probs"][micro, pair]
            dprobs = dot_nt(grads, pieces[2])
            dscores = (probs * (dprobs - jnp.sum(dprobs * probs, -1, keepdims=True))).astype(LOW)
            dqueries = dot(side_by_side(dscores), keys) * 0.125
            dkeys = dot_tn(dscores, queries) * 0.125
            dvalues = dot_tn(probs.astype(LOW), grads)
            for part, value in enumerate((dqueries, dkeys, dvalues)):
                s["dwide"][micro, :, cols(part * PAIRS + pair, 128)] = value.astype(LOW)
        total = s["normed"][micro]
        for index in range(3):
            total = total + dot_nt(s["dwide"][micro, :, cols(index)], s["proj"][index])
        s["normed"][micro] = total

    def feed_backward(self, micro):
        s = self.s
        total = s["normed"][micro]
        dbranch = s["dbranch"][micro]
        for index in range(CHUNKS):
            dact = dot_nt(dbranch, self.down(index))
            dhidden = (dact * s["slope"][micro, :, cols(index)]).astype(LOW)
            s["dwide"][micro, :, cols(index)] = dhidden
            total = total + dot_nt(dhidden, s["proj"][index])
        s["normed"][micro] = total

    def weight_gradients(self, block):
        s = self.s
        lowered = s["lowered"][...].reshape(2 * SEQ, WIDTH)
        for side in range(2):
            quarter = 2 * side + block
            if quarter == 3:
                @pl.when(self.attention)
                def _():
                    left = s["mixed"][...].reshape(2 * SEQ, WIDTH)
                    s["dweight"][1] = dot_tn(left, s["dbranch"][...].reshape(2 * SEQ, WIDTH))

                @pl.when(jnp.logical_not(self.attention))
                def _():
                    right = s["dwide"][:, :, cols(3)].reshape(2 * SEQ, WIDTH)
                    s["dweight"][1] = dot_tn(lowered, right)
            else:
                right = s["dwide"][:, :, cols(quarter)].reshape(2 * SEQ, WIDTH)
                s["dweight"][side] = dot_tn(lowered, right)

        def run(index, _):
            half, depth = lax.div(index, 4), lax.rem(index, 4)
            rows = pl.ds(pl.multiple_of(index * 96, 96), 96)
            sides = [s["dweight"][side, rows].reshape(12, 1, 8, WIDTH) for side in range(2)]
            value = jnp.concatenate(sides, 1).reshape(4, ROWS, WIDTH)
            self.grads[block, half, depth] = value.astype(LOW)
            return 0

        lax.fori_loop(0, 8, run, 0)

    def down_gradients(self, block):
        s = self.s
        dbranch = s["dbranch"][...].reshape(2 * SEQ, WIDTH)
        for half in range(2):
            act = s["act"][:, :, cols(2 * (block - 2) + half)].reshape(2 * SEQ, WIDTH)
            self.grads[block, half] = dot_tn(act, dbranch).astype(LOW).reshape(4, 4, ROWS, WIDTH)

    def start_stats(self):
        self.outs["stats"][...] = jnp.zeros((8, WIDTH), WIDE)
        self.outs["region"][...] = jnp.zeros((1, 2, 4, 4, 8, WIDTH), WIDE)

    def end_stats(self):
        region, stats = self.outs["region"][0].reshape(REGIONS, WIDTH), self.outs["stats"]
        stats[0:1] = jnp.sum(region, 0, keepdims=True)
        stats[1:2] = jnp.sum(region * self.s["normed_rows"][...], 0, keepdims=True)

    def each(self, action):
        lax.fori_loop(0, 2, lambda micro, _: (action(micro), 0)[1], 0)

    def finish(self):
        def run(micro):
            @pl.when(self.pipe < 3)
            def _():
                self.hop(0, micro).wait_send()

            @pl.when(self.pipe > 0)
            def _():
                self.hop(1, micro).wait_send()

        self.each(run)


ARGS = ("tokens", "doc_ids", "region_ids", "ln_gain", "ln_bias", "bn_gain", "bn_bias", "table", "out_cot")
def pack_proj(proj_ref, gather):
    for block in range(2):
        parts = []
        for turn in range(3):
            rows = slice(8 * turn, 8 * turn + 8)
            for side in range(2):
                parts.append(proj_ref[0, rows, cols(2 * side + block)].astype(WIDE))
        gather.own(block)[...] = jnp.concatenate(parts, 0).astype(LOW)


def own_counts(region_ids_ref):
    rank = lax.broadcasted_iota(jnp.int32, (REGIONS, SEQ), 0)
    total = jnp.zeros((8, REGIONS), WIDE)
    for micro in range(2):
        marks = jnp.where(rank == region_ids_ref[micro : micro + 1, :], 1.0, 0.0).astype(LOW)
        total = total + dot_nt(jnp.ones((8, SEQ), LOW), marks)
    return total


FAR = ("tokens", "table", "out_cot")


def whole_kernel(*refs):
    refs = list(refs)

    def take(count):
        taken = refs[:count]
        del refs[:count]
        return taken

    given = dict(zip(ARGS, take(len(ARGS))))
    proj_in, down_in = take(2)
    acts, dins, proj_out, down_out, table_out, summed_out, counts_out = take(7)
    local_sem, cross_send, cross_recv = take(3)
    s = dict(zip(chain_scratch(), take(len(chain_scratch()))))
    near = dict(zip(FAR, take(len(FAR))))
    full = take(1)[0]
    gather = Gather(full, take(5), take(5))
    counted = Total(*take(5))
    held, region_held, stats = take(3)
    main = Scatter(held, take(5), take(5), take(5))
    region = Scatter(region_held, take(5), take(5), take(5))
    total = Total(*take(5))

    pipe = gather.pipe
    ffn = lax.rem(pipe, 2) == 1
    pairs = lax.rem(pipe, 2) + 1
    sibling = pipe + 1 - 2 * lax.rem(pipe, 2)
    fetches = [
        pltpu.make_async_copy(given[name], near[name], local_sem.at[index]) for index, name in enumerate(FAR)
    ]
    for fetch in fetches:
        fetch.start()
    pack_proj(proj_in, gather)
    gather.own(3)[...] = down_in[0]
    greet(all_dp_devices() + [{"pipe": lax.rem(pipe + 1, 4)}, {"pipe": lax.rem(pipe + 3, 4)}])
    for route in range(2):
        gather.start(route, route)
    cross = pltpu.make_async_remote_copy(
        src_ref=gather.own(3), dst_ref=gather.own(2), send_sem=cross_send.at[0], recv_sem=cross_recv.at[0],
        device_id={"pipe": sibling}, device_id_type=MESH,
    )

    @pl.when(jnp.logical_not(ffn))
    def _():
        cross.start()

    @pl.when(ffn)
    def _():
        gather.start(1, 3)
        cross.wait_recv()
        gather.start(0, 2)

    counted.send(0, own_counts(given["region_ids"]))

    def each(action):
        def run(pair, _):
            for route in range(2):
                action(route, 2 * pair + route)
            return 0

        lax.fori_loop(0, pairs, run, 0)

    for index, step in enumerate(STEPS[:5]):
        each(getattr(gather, step))
        if index < 2:
            counted.send(index + 1, counted.receive(index))
        elif index == 2:
            counts_out[...] = counted.receive(2)
    for fetch in fetches:
        fetch.wait()
    unpack_proj(full, s["proj"])
    args = dict(given, **near)
    outs = dict(acts=acts, dins=dins, stats=stats, region=region_held)
    chain = Chain(args, full, counts_out[...], outs, held, s)
    chain.start_stats()
    chain.each(chain.forward)
    chain.each(chain.backward)
    chain.end_stats()
    region.start(0, 0)
    total.send(0, stats[...])
    for block in range(2):
        chain.weight_gradients(block)
        main.start(block, block)

    @pl.when(ffn)
    def _():
        for block in range(2, 4):
            chain.down_gradients(block)
            main.start(block - 2, block)

    for index, step in enumerate(STEPS[:5]):
        each(getattr(main, step))
        getattr(region, step)(0, 0)
        if index < 2:
            total.send(index + 1, total.receive(index))
        elif index == 2:
            summed_out[...] = total.receive(2)
    back = pltpu.make_async_remote_copy(
        src_ref=main.own(2), dst_ref=down_out, send_sem=cross_send.at[1], recv_sem=cross_recv.at[1],
        device_id={"pipe": sibling}, device_id_type=MESH,
    )

    @pl.when(ffn)
    def _():
        back.start()
        down_out[...] = main.own(3)[...]

    for block in range(2):
        proj_out[block] = main.own(block)[...]
    table_out[...] = region.own(0)[...]
    each(gather.finish)
    each(main.finish)
    region.finish(0, 0)
    counted.finish()
    total.finish()
    chain.finish()

    @pl.when(ffn)
    def _():
        back.wait_send()

    @pl.when(jnp.logical_not(ffn))
    def _():
        cross.wait_send()
        back.wait_recv()


def run_whole(args, proj, down):
    micro = (2, SEQ, WIDTH)
    vmem, far = pl.BlockSpec(memory_space=pltpu.VMEM), pl.BlockSpec(memory_space=pl.ANY)
    out_shape = [
        jax.ShapeDtypeStruct(micro, LOW),
        jax.ShapeDtypeStruct(micro, LOW),
        jax.ShapeDtypeStruct((2, ROWS, WIDTH), LOW),
        jax.ShapeDtypeStruct((ROWS, WIDTH), LOW),
        jax.ShapeDtypeStruct((8, WIDTH), WIDE),
        jax.ShapeDtypeStruct((8, WIDTH), WIDE),
        jax.ShapeDtypeStruct((8, REGIONS), WIDE),
    ]
    blocks = (BLOCKS, 2, 4, 4, ROWS, WIDTH)
    scratch = [DMA((len(FAR),)), DMA((2,)), DMA((2,))]
    scratch += list(chain_scratch().values())
    scratch += [pltpu.VMEM(args[name].shape, args[name].dtype) for name in FAR]
    scratch += [pltpu.VMEM(blocks, LOW)] + gather_sems() + gather_sems()
    scratch += total_scratch((8, REGIONS))
    scratch += [pltpu.VMEM(blocks, LOW), pltpu.VMEM((1, 2, 4, 4, 8, WIDTH), WIDE), pltpu.VMEM((8, WIDTH), WIDE)]
    scratch += scatter_buffers(BLOCKS, ROWS, WIDTH, LOW) + scatter_sems(BLOCKS) + scatter_sems(BLOCKS)
    scratch += scatter_buffers(1, 8, WIDTH, WIDE) + scatter_sems(1) + scatter_sems(1)
    scratch += total_scratch((8, WIDTH))
    return pl.pallas_call(
        whole_kernel,
        out_shape=out_shape,
        in_specs=[far if name in FAR else vmem for name in ARGS] + [vmem] * 2,
        out_specs=[vmem] * len(out_shape),
        scratch_shapes=scratch,
        compiler_params=pltpu.CompilerParams(
            collective_id=0, has_side_effects=True, vmem_limit_bytes=62 * 2**20
        ),
    )(*[args[name] for name in ARGS], proj, down)


def body(
    tokens, doc_ids, region_ids, proj, down, ln_gain, ln_bias, bn_gain, bn_bias, region_table, out_cot
):
    group = lax.axis_index("dp")
    args = dict(
        tokens=tokens.reshape(2, SEQ, WIDTH), doc_ids=doc_ids, region_ids=region_ids, ln_gain=ln_gain,
        ln_bias=ln_bias, bn_gain=bn_gain, bn_bias=bn_bias, table=region_table[0],
        out_cot=out_cot.reshape(2, SEQ, WIDTH),
    )
    acts, dins, proj_sum, down_sum, table_sum, summed_stats, counted = run_whole(args, proj, down)
    counts = counted[0]
    wide_table = region_table[0].astype(WIDE)
    mean = jnp.sum(counts[:, None] * wide_table, 0) / TOKENS
    second = jnp.sum(counts[:, None] * wide_table * wide_table, 0) / TOKENS
    inverse = lax.rsqrt(second - mean * mean + EPSILON)
    bias_sum, gain_sum = summed_stats[0], summed_stats[1]
    own_counts = lax.dynamic_slice_in_dim(counts, group * 8, 8, 0)
    own_normed = (lax.dynamic_slice_in_dim(wide_table, group * 8, 8, 0) - mean) * inverse
    table_grad = bn_gain[0] * inverse * (
        table_sum - own_counts[:, None] * (bias_sum / TOKENS + own_normed * (gain_sum / TOKENS))
    )
    proj_out = proj_sum.transpose(1, 0, 2).reshape(3, 2, 8, 1536).transpose(0, 2, 1, 3).reshape(24, FF)
    shares = lax.dynamic_slice_in_dim(summed_stats, group * 24, 24, 1)
    return (
        acts.reshape(1, 2 * SEQ, WIDTH),
        dins.reshape(1, 2 * SEQ, WIDTH),
        proj_out.astype(WIDE)[None],
        down_sum.astype(WIDE)[None],
        shares[2][None],
        shares[3][None],
        shares[1][None],
        shares[0][None],
        table_grad[None],
    )


def solution(mesh):
    in_specs = (
        P("dp", None),
        P("dp", None),
        P("dp", None),
        P("pipe", "dp", None),
        P("pipe", "dp", None),
        P("pipe", None),
        P("pipe", None),
        P("pipe", None),
        P("pipe", None),
        P("pipe", None, None),
        P("dp", None),
    )
    out_specs = (
        P("pipe", "dp", None),
        P("pipe", "dp", None),
        P("pipe", "dp", None),
        P("pipe", "dp", None),
        P("pipe", "dp"),
        P("pipe", "dp"),
        P("pipe", "dp"),
        P("pipe", "dp"),
        P("pipe", "dp", None),
    )
    return jax.shard_map(body, mesh=mesh, in_specs=in_specs, out_specs=out_specs, check_vma=False)
```

```python
from functools import partial

import jax
import jax.numpy as jnp
from jax import lax
from jax.experimental import pallas as pl
from jax.experimental.pallas import tpu as pltpu
from jax.sharding import PartitionSpec as P

HEADS = 12
FF = 3072
EPSILON = 1e-05
LOW = jnp.bfloat16
WIDE = jnp.float32
MESH = pl.DeviceIdType.MESH
DMA = pltpu.SemaphoreType.DMA
BLOCKS = 4
ROWS = 48
WIDTH = 768


def place():
    group = lax.axis_index("dp")
    pipe = lax.axis_index("pipe")
    half = lax.div(group, 16)
    rest = lax.rem(group, 16)
    return group, pipe, half, lax.div(rest, 4), lax.rem(rest, 4)


def around(position, distance):
    return lax.rem(position + distance + 4, 4)


def group_of(half, depth, column):
    return half * 16 + depth * 4 + column


def along(route, first, second):
    return (second, first) if route == 0 else (first, second)


def to_group(src, dst, send, recv, group):
    return pltpu.make_async_remote_copy(
        src_ref=src,
        dst_ref=dst,
        send_sem=send,
        recv_sem=recv,
        device_id={"dp": group},
        device_id_type=MESH,
    )


def arrived(dst, recv):
    pltpu.make_async_copy(dst, dst, recv).wait()


def narrow(ref, route, block, half, first, second):
    depth, column = along(route, first, second)
    return ref.at[block, half, depth, column]


def wide(ref, route, block, half, second):
    if route == 0:
        return ref.at[block, half, second]
    return ref.at[block, half, :, second]


def greet(others):
    barrier = pltpu.get_barrier_semaphore()
    for device in others:
        pl.semaphore_signal(barrier, inc=1, device_id=device, device_id_type=MESH)
    pl.semaphore_wait(barrier, len(others))


def ring_devices():
    group, pipe, half, depth, column = place()
    return [
        {"dp": group_of(1 - half, depth, column)},
        {"dp": group_of(half, around(depth, 1), column)},
        {"dp": group_of(half, around(depth, -1), column)},
        {"dp": group_of(half, depth, around(column, 1))},
        {"dp": group_of(half, depth, around(column, -1))},
    ]


def gather_sems():
    return [DMA((BLOCKS,)), DMA((BLOCKS, 3)), DMA((BLOCKS, 2, 2)), DMA((BLOCKS, 2, 2))]


def part(ref, way):
    return ref.at[pl.ds(2 * way, 2)]


class Rings:
    def __init__(self, ref, sends, recvs):
        self.ref, self.sends, self.recvs = ref, sends, recvs
        self.group, self.pipe, self.half, self.depth, self.column = place()
        self.partner = group_of(1 - self.half, self.depth, self.column)

    def axes(self, route):
        return (self.column, self.depth) if route == 0 else (self.depth, self.column)

    def small_peer(self, route, distance):
        if route == 0:
            return group_of(self.half, self.depth, around(self.column, distance))
        return group_of(self.half, around(self.depth, distance), self.column)

    def large_peer(self, route, distance):
        return self.small_peer(1 - route, distance)

    def own(self, block):
        return self.ref.at[block, self.half, self.depth, self.column]

    def send(self, kind, index, src, dst, group):
        return to_group(src, dst, self.sends[kind].at[index], self.recvs[kind].at[index], group)


class Gather(Rings):
    def swap(self, route, block, half, position=None):
        second = self.axes(route)[1]
        slot = wide(self.ref, route, block, half, second)
        if position is not None:
            slot = narrow(self.ref, route, block, half, position, second)
        return self.send(0, (block,), slot, slot, self.partner)

    def small(self, route, block, distance):
        slot = self.own(block)
        return self.send(1, (block, distance - 1), slot, slot, self.small_peer(route, distance))

    def large(self, route, block, half, way, position=None):
        second = self.axes(route)[1]
        slot = wide(self.ref, route, block, half, second)
        if position is not None:
            slot = narrow(self.ref, route, block, half, position, second)
        return self.send(2, (block, half, way), slot, slot, self.large_peer(route, 1 - 2 * way))

    def large_relay(self, route, block, half, way):
        second = self.axes(route)[1]
        distance = 1 - 2 * way
        slot = part(wide(self.ref, route, block, half, around(second, -distance)), way)
        return self.send(3, (block, half, way), slot, slot, self.large_peer(route, distance))

    def pass_on(self, route, block, position):
        for way in range(2):
            self.large(route, block, self.half, way, position).start()
        self.swap(route, block, self.half, position).start()

    def start(self, route, block):
        for distance in range(1, 4):
            self.small(route, block, distance).start()
        self.pass_on(route, block, self.axes(route)[0])

    def end_small(self, route, block):
        for distance in (1, 3, 2):
            self.small(route, block, distance).wait_recv()
            self.pass_on(route, block, around(self.axes(route)[0], -distance))

    def relay_large(self, route, block, half):
        for way in range(2):
            self.large(route, block, half, way).wait_recv()
            self.large_relay(route, block, half, way).start()

    def swap_in(self, route, block):
        self.swap(route, block, 1 - self.half).wait_recv()
        for way in range(2):
            self.large(route, block, 1 - self.half, way).start()
        self.relay_large(route, block, self.half)

    def last(self, route, block):
        for half in range(2):
            for way in range(2):
                self.large_relay(route, block, half, way).wait_recv()

    def steps(self):
        return [
            self.end_small,
            self.swap_in,
            lambda route, block: self.relay_large(route, block, 1 - self.half),
        ]

    def finish(self, route, block):
        self.swap(route, block, self.half).wait_send()
        for distance in range(1, 4):
            self.small(route, block, distance).wait_send()
        for half in range(2):
            for way in range(2):
                self.large(route, block, half, way).wait_send()
                self.large_relay(route, block, half, way).wait_send()


def scatter_buffers(blocks, rows, dtype):
    return [
        pltpu.VMEM((blocks, 2, 4, rows, WIDTH), dtype),
        pltpu.VMEM((blocks, 2, 2, 4, rows, WIDTH), dtype),
        pltpu.VMEM((blocks, 4, rows, WIDTH), dtype),
        pltpu.VMEM((blocks, 3, rows, WIDTH), dtype),
    ]


def scatter_sems(blocks):
    return [DMA((blocks, 2, 2)), DMA((blocks, 2, 2)), DMA((blocks,)), DMA((blocks, 3))]


def accumulate(target, others):
    total = target[...].astype(WIDE)
    for other in others:
        total = total + other[...].astype(WIDE)
    target[...] = total.astype(target.dtype)


class Scatter(Rings):
    def __init__(self, ref, buffers, sends, recvs, single=False):
        super().__init__(ref, sends, recvs)
        self.buffers, self.single = buffers, single

    def large_early(self, route, block, half, way):
        second = self.axes(route)[1]
        return self.send(
            0, (block, half, way), part(wide(self.ref, route, block, half, around(second, 2)), way),
            part(self.buffers[0].at[block, half], way), self.large_peer(route, 1 - 2 * way),
        )

    def large(self, route, block, half, way, side=None):
        second = self.axes(route)[1]
        distance = 1 - 2 * way
        src = wide(self.ref, route, block, half, around(second, distance))
        dst = self.buffers[1].at[block, way, half]
        if side is not None:
            src, dst = part(src, side), part(dst, side)
        return self.send(1, (block, way, half), src, dst, self.large_peer(route, distance))

    def swap(self, route, block, half):
        second = self.axes(route)[1]
        return self.send(
            2, (block,), wide(self.ref, route, block, half, second), self.buffers[2].at[block], self.partner
        )

    def target(self, route, block, distance):
        first, second = self.axes(route)
        half = 0 if self.single else self.half
        return narrow(self.ref, route, block, half, around(first, distance), second)

    def small(self, route, block, distance):
        return self.send(
            3, (block, distance - 1), self.target(route, block, distance), self.buffers[3].at[block, distance - 1],
            self.small_peer(route, distance),
        )

    def where(self, half, action):
        if self.single:
            pl.when(half == 0)(lambda: action(0))
        else:
            action(half)

    def begin(self, route, block, half):
        def run(half):
            for way in range(2):
                self.large_early(route, block, half, way).start()
                self.large(route, block, half, way, 1 - way).start()

        self.where(half, run)

    def middle(self, route, block, half):
        def run(half):
            second = self.axes(route)[1]
            for way in range(2):
                self.large_early(route, block, half, way).wait_recv()
                accumulate(
                    part(wide(self.ref, route, block, half, around(second, 1 - 2 * way)), way),
                    [part(self.buffers[0].at[block, half], way)],
                )
                self.large(route, block, half, way, way).start()

        self.where(half, run)

    def sum_large(self, route, block, half, others):
        for way in range(2):
            self.large(route, block, half, way).wait_recv()
        arrivals = [self.buffers[1].at[block, way, half] for way in range(2)]
        accumulate(wide(self.ref, route, block, half, self.axes(route)[1]), arrivals + others)

    def start(self, route, block):
        self.begin(route, block, 1 - self.half)

    def turn(self, route, block):
        self.middle(route, block, 1 - self.half)
        self.begin(route, block, self.half)

    def sum_other(self, route, block):
        def run(half):
            self.sum_large(route, block, half, [])
            self.swap(route, block, half).start()

        self.where(1 - self.half, run)

    def sum_own(self, route, block):
        def run(half):
            self.swap(route, block, half).wait_recv()
            self.sum_large(route, block, half, [self.buffers[2].at[block]])
            for distance in range(1, 4):
                self.small(route, block, distance).start()

        self.where(self.half, run)

    def last(self, route, block):
        def run(half):
            for distance in range(1, 4):
                self.small(route, block, distance).wait_recv()
            arrivals = [self.buffers[3].at[block, index] for index in range(3)]
            accumulate(self.target(route, block, 0), arrivals)

        self.where(self.half, run)

    def steps(self):
        return [
            self.turn,
            self.sum_other,
            lambda route, block: self.middle(route, block, self.half),
            self.sum_own,
            self.last,
        ]

    def finish(self, route, block):
        def large(half):
            for way in range(2):
                self.large_early(route, block, half, way).wait_send()
                self.large(route, block, half, way).wait_send()

        def other(half):
            large(half)
            self.swap(route, block, half).wait_send()

        def own(half):
            large(half)
            for distance in range(1, 4):
                self.small(route, block, distance).wait_send()

        self.where(1 - self.half, other)
        self.where(self.half, own)


class Total:
    def __init__(self, first, second, third, sends, recvs):
        self.stages, self.sends, self.recvs = (first, second, third), sends, recvs
        self.group, self.pipe, self.half, self.depth, self.column = place()
        self.where = (self.column, self.depth, self.half)

    def copy(self, stage, distance):
        here, buffer = self.where[stage], self.stages[stage]
        if stage == 0:
            peer = group_of(self.half, self.depth, around(here, distance))
        elif stage == 1:
            peer = group_of(self.half, around(here, distance), self.column)
        else:
            peer = group_of(1 - here, self.depth, self.column)
        return to_group(
            buffer.at[here], buffer.at[here],
            self.sends.at[stage, distance - 1], self.recvs.at[stage, distance - 1], peer,
        )

    def distances(self, stage):
        return range(1, 4) if stage < 2 else range(1, 2)

    def send(self, stage, value):
        self.stages[stage][self.where[stage]] = value
        for distance in self.distances(stage):
            self.copy(stage, distance).start()

    def receive(self, stage):
        for distance in self.distances(stage):
            self.copy(stage, distance).wait_recv()
        total = self.stages[stage][0]
        for index in range(1, 4 if stage < 2 else 2):
            total = total + self.stages[stage][index]
        return total

    def finish(self):
        for stage in range(3):
            for distance in self.distances(stage):
                self.copy(stage, distance).wait_send()


def total_scratch(shape):
    return [
        pltpu.VMEM((4,) + shape, WIDE),
        pltpu.VMEM((4,) + shape, WIDE),
        pltpu.VMEM((2,) + shape, WIDE),
        DMA((3, 3)),
        DMA((3, 3)),
    ]


def all_dp_devices():
    group, pipe, half, depth, column = place()
    return ring_devices() + [
        {"dp": group_of(half, around(depth, 2), column)},
        {"dp": group_of(half, depth, around(column, 2))},
    ]


PAIRS = HEADS // 2
SEQ = 128
REGIONS = 128
TOKENS = 8192
CHUNKS = 4


def dot(left, right):
    return lax.dot_general(left, right, (((1,), (0,)), ((), ())), preferred_element_type=WIDE)


def dot_nt(left, right):
    return lax.dot_general(left, right, (((1,), (1,)), ((), ())), preferred_element_type=WIDE)


def dot_tn(left, right):
    return lax.dot_general(left, right, (((0,), (0,)), ((), ())), preferred_element_type=WIDE)


def cols(index, width=WIDTH):
    return slice(index * width, (index + 1) * width)


def two_heads(pair):
    lane = lax.broadcasted_iota(jnp.int32, pair.shape, 1)
    zero = jnp.zeros_like(pair)
    return jnp.concatenate([jnp.where(lane < 64, pair, zero), jnp.where(lane < 64, zero, pair)], 0)


def side_by_side(stacked):
    return jnp.concatenate([stacked[:SEQ], stacked[SEQ:]], 1)


def row_mean(value):
    return jnp.mean(value, -1, keepdims=True)


def chain_scratch():
    return dict(
        proj=pltpu.VMEM((CHUNKS, WIDTH, WIDTH), LOW),
        fin=pltpu.VMEM((2, SEQ, WIDTH), LOW),
        bin=pltpu.VMEM((2, SEQ, WIDTH), LOW),
        lowered=pltpu.VMEM((2, SEQ, WIDTH), LOW),
        normed=pltpu.VMEM((2, SEQ, WIDTH), WIDE),
        inverse=pltpu.VMEM((2, SEQ, 128), WIDE),
        normed_rows=pltpu.VMEM((REGIONS, WIDTH), WIDE),
        region_info=pltpu.VMEM((8, WIDTH), WIDE),
        column=pltpu.VMEM((REGIONS, 128), WIDE),
        qkv=pltpu.VMEM((2, SEQ, 3 * WIDTH), LOW),
        probs=pltpu.VMEM((2, PAIRS, 2 * SEQ, SEQ), WIDE),
        mixed=pltpu.VMEM((2, SEQ, WIDTH), LOW),
        dbranch=pltpu.VMEM((2, SEQ, WIDTH), LOW),
        dwide=pltpu.VMEM((2, SEQ, FF), LOW),
        act=pltpu.VMEM((2, SEQ, FF), LOW),
        slope=pltpu.VMEM((2, SEQ, FF), WIDE),
        dweight=pltpu.VMEM((2, WIDTH, WIDTH), WIDE),
        send=DMA((2, 2)),
        recv=DMA((2, 2)),
    )


def unpack_proj(full_ref, proj_ref):
    def run(index, _):
        half, depth = lax.div(index, 4), lax.rem(index, 4)
        rows = pl.ds(pl.multiple_of(index * 96, 96), 96)
        for block in range(2):
            value = full_ref[block, half, depth].astype(WIDE).reshape(12, 2, 8, WIDTH)
            for side in range(2):
                proj_ref[2 * side + block, rows] = value[:, side].reshape(96, WIDTH).astype(LOW)
        return 0

    lax.fori_loop(0, 8, run, 0)


class Chain:
    def __init__(self, args, full_ref, counts, outs, grads, s, await_down, send_down):
        self.await_down, self.send_down = await_down, send_down
        self.args, self.full, self.outs, self.grads, self.s = args, full_ref, outs, grads, s
        self.pipe = lax.axis_index("pipe")
        self.attention = lax.rem(self.pipe, 2) == 0
        self.region_statistics(counts)

    def region_statistics(self, counts):
        table_ref, s = self.args["table"], self.s
        column = jnp.transpose(jnp.broadcast_to(counts[0:1], (SEQ, REGIONS)))
        s["column"][...] = column
        for index in range(WIDTH // 128):
            lanes = cols(index, 128)
            table = table_ref[:, lanes].astype(WIDE)
            mean = jnp.sum(table * column, 0, keepdims=True) / TOKENS
            second = jnp.sum(table * table * column, 0, keepdims=True) / TOKENS
            inverse = lax.rsqrt(second - mean * mean + EPSILON)
            s["normed_rows"][:, lanes] = (table - mean) * inverse
            s["region_info"][0:1, lanes] = mean
            s["region_info"][1:2, lanes] = inverse
            s["region_info"][2:3, lanes] = inverse * self.args["bn_gain"][0:1, lanes]

    def marks(self, micro):
        ids = self.args["region_ids"][pl.ds(micro, 1), :]
        rank = lax.broadcasted_iota(jnp.int32, (REGIONS, SEQ), 0)
        return jnp.where(rank == ids, 1.0, 0.0).astype(LOW)

    def same_document(self, micro):
        ids = jnp.broadcast_to(self.args["doc_ids"][pl.ds(micro, 1), :].astype(WIDE), (SEQ, SEQ))
        same = jnp.where(ids == jnp.transpose(ids), 1.0, 0.0)
        return jnp.concatenate([same, same], 0) > 0.5

    def down(self, index):
        return self.full[2 + index // 2, index % 2].reshape(WIDTH, WIDTH)

    def hop(self, direction, micro):
        source, target = (self.outs["acts"], self.s["fin"]) if direction == 0 else (self.outs["dins"], self.s["bin"])
        return pltpu.make_async_remote_copy(
            src_ref=source.at[micro], dst_ref=target.at[micro],
            send_sem=self.s["send"].at[direction, micro], recv_sem=self.s["recv"].at[direction, micro],
            device_id={"pipe": lax.rem(self.pipe + 1 + 2 * direction, 4)}, device_id_type=MESH,
        )

    def forward(self, micro):
        s, args = self.s, self.args

        @pl.when(self.pipe == 0)
        def _():
            s["fin"][micro] = args["tokens"][micro]

        @pl.when(self.pipe > 0)
        def _():
            self.hop(0, micro).wait_recv()

        embedded = dot_tn(self.marks(micro), args["table"][...])
        info = s["region_info"]
        summed = (
            s["fin"][micro].astype(WIDE)
            + (embedded - info[0:1]) * info[2:3] + args["bn_bias"][...]
        )
        lowered = summed.astype(LOW)
        s["lowered"][micro] = lowered
        s["normed"][micro] = summed

        @pl.when(self.attention)
        def _():
            self.attention_forward(micro, lowered)

        @pl.when(jnp.logical_not(self.attention))
        def _():
            self.feed_forward(micro, lowered)

        residual = s["normed"][micro]
        centered = residual - row_mean(residual)
        inverse = lax.rsqrt(row_mean(centered * centered) + EPSILON)
        normed = centered * inverse
        s["normed"][micro] = normed
        s["inverse"][micro] = jnp.broadcast_to(inverse, (SEQ, 128))
        self.outs["acts"][micro] = (normed * args["ln_gain"][...] + args["ln_bias"][...]).astype(LOW)

        @pl.when(self.pipe < 3)
        def _():
            self.hop(0, micro).start()

    def attention_forward(self, micro, lowered):
        s = self.s
        for index in range(3):
            s["qkv"][micro, :, cols(index)] = dot(lowered, s["proj"][index]).astype(LOW)
        same = self.same_document(micro)
        for pair in range(PAIRS):
            queries = two_heads(s["qkv"][micro, :, cols(pair, 128)])
            keys = s["qkv"][micro, :, cols(PAIRS + pair, 128)]
            values = two_heads(s["qkv"][micro, :, cols(2 * PAIRS + pair, 128)])
            scores = jnp.where(same, dot_nt(queries, keys) * 0.125, -1e30)
            powers = jnp.exp(scores - jnp.max(scores, -1, keepdims=True))
            probs = powers / jnp.sum(powers, -1, keepdims=True)
            s["probs"][micro, pair] = probs
            s["mixed"][micro, :, cols(pair, 128)] = dot(side_by_side(probs.astype(LOW)), values).astype(LOW)
        s["normed"][micro] = s["normed"][micro] + dot(s["mixed"][micro], s["proj"][3])

    def feed_forward(self, micro, lowered):
        s = self.s
        branch = s["normed"][micro]
        for index in range(CHUNKS):
            hidden = dot(lowered, s["proj"][index])
            cumulative = 0.5 * (1.0 + lax.erf(hidden * (0.5 ** 0.5)))
            density = jnp.exp(hidden * hidden * -0.5) * 0.3989422804014327
            s["act"][micro, :, cols(index)] = (hidden * cumulative).astype(LOW)
            s["slope"][micro, :, cols(index)] = cumulative + hidden * density

        @pl.when(micro == 0)
        def _():
            self.await_down()

        for index in range(CHUNKS):
            branch = branch + dot(s["act"][micro, :, cols(index)], self.down(index))
        s["normed"][micro] = branch

    def backward(self, micro):
        s, args = self.s, self.args

        @pl.when(self.pipe == 3)
        def _():
            s["bin"][micro] = args["out_cot"][micro]

        @pl.when(self.pipe < 3)
        def _():
            self.hop(1, micro).wait_recv()

        gout = s["bin"][micro].astype(WIDE)
        normed = s["normed"][micro]
        stats = self.outs["stats"]
        stats[2:3] = stats[2:3] + jnp.sum(gout * normed, 0, keepdims=True)
        stats[3:4] = stats[3:4] + jnp.sum(gout, 0, keepdims=True)
        dnormed = gout * args["ln_gain"][...]
        dres = s["inverse"][micro][:, 0:1] * (
            dnormed - row_mean(dnormed) - normed * row_mean(dnormed * normed)
        )
        s["normed"][micro] = dres
        s["dbranch"][micro] = dres.astype(LOW)

        @pl.when(self.attention)
        def _():
            self.attention_backward(micro)

        @pl.when((self.pipe == 1) & (micro == 1))
        def _():
            self.send_down(self)

        @pl.when(jnp.logical_not(self.attention))
        def _():
            self.feed_backward(micro)

        dsum = s["normed"][micro]
        high = dsum.astype(LOW)
        self.outs["dins"][micro] = high

        @pl.when(self.pipe > 0)
        def _():
            self.hop(1, micro).start()

        marks = self.marks(micro)
        rest = (dsum - high.astype(WIDE)).astype(LOW)
        region = self.outs["region"]
        added = dot(marks, high) + dot(marks, rest)
        region[0, 0] = region[0, 0] + added.reshape(4, 4, 8, WIDTH)

    def attention_backward(self, micro):
        s = self.s
        dmixed = dot_nt(s["dbranch"][micro], s["proj"][3]).astype(LOW)
        for pair in range(PAIRS):
            pieces = [s["qkv"][micro, :, cols(part * PAIRS + pair, 128)] for part in range(3)]
            queries, keys = two_heads(pieces[0]), two_heads(pieces[1])
            grads = two_heads(dmixed[:, cols(pair, 128)])
            probs = s["probs"][micro, pair]
            dprobs = dot_nt(grads, pieces[2])
            dscores = (probs * (dprobs - jnp.sum(dprobs * probs, -1, keepdims=True))).astype(LOW)
            dqueries = dot(side_by_side(dscores), keys) * 0.125
            dkeys = dot_tn(dscores, queries) * 0.125
            dvalues = dot_tn(probs.astype(LOW), grads)
            for part, value in enumerate((dqueries, dkeys, dvalues)):
                s["dwide"][micro, :, cols(part * PAIRS + pair, 128)] = value.astype(LOW)
        total = s["normed"][micro]
        for index in range(3):
            total = total + dot_nt(s["dwide"][micro, :, cols(index)], s["proj"][index])
        s["normed"][micro] = total

    def feed_backward(self, micro):
        s = self.s
        total = s["normed"][micro]
        dbranch = s["dbranch"][micro]
        for index in range(CHUNKS):
            dact = dot_nt(dbranch, self.down(index))
            dhidden = (dact * s["slope"][micro, :, cols(index)]).astype(LOW)
            s["dwide"][micro, :, cols(index)] = dhidden
            total = total + dot_nt(dhidden, s["proj"][index])
        s["normed"][micro] = total

    def weight_gradients(self, block):
        s = self.s
        lowered = s["lowered"][...].reshape(2 * SEQ, WIDTH)
        for side in range(2):
            quarter = 2 * side + block
            if quarter == 3:
                @pl.when(self.attention)
                def _():
                    left = s["mixed"][...].reshape(2 * SEQ, WIDTH)
                    s["dweight"][1] = dot_tn(left, s["dbranch"][...].reshape(2 * SEQ, WIDTH))

                @pl.when(jnp.logical_not(self.attention))
                def _():
                    right = s["dwide"][:, :, cols(3)].reshape(2 * SEQ, WIDTH)
                    s["dweight"][1] = dot_tn(lowered, right)
            else:
                right = s["dwide"][:, :, cols(quarter)].reshape(2 * SEQ, WIDTH)
                s["dweight"][side] = dot_tn(lowered, right)

        def run(index, _):
            half, depth = lax.div(index, 4), lax.rem(index, 4)
            rows = pl.ds(pl.multiple_of(index * 96, 96), 96)
            sides = [s["dweight"][side, rows].reshape(12, 1, 8, WIDTH) for side in range(2)]
            value = jnp.concatenate(sides, 1).reshape(4, ROWS, WIDTH)
            self.grads[block, half, depth] = value.astype(LOW)
            return 0

        lax.fori_loop(0, 8, run, 0)

    def down_gradients(self, block):
        s = self.s
        dbranch = s["dbranch"][...].reshape(2 * SEQ, WIDTH)
        for half in range(2):
            act = s["act"][:, :, cols(2 * (block - 2) + half)].reshape(2 * SEQ, WIDTH)
            self.grads[block, half] = dot_tn(act, dbranch).astype(LOW).reshape(4, 4, ROWS, WIDTH)

    def table_gradient(self, table_sum, stats):
        s = self.s
        group = lax.axis_index("dp")
        rows = pl.ds(pl.multiple_of(lax.rem(group, 16) * 8, 8), 8)
        counts = jnp.concatenate([s["column"][rows]] * (WIDTH // 128), 1)
        mean = stats[0:1] / TOKENS + s["normed_rows"][rows] * (stats[1:2] / TOKENS)
        grad = s["region_info"][2:3] * (table_sum - counts * mean)
        return jnp.where(group < 16, grad, 0.0)

    def start_stats(self):
        self.outs["stats"][...] = jnp.zeros((8, WIDTH), WIDE)
        self.outs["region"][...] = jnp.zeros((1, 1, 4, 4, 8, WIDTH), WIDE)

    def end_stats(self):
        region, stats = self.outs["region"][0, 0].reshape(REGIONS, WIDTH), self.outs["stats"]
        stats[0:1] = jnp.sum(region, 0, keepdims=True)
        stats[1:2] = jnp.sum(region * self.s["normed_rows"][...], 0, keepdims=True)

    def each(self, action):
        lax.fori_loop(0, 2, lambda micro, _: (action(micro), 0)[1], 0)

    def finish(self):
        def run(micro):
            @pl.when(self.pipe < 3)
            def _():
                self.hop(0, micro).wait_send()

            @pl.when(self.pipe > 0)
            def _():
                self.hop(1, micro).wait_send()

        self.each(run)


ARGS = ("tokens", "doc_ids", "region_ids", "ln_gain", "ln_bias", "bn_gain", "bn_bias", "table", "out_cot")
def pack_proj(proj_ref, gather):
    for block in range(2):
        parts = []
        for turn in range(3):
            rows = slice(8 * turn, 8 * turn + 8)
            for side in range(2):
                parts.append(proj_ref[0, rows, cols(2 * side + block)].astype(WIDE))
        gather.own(block)[...] = jnp.concatenate(parts, 0).astype(LOW)


def own_counts(region_ids_ref):
    rank = lax.broadcasted_iota(jnp.int32, (REGIONS, SEQ), 0)
    total = jnp.zeros((8, REGIONS), WIDE)
    for micro in range(2):
        marks = jnp.where(rank == region_ids_ref[micro : micro + 1, :], 1.0, 0.0).astype(LOW)
        total = total + dot_nt(jnp.ones((8, SEQ), LOW), marks)
    return total


FAR = ("tokens", "table", "out_cot")


def whole_kernel(*refs):
    refs = list(refs)

    def take(count):
        taken = refs[:count]
        del refs[:count]
        return taken

    given = dict(zip(ARGS, take(len(ARGS))))
    proj_in, down_in = take(2)
    acts, dins, proj_out, down_out, table_out, shares_out = take(6)
    local_sem, cross_send, cross_recv = take(3)
    s = dict(zip(chain_scratch(), take(len(chain_scratch()))))
    near = dict(zip(FAR, take(len(FAR))))
    full = take(1)[0]
    gather = Gather(full, take(4), take(4))
    counted = Total(*take(5))
    held, region_held, stats = take(3)
    main = Scatter(held, take(4), take(4), take(4))
    region = Scatter(region_held, take(4), take(4), take(4), single=True)
    total = Total(*take(5))

    pipe = gather.pipe
    ffn = lax.rem(pipe, 2) == 1
    pairs = lax.rem(pipe, 2) + 1
    sibling = pipe + 1 - 2 * lax.rem(pipe, 2)
    fetches = [
        pltpu.make_async_copy(
            given[name].at[:REGIONS] if name == "table" else given[name], near[name], local_sem.at[index]
        )
        for index, name in enumerate(FAR)
    ]
    for fetch in fetches:
        fetch.start()
    pack_proj(proj_in, gather)
    gather.own(3)[...] = down_in[0]
    greet(all_dp_devices() + [{"pipe": lax.rem(pipe + 1, 4)}, {"pipe": lax.rem(pipe + 3, 4)}])
    for route in range(2):
        gather.start(route, route)
    cross = pltpu.make_async_remote_copy(
        src_ref=gather.own(3), dst_ref=gather.own(2), send_sem=cross_send.at[0], recv_sem=cross_recv.at[0],
        device_id={"pipe": sibling}, device_id_type=MESH,
    )

    @pl.when(jnp.logical_not(ffn))
    def _():
        cross.start()

    @pl.when(ffn)
    def _():
        gather.start(1, 3)
        cross.wait_recv()
        gather.start(0, 2)

    counted.send(0, own_counts(given["region_ids"]))

    def each(action):
        def run(pair, _):
            for route in range(2):
                action(route, 2 * pair + route)
            return 0

        lax.fori_loop(0, pairs, run, 0)

    for index, step in enumerate(gather.steps()):
        each(step)
        if index < 2:
            counted.send(index + 1, counted.receive(index))
    for route in range(2):
        gather.last(route, route)
    for fetch in fetches:
        fetch.wait()
    unpack_proj(full, s["proj"])
    args = dict(given, **near)
    outs = dict(acts=acts, dins=dins, stats=stats, region=region_held)

    def await_down():
        for route in range(2):
            gather.last(route, 2 + route)

    def send_down(chain):
        for route in range(2):
            chain.down_gradients(2 + route)
            main.start(route, 2 + route)

    chain = Chain(args, full, counted.receive(2), outs, held, s, await_down, send_down)
    chain.start_stats()
    chain.each(chain.forward)
    chain.each(chain.backward)
    chain.end_stats()
    total.send(0, stats[...])
    for block in range(2):
        chain.weight_gradients(block)
        main.start(block, block)

    def regions(action):
        for route in range(2):
            pl.when(lax.rem(pipe, 2) == route)(lambda route=route: action(route, 0))

    regions(region.start)

    @pl.when(pipe == 3)
    def _():
        send_down(chain)

    for index, (step, region_step) in enumerate(zip(main.steps(), region.steps())):
        each(step)
        regions(region_step)
        if index in (1, 2):
            total.send(index, total.receive(index - 1))
    back = pltpu.make_async_remote_copy(
        src_ref=main.own(2), dst_ref=down_out, send_sem=cross_send.at[1], recv_sem=cross_recv.at[1],
        device_id={"pipe": sibling}, device_id_type=MESH,
    )

    @pl.when(ffn)
    def _():
        back.start()
        down_out[...] = main.own(3)[...]

    for block in range(2):
        proj_out[block] = main.own(block)[...]
    summed = total.receive(2)
    table_out[...] = chain.table_gradient(region_held[0, 0, main.depth, main.column], summed)
    shift = lax.rem(WIDTH - 24 * gather.group, WIDTH)
    shares_out[...] = pltpu.roll(summed, shift, 1)[:, :128]
    each(gather.finish)
    each(main.finish)
    regions(region.finish)
    counted.finish()
    total.finish()
    chain.finish()

    @pl.when(ffn)
    def _():
        back.wait_send()

    @pl.when(jnp.logical_not(ffn))
    def _():
        cross.wait_send()
        back.wait_recv()


def run_whole(args, proj, down):
    micro = (2, SEQ, WIDTH)
    vmem, far = pl.BlockSpec(memory_space=pltpu.VMEM), pl.BlockSpec(memory_space=pl.ANY)
    out_shape = [
        jax.ShapeDtypeStruct(micro, LOW),
        jax.ShapeDtypeStruct(micro, LOW),
        jax.ShapeDtypeStruct((2, ROWS, WIDTH), LOW),
        jax.ShapeDtypeStruct((ROWS, WIDTH), LOW),
        jax.ShapeDtypeStruct((8, WIDTH), WIDE),
        jax.ShapeDtypeStruct((8, 128), WIDE),
    ]
    blocks = (BLOCKS, 2, 4, 4, ROWS, WIDTH)
    scratch = [DMA((len(FAR),)), DMA((2,)), DMA((2,))]
    scratch += list(chain_scratch().values())
    scratch += [
        pltpu.VMEM((REGIONS, WIDTH) if name == "table" else args[name].shape, LOW) for name in FAR
    ]
    scratch += [pltpu.VMEM(blocks, LOW)] + gather_sems() + gather_sems()
    scratch += total_scratch((8, REGIONS))
    scratch += [pltpu.VMEM(blocks, LOW), pltpu.VMEM((1, 1, 4, 4, 8, WIDTH), WIDE), pltpu.VMEM((8, WIDTH), WIDE)]
    scratch += scatter_buffers(BLOCKS, ROWS, LOW) + scatter_sems(BLOCKS) + scatter_sems(BLOCKS)
    scratch += scatter_buffers(1, 8, WIDE) + scatter_sems(1) + scatter_sems(1)
    scratch += total_scratch((8, WIDTH))
    return pl.pallas_call(
        whole_kernel,
        out_shape=out_shape,
        in_specs=[far if name in FAR else vmem for name in ARGS] + [vmem] * 2,
        out_specs=[vmem] * len(out_shape),
        scratch_shapes=scratch,
        compiler_params=pltpu.CompilerParams(
            collective_id=0, has_side_effects=True, vmem_limit_bytes=62 * 2**20
        ),
    )(*[args[name] for name in ARGS], proj, down)


def finish_kernel(acts, dins, proj, down, table, shares, *outs):
    outs[0][...] = acts[...].reshape(1, 2 * SEQ, WIDTH)
    outs[1][...] = dins[...].reshape(1, 2 * SEQ, WIDTH)
    for block in range(2):
        rows = proj[block].astype(WIDE)
        for turn in range(3):
            for side in range(2):
                start = 16 * turn + 8 * side
                outs[2][0, 8 * turn : 8 * turn + 8, cols(2 * side + block)] = rows[start : start + 8]
    outs[3][0] = down[...].astype(WIDE)
    for out, row in zip(outs[4:8], (2, 3, 1, 0)):
        out[...] = shares[row : row + 1, :24]
    outs[8][0] = table[...]


def finish(*arrays):
    vmem = pl.BlockSpec(memory_space=pltpu.VMEM)
    share = jax.ShapeDtypeStruct((1, 24), WIDE)
    out_shape = [
        jax.ShapeDtypeStruct((1, 2 * SEQ, WIDTH), LOW),
        jax.ShapeDtypeStruct((1, 2 * SEQ, WIDTH), LOW),
        jax.ShapeDtypeStruct((1, 24, FF), WIDE),
        jax.ShapeDtypeStruct((1, ROWS, WIDTH), WIDE),
        share, share, share, share,
        jax.ShapeDtypeStruct((1, 8, WIDTH), WIDE),
    ]
    return pl.pallas_call(
        finish_kernel, out_shape=out_shape, in_specs=[vmem] * 6, out_specs=[vmem] * 9,
        compiler_params=pltpu.CompilerParams(vmem_limit_bytes=62 * 2**20),
    )(*arrays)


def body(
    tokens, doc_ids, region_ids, proj, down, ln_gain, ln_bias, bn_gain, bn_bias, region_table, out_cot
):
    args = dict(
        tokens=tokens.reshape(2, SEQ, WIDTH), doc_ids=doc_ids, region_ids=region_ids, ln_gain=ln_gain,
        ln_bias=ln_bias, bn_gain=bn_gain, bn_bias=bn_bias, table=region_table[0],
        out_cot=out_cot.reshape(2, SEQ, WIDTH),
    )
    return tuple(finish(*run_whole(args, proj, down)))


def solution(mesh):
    in_specs = (
        P("dp", None),
        P("dp", None),
        P("dp", None),
        P("pipe", "dp", None),
        P("pipe", "dp", None),
        P("pipe", None),
        P("pipe", None),
        P("pipe", None),
        P("pipe", None),
        P("pipe", None, None),
        P("dp", None),
    )
    out_specs = (
        P("pipe", "dp", None),
        P("pipe", "dp", None),
        P("pipe", "dp", None),
        P("pipe", "dp", None),
        P("pipe", "dp"),
        P("pipe", "dp"),
        P("pipe", "dp"),
        P("pipe", "dp"),
        P("pipe", "dp", None),
    )
    return jax.shard_map(body, mesh=mesh, in_specs=in_specs, out_specs=out_specs, check_vma=False)
```

```python
from functools import partial

import jax
import jax.numpy as jnp
from jax import lax
from jax.experimental import pallas as pl
from jax.experimental.pallas import tpu as pltpu
from jax.sharding import PartitionSpec as P

HEADS = 12
FF = 3072
EPSILON = 1e-05
LOW = jnp.bfloat16
WIDE = jnp.float32
MESH = pl.DeviceIdType.MESH
DMA = pltpu.SemaphoreType.DMA
BLOCKS = 4
ROWS = 48
WIDTH = 768


def place():
    group = lax.axis_index("dp")
    pipe = lax.axis_index("pipe")
    half = lax.div(group, 16)
    rest = lax.rem(group, 16)
    return group, pipe, half, lax.div(rest, 4), lax.rem(rest, 4)


def around(position, distance):
    return lax.rem(position + distance + 4, 4)


def group_of(half, depth, column):
    return half * 16 + depth * 4 + column


def along(route, first, second):
    return (second, first) if route == 0 else (first, second)


def to_group(src, dst, send, recv, group):
    return pltpu.make_async_remote_copy(
        src_ref=src,
        dst_ref=dst,
        send_sem=send,
        recv_sem=recv,
        device_id={"dp": group},
        device_id_type=MESH,
    )


def arrived(dst, recv):
    pltpu.make_async_copy(dst, dst, recv).wait()


def narrow(ref, route, block, half, first, second):
    depth, column = along(route, first, second)
    return ref.at[block, half, depth, column]


def wide(ref, route, block, half, second):
    if route == 0:
        return ref.at[block, half, second]
    return ref.at[block, half, :, second]


def greet(others):
    barrier = pltpu.get_barrier_semaphore()
    for device in others:
        pl.semaphore_signal(barrier, inc=1, device_id=device, device_id_type=MESH)


def meet(others):
    pl.semaphore_wait(pltpu.get_barrier_semaphore(), len(others))


def ring_devices():
    group, pipe, half, depth, column = place()
    return [
        {"dp": group_of(1 - half, depth, column)},
        {"dp": group_of(half, around(depth, 1), column)},
        {"dp": group_of(half, around(depth, -1), column)},
        {"dp": group_of(half, depth, around(column, 1))},
        {"dp": group_of(half, depth, around(column, -1))},
    ]


def gather_sems():
    return [DMA((BLOCKS,)), DMA((BLOCKS, 3)), DMA((BLOCKS, 2, 2)), DMA((BLOCKS, 2, 2))]


def part(ref, way):
    return ref.at[pl.ds(2 * way, 2)]


class Rings:
    def __init__(self, ref, sends, recvs):
        self.ref, self.sends, self.recvs = ref, sends, recvs
        self.group, self.pipe, self.half, self.depth, self.column = place()
        self.partner = group_of(1 - self.half, self.depth, self.column)

    def axes(self, route):
        return (self.column, self.depth) if route == 0 else (self.depth, self.column)

    def small_peer(self, route, distance):
        if route == 0:
            return group_of(self.half, self.depth, around(self.column, distance))
        return group_of(self.half, around(self.depth, distance), self.column)

    def large_peer(self, route, distance):
        return self.small_peer(1 - route, distance)

    def own(self, block):
        return self.ref.at[block, self.half, self.depth, self.column]

    def send(self, kind, index, src, dst, group):
        return to_group(src, dst, self.sends[kind].at[index], self.recvs[kind].at[index], group)


class Gather(Rings):
    def swap(self, route, block, half, position=None):
        second = self.axes(route)[1]
        slot = wide(self.ref, route, block, half, second)
        if position is not None:
            slot = narrow(self.ref, route, block, half, position, second)
        return self.send(0, (block,), slot, slot, self.partner)

    def small(self, route, block, distance):
        slot = self.own(block)
        return self.send(1, (block, distance - 1), slot, slot, self.small_peer(route, distance))

    def large(self, route, block, half, way, position=None):
        second = self.axes(route)[1]
        slot = wide(self.ref, route, block, half, second)
        if position is not None:
            slot = narrow(self.ref, route, block, half, position, second)
        return self.send(2, (block, half, way), slot, slot, self.large_peer(route, 1 - 2 * way))

    def large_relay(self, route, block, half, way):
        second = self.axes(route)[1]
        distance = 1 - 2 * way
        slot = part(wide(self.ref, route, block, half, around(second, -distance)), way)
        return self.send(3, (block, half, way), slot, slot, self.large_peer(route, distance))

    def pass_on(self, route, block, position):
        for way in range(2):
            self.large(route, block, self.half, way, position).start()
        self.swap(route, block, self.half, position).start()

    def start(self, route, block):
        for distance in range(1, 4):
            self.small(route, block, distance).start()
        self.pass_on(route, block, self.axes(route)[0])

    def end_small(self, route, block):
        for distance in (1, 3, 2):
            self.small(route, block, distance).wait_recv()
            self.pass_on(route, block, around(self.axes(route)[0], -distance))

    def relay_large(self, route, block, half):
        for way in range(2):
            self.large(route, block, half, way).wait_recv()
            self.large_relay(route, block, half, way).start()

    def swap_in(self, route, block):
        self.swap(route, block, 1 - self.half).wait_recv()
        for way in range(2):
            self.large(route, block, 1 - self.half, way).start()

    def last(self, route, block):
        for half in range(2):
            for way in range(2):
                self.large_relay(route, block, half, way).wait_recv()

    def steps(self):
        return [
            self.end_small,
            lambda route, block: self.relay_large(route, block, self.half),
            self.swap_in,
            lambda route, block: self.relay_large(route, block, 1 - self.half),
        ]

    def finish(self, route, block):
        self.swap(route, block, self.half).wait_send()
        for distance in range(1, 4):
            self.small(route, block, distance).wait_send()
        for half in range(2):
            for way in range(2):
                self.large(route, block, half, way).wait_send()
                self.large_relay(route, block, half, way).wait_send()


def scatter_buffers(blocks, rows, dtype):
    return [
        pltpu.VMEM((blocks, 2, 4, rows, WIDTH), dtype),
        pltpu.VMEM((blocks, 2, 2, 4, rows, WIDTH), dtype),
        pltpu.VMEM((blocks, 4, rows, WIDTH), dtype),
        pltpu.VMEM((blocks, 3, rows, WIDTH), dtype),
    ]


def scatter_sems(blocks):
    return [DMA((blocks, 2, 2)), DMA((blocks, 2, 2)), DMA((blocks,)), DMA((blocks, 3))]


def accumulate(target, others):
    total = target[...].astype(WIDE)
    for other in others:
        total = total + other[...].astype(WIDE)
    target[...] = total.astype(target.dtype)


class Scatter(Rings):
    def __init__(self, ref, buffers, sends, recvs, single=False):
        super().__init__(ref, sends, recvs)
        self.buffers, self.single = buffers, single

    def large_early(self, route, block, half, way):
        second = self.axes(route)[1]
        return self.send(
            0, (block, half, way), part(wide(self.ref, route, block, half, around(second, 2)), way),
            part(self.buffers[0].at[block, half], way), self.large_peer(route, 1 - 2 * way),
        )

    def large(self, route, block, half, way, side=None):
        second = self.axes(route)[1]
        distance = 1 - 2 * way
        src = wide(self.ref, route, block, half, around(second, distance))
        dst = self.buffers[1].at[block, way, half]
        if side is not None:
            src, dst = part(src, side), part(dst, side)
        return self.send(1, (block, way, half), src, dst, self.large_peer(route, distance))

    def swap(self, route, block, half):
        second = self.axes(route)[1]
        return self.send(
            2, (block,), wide(self.ref, route, block, half, second), self.buffers[2].at[block], self.partner
        )

    def target(self, route, block, distance):
        first, second = self.axes(route)
        half = 0 if self.single else self.half
        return narrow(self.ref, route, block, half, around(first, distance), second)

    def small(self, route, block, distance):
        return self.send(
            3, (block, distance - 1), self.target(route, block, distance), self.buffers[3].at[block, distance - 1],
            self.small_peer(route, distance),
        )

    def where(self, half, action):
        if self.single:
            pl.when(half == 0)(lambda: action(0))
        else:
            action(half)

    def begin(self, route, block, half):
        def run(half):
            for way in range(2):
                self.large_early(route, block, half, way).start()
                self.large(route, block, half, way, 1 - way).start()

        self.where(half, run)

    def middle(self, route, block, half):
        def run(half):
            second = self.axes(route)[1]
            for way in range(2):
                self.large_early(route, block, half, way).wait_recv()
                accumulate(
                    part(wide(self.ref, route, block, half, around(second, 1 - 2 * way)), way),
                    [part(self.buffers[0].at[block, half], way)],
                )
                self.large(route, block, half, way, way).start()

        self.where(half, run)

    def sum_large(self, route, block, half, others):
        for way in range(2):
            self.large(route, block, half, way).wait_recv()
        arrivals = [self.buffers[1].at[block, way, half] for way in range(2)]
        accumulate(wide(self.ref, route, block, half, self.axes(route)[1]), arrivals + others)

    def start(self, route, block):
        self.begin(route, block, 1 - self.half)

    def turn(self, route, block):
        self.middle(route, block, 1 - self.half)
        self.begin(route, block, self.half)

    def sum_other(self, route, block):
        def run(half):
            self.sum_large(route, block, half, [])
            self.swap(route, block, half).start()

        self.where(1 - self.half, run)

    def sum_own(self, route, block):
        def run(half):
            self.swap(route, block, half).wait_recv()
            self.sum_large(route, block, half, [self.buffers[2].at[block]])
            for distance in range(1, 4):
                self.small(route, block, distance).start()

        self.where(self.half, run)

    def last(self, route, block):
        def run(half):
            for distance in range(1, 4):
                self.small(route, block, distance).wait_recv()
            arrivals = [self.buffers[3].at[block, index] for index in range(3)]
            accumulate(self.target(route, block, 0), arrivals)

        self.where(self.half, run)

    def steps(self):
        return [
            self.turn,
            self.sum_other,
            lambda route, block: self.middle(route, block, self.half),
            self.sum_own,
            self.last,
        ]

    def finish(self, route, block):
        def large(half):
            for way in range(2):
                self.large_early(route, block, half, way).wait_send()
                self.large(route, block, half, way).wait_send()

        def other(half):
            large(half)
            self.swap(route, block, half).wait_send()

        def own(half):
            large(half)
            for distance in range(1, 4):
                self.small(route, block, distance).wait_send()

        self.where(1 - self.half, other)
        self.where(self.half, own)


class Total:
    def __init__(self, first, second, third, sends, recvs):
        self.stages, self.sends, self.recvs = (first, second, third), sends, recvs
        self.group, self.pipe, self.half, self.depth, self.column = place()
        self.where = (self.column, self.depth, self.half)

    def copy(self, stage, distance):
        here, buffer = self.where[stage], self.stages[stage]
        if stage == 0:
            peer = group_of(self.half, self.depth, around(here, distance))
        elif stage == 1:
            peer = group_of(self.half, around(here, distance), self.column)
        else:
            peer = group_of(1 - here, self.depth, self.column)
        return to_group(
            buffer.at[here], buffer.at[here],
            self.sends.at[stage, distance - 1], self.recvs.at[stage, distance - 1], peer,
        )

    def distances(self, stage):
        return range(1, 4) if stage < 2 else range(1, 2)

    def send(self, stage, value):
        self.stages[stage][self.where[stage]] = value
        for distance in self.distances(stage):
            self.copy(stage, distance).start()

    def receive(self, stage):
        for distance in self.distances(stage):
            self.copy(stage, distance).wait_recv()
        total = self.stages[stage][0]
        for index in range(1, 4 if stage < 2 else 2):
            total = total + self.stages[stage][index]
        return total

    def finish(self):
        for stage in range(3):
            for distance in self.distances(stage):
                self.copy(stage, distance).wait_send()


def total_scratch(shape):
    return [
        pltpu.VMEM((4,) + shape, WIDE),
        pltpu.VMEM((4,) + shape, WIDE),
        pltpu.VMEM((2,) + shape, WIDE),
        DMA((3, 3)),
        DMA((3, 3)),
    ]


def all_dp_devices():
    group, pipe, half, depth, column = place()
    return ring_devices() + [
        {"dp": group_of(half, around(depth, 2), column)},
        {"dp": group_of(half, depth, around(column, 2))},
    ]


PAIRS = HEADS // 2
SEQ = 128
REGIONS = 128
TOKENS = 8192
CHUNKS = 4


def dot(left, right):
    return lax.dot_general(left, right, (((1,), (0,)), ((), ())), preferred_element_type=WIDE)


def dot_nt(left, right):
    return lax.dot_general(left, right, (((1,), (1,)), ((), ())), preferred_element_type=WIDE)


def dot_tn(left, right):
    return lax.dot_general(left, right, (((0,), (0,)), ((), ())), preferred_element_type=WIDE)


def cols(index, width=WIDTH):
    return slice(index * width, (index + 1) * width)


def two_heads(pair):
    lane = lax.broadcasted_iota(jnp.int32, pair.shape, 1)
    zero = jnp.zeros_like(pair)
    return jnp.concatenate([jnp.where(lane < 64, pair, zero), jnp.where(lane < 64, zero, pair)], 0)


def side_by_side(stacked):
    return jnp.concatenate([stacked[:SEQ], stacked[SEQ:]], 1)


def row_mean(value):
    return jnp.mean(value, -1, keepdims=True)


def chain_scratch():
    return dict(
        proj=pltpu.VMEM((CHUNKS, WIDTH, WIDTH), LOW),
        fin=pltpu.VMEM((2, SEQ, WIDTH), LOW),
        bin=pltpu.VMEM((2, SEQ, WIDTH), LOW),
        lowered=pltpu.VMEM((2, SEQ, WIDTH), LOW),
        acts=pltpu.VMEM((2, SEQ, WIDTH), LOW),
        dins=pltpu.VMEM((2, SEQ, WIDTH), LOW),
        extra=pltpu.VMEM((2, SEQ, WIDTH), WIDE),
        resid=pltpu.VMEM((2, SEQ, WIDTH), WIDE),
        normed=pltpu.VMEM((2, SEQ, WIDTH), WIDE),
        inverse=pltpu.VMEM((2, SEQ, 128), WIDE),
        normed_rows=pltpu.VMEM((REGIONS, WIDTH), WIDE),
        region_info=pltpu.VMEM((8, WIDTH), WIDE),
        column=pltpu.VMEM((REGIONS, 128), WIDE),
        qkv=pltpu.VMEM((2, SEQ, 3 * WIDTH), LOW),
        probs=pltpu.VMEM((2, PAIRS, 2 * SEQ, SEQ), WIDE),
        mixed=pltpu.VMEM((2, SEQ, WIDTH), LOW),
        dbranch=pltpu.VMEM((2, SEQ, WIDTH), LOW),
        dwide=pltpu.VMEM((2, SEQ, FF), LOW),
        act=pltpu.VMEM((2, SEQ, FF), LOW),
        slope=pltpu.VMEM((2, SEQ, FF), WIDE),
        dweight=pltpu.VMEM((2, WIDTH, WIDTH), WIDE),
        send=DMA((2, 2)),
        recv=DMA((2, 2)),
    )


def unpack_proj(full_ref, proj_ref):
    def run(index, _):
        half, depth = lax.div(index, 4), lax.rem(index, 4)
        rows = pl.ds(pl.multiple_of(index * 96, 96), 96)
        for block in range(2):
            value = full_ref[block, half, depth].astype(WIDE).reshape(12, 2, 8, WIDTH)
            for side in range(2):
                proj_ref[2 * side + block, rows] = value[:, side].reshape(96, WIDTH).astype(LOW)
        return 0

    lax.fori_loop(0, 8, run, 0)


class Chain:
    def __init__(self, args, full_ref, counts, outs, grads, s, await_down, send_down, send_proj):
        self.await_down, self.send_down, self.send_proj = await_down, send_down, send_proj
        self.args, self.full, self.outs, self.grads, self.s = args, full_ref, outs, grads, s
        self.pipe = lax.axis_index("pipe")
        self.attention = lax.rem(self.pipe, 2) == 0
        self.region_statistics(counts)
        self.each(self.region_terms)

    def region_statistics(self, counts):
        table_ref, s = self.args["table"], self.s
        column = jnp.transpose(jnp.broadcast_to(counts[0:1], (SEQ, REGIONS)))
        s["column"][...] = column
        for index in range(WIDTH // 128):
            lanes = cols(index, 128)
            table = table_ref[:, lanes].astype(WIDE)
            mean = jnp.sum(table * column, 0, keepdims=True) / TOKENS
            second = jnp.sum(table * table * column, 0, keepdims=True) / TOKENS
            inverse = lax.rsqrt(second - mean * mean + EPSILON)
            s["normed_rows"][:, lanes] = (table - mean) * inverse
            s["region_info"][0:1, lanes] = mean
            s["region_info"][1:2, lanes] = inverse
            s["region_info"][2:3, lanes] = inverse * self.args["bn_gain"][0:1, lanes]

    def region_terms(self, micro):
        embedded = dot_tn(self.marks(micro), self.args["table"][...])
        info = self.s["region_info"]
        self.s["extra"][micro] = (embedded - info[0:1]) * info[2:3] + self.args["bn_bias"][...]

    def marks(self, micro):
        ids = self.args["region_ids"][pl.ds(micro, 1), :]
        rank = lax.broadcasted_iota(jnp.int32, (REGIONS, SEQ), 0)
        return jnp.where(rank == ids, 1.0, 0.0).astype(LOW)

    def same_document(self, micro):
        ids = jnp.broadcast_to(self.args["doc_ids"][pl.ds(micro, 1), :].astype(WIDE), (SEQ, SEQ))
        same = jnp.where(ids == jnp.transpose(ids), 1.0, 0.0)
        return jnp.concatenate([same, same], 0) > 0.5

    def down(self, index):
        return self.full[2 + index // 2, index % 2].reshape(WIDTH, WIDTH)

    def turned_proj(self, index):
        return self.full[index // 2, index % 2].reshape(WIDTH, WIDTH)

    def turned_down(self, index):
        return self.grads[index // 2, index % 2].reshape(WIDTH, WIDTH)

    def turn_proj(self):
        for index in range(CHUNKS):
            turned = jnp.transpose(self.s["proj"][index])
            self.full[index // 2, index % 2] = turned.reshape(4, 4, ROWS, WIDTH)

    def turn_down(self):
        for index in range(CHUNKS):
            turned = jnp.transpose(self.down(index))
            self.grads[index // 2, index % 2] = turned.reshape(4, 4, ROWS, WIDTH)

    def hop(self, direction, micro):
        names = ("acts", "fin") if direction == 0 else ("dins", "bin")
        source, target = self.s[names[0]], self.s[names[1]]
        return pltpu.make_async_remote_copy(
            src_ref=source.at[micro], dst_ref=target.at[micro],
            send_sem=self.s["send"].at[direction, micro], recv_sem=self.s["recv"].at[direction, micro],
            device_id={"pipe": lax.rem(self.pipe + 1 + 2 * direction, 4)}, device_id_type=MESH,
        )

    def forward(self, micro):
        s, args = self.s, self.args

        @pl.when(self.pipe == 0)
        def _():
            s["fin"][micro] = args["tokens"][micro]

        @pl.when(self.pipe > 0)
        def _():
            self.hop(0, micro).wait_recv()

        summed = s["fin"][micro].astype(WIDE) + s["extra"][micro]
        lowered = summed.astype(LOW)
        s["lowered"][micro] = lowered
        s["resid"][micro] = summed

        @pl.when(self.attention)
        def _():
            self.attention_forward(micro, lowered)

        @pl.when(jnp.logical_not(self.attention))
        def _():
            self.feed_forward(micro, lowered)

        residual = s["resid"][micro]
        centered = residual - row_mean(residual)
        inverse = lax.rsqrt(row_mean(centered * centered) + EPSILON)
        normed = centered * inverse
        s["normed"][micro] = normed
        s["inverse"][micro] = jnp.broadcast_to(inverse, (SEQ, 128))
        s["acts"][micro] = (normed * args["ln_gain"][...] + args["ln_bias"][...]).astype(LOW)

        @pl.when(self.pipe < 3)
        def _():
            self.hop(0, micro).start()

    def attention_forward(self, micro, lowered):
        s = self.s
        for index in range(3):
            s["qkv"][micro, :, cols(index)] = dot(lowered, s["proj"][index]).astype(LOW)
        same = self.same_document(micro)
        scores, probs, mixed = [], [], []
        for pair in range(PAIRS):
            queries = two_heads(s["qkv"][micro, :, cols(pair, 128)])
            scores.append(dot_nt(queries, s["qkv"][micro, :, cols(PAIRS + pair, 128)]))
        scores = [jnp.where(same, score * 0.125, -1e30) for score in scores]
        tops = [jnp.max(score, -1, keepdims=True) for score in scores]
        powers = [jnp.exp(score - top) for score, top in zip(scores, tops)]
        totals = [jnp.sum(power, -1, keepdims=True) for power in powers]
        for pair in range(PAIRS):
            probs.append(powers[pair] / totals[pair])
            s["probs"][micro, pair] = probs[pair]
        for pair in range(PAIRS):
            values = two_heads(s["qkv"][micro, :, cols(2 * PAIRS + pair, 128)])
            mixed.append(dot(side_by_side(probs[pair].astype(LOW)), values))
        for pair in range(PAIRS):
            s["mixed"][micro, :, cols(pair, 128)] = mixed[pair].astype(LOW)
        s["resid"][micro] = s["resid"][micro] + dot(s["mixed"][micro], s["proj"][3])

    def feed_forward(self, micro, lowered):
        s = self.s
        branch = s["resid"][micro]
        for index in range(CHUNKS):
            hidden = dot(lowered, s["proj"][index])
            cumulative = 0.5 * (1.0 + lax.erf(hidden * (0.5 ** 0.5)))
            density = jnp.exp(hidden * hidden * -0.5) * 0.3989422804014327
            s["act"][micro, :, cols(index)] = (hidden * cumulative).astype(LOW)
            s["slope"][micro, :, cols(index)] = cumulative + hidden * density

        @pl.when((micro == 0) & (self.pipe == 1))
        def _():
            self.await_down()

        for index in range(CHUNKS):
            branch = branch + dot(s["act"][micro, :, cols(index)], self.down(index))
        s["resid"][micro] = branch

    def backward(self, micro):
        s, args = self.s, self.args

        @pl.when(self.pipe == 3)
        def _():
            s["bin"][micro] = args["out_cot"][micro]

        @pl.when(self.pipe < 3)
        def _():
            self.hop(1, micro).wait_recv()

        gout = s["bin"][micro].astype(WIDE)
        normed = s["normed"][micro]
        dnormed = gout * args["ln_gain"][...]
        dres = s["inverse"][micro][:, 0:1] * (
            dnormed - row_mean(dnormed) - normed * row_mean(dnormed * normed)
        )
        s["resid"][micro] = dres
        s["dbranch"][micro] = dres.astype(LOW)

        @pl.when(self.attention)
        def _():
            self.attention_backward(micro)

        @pl.when((self.pipe == 0) & (micro == 1))
        def _():
            self.send_proj(self)

        @pl.when(self.attention)
        def _():
            total = s["resid"][micro]
            for index in range(3):
                total = total + dot(s["dwide"][micro, :, cols(index)], self.turned_proj(index))
            self.input_gradient(micro, total)

        @pl.when((self.pipe == 1) & (micro == 1))
        def _():
            self.send_down(self)

        @pl.when(jnp.logical_not(self.attention))
        def _():
            self.input_gradient(micro, self.feed_backward(micro))

        @pl.when(self.pipe > 0)
        def _():
            self.hop(1, micro).start()

        stats = self.outs["stats"]
        gout = s["bin"][micro].astype(WIDE)
        stats[2:3] = stats[2:3] + jnp.sum(gout * s["normed"][micro], 0, keepdims=True)
        stats[3:4] = stats[3:4] + jnp.sum(gout, 0, keepdims=True)
        marks = self.marks(micro)
        dsum = s["resid"][micro]
        high = s["dins"][micro]
        rest = (dsum - high.astype(WIDE)).astype(LOW)
        region = self.outs["region"]
        added = dot(marks, high) + dot(marks, rest)
        region[0, 0] = region[0, 0] + added.reshape(4, 4, 8, WIDTH)

    def input_gradient(self, micro, dsum):
        self.s["resid"][micro] = dsum
        self.s["dins"][micro] = dsum.astype(LOW)

    def attention_backward(self, micro):
        s, pairs = self.s, range(PAIRS)
        dmixed = dot(s["dbranch"][micro], self.turned_proj(3)).astype(LOW)
        pieces = [[s["qkv"][micro, :, cols(part * PAIRS + pair, 128)] for part in range(3)] for pair in pairs]
        grads = [two_heads(dmixed[:, cols(pair, 128)]) for pair in pairs]
        dprobs = [dot_nt(grads[pair], pieces[pair][2]) for pair in pairs]
        probs = [s["probs"][micro, pair] for pair in pairs]
        dvalues = [dot_tn(probs[pair].astype(LOW), grads[pair]) for pair in pairs]
        sums = [jnp.sum(dprobs[pair] * probs[pair], -1, keepdims=True) for pair in pairs]
        dscores = [(probs[pair] * (dprobs[pair] - sums[pair])).astype(LOW) for pair in pairs]
        dkeys = [dot_tn(dscores[pair], two_heads(pieces[pair][0])) * 0.125 for pair in pairs]
        dqueries = [dot(side_by_side(dscores[pair]), two_heads(pieces[pair][1])) * 0.125 for pair in pairs]
        for pair in pairs:
            for part, value in enumerate((dqueries[pair], dkeys[pair], dvalues[pair])):
                s["dwide"][micro, :, cols(part * PAIRS + pair, 128)] = value.astype(LOW)

    def feed_backward(self, micro):
        s = self.s
        total = s["resid"][micro]
        dbranch = s["dbranch"][micro]
        for index in range(CHUNKS):
            dact = dot(dbranch, self.turned_down(index))
            s["dwide"][micro, :, cols(index)] = (dact * s["slope"][micro, :, cols(index)]).astype(LOW)
        for index in range(CHUNKS):
            total = total + dot(s["dwide"][micro, :, cols(index)], self.turned_proj(index))
        return total

    def weight_gradients(self, block):
        s = self.s
        lowered = s["lowered"][...].reshape(2 * SEQ, WIDTH)
        for side in range(2):
            quarter = 2 * side + block
            if quarter == 3:
                @pl.when(self.attention)
                def _():
                    left = s["mixed"][...].reshape(2 * SEQ, WIDTH)
                    s["dweight"][1] = dot_tn(left, s["dbranch"][...].reshape(2 * SEQ, WIDTH))

                @pl.when(jnp.logical_not(self.attention))
                def _():
                    right = s["dwide"][:, :, cols(3)].reshape(2 * SEQ, WIDTH)
                    s["dweight"][1] = dot_tn(lowered, right)
            else:
                right = s["dwide"][:, :, cols(quarter)].reshape(2 * SEQ, WIDTH)
                s["dweight"][side] = dot_tn(lowered, right)

        def run(index, _):
            half, depth = lax.div(index, 4), lax.rem(index, 4)
            rows = pl.ds(pl.multiple_of(index * 96, 96), 96)
            sides = [s["dweight"][side, rows].reshape(12, 1, 8, WIDTH) for side in range(2)]
            value = jnp.concatenate(sides, 1).reshape(4, ROWS, WIDTH)
            self.grads[block, half, depth] = value.astype(LOW)
            return 0

        lax.fori_loop(0, 8, run, 0)

    def down_gradients(self, block):
        s = self.s
        dbranch = s["dbranch"][...].reshape(2 * SEQ, WIDTH)
        for half in range(2):
            act = s["act"][:, :, cols(2 * (block - 2) + half)].reshape(2 * SEQ, WIDTH)
            self.grads[block, half] = dot_tn(act, dbranch).astype(LOW).reshape(4, 4, ROWS, WIDTH)

    def table_gradient(self, table_sum, stats):
        s = self.s
        group = lax.axis_index("dp")
        rows = pl.ds(pl.multiple_of(lax.rem(group, 16) * 8, 8), 8)
        counts = jnp.concatenate([s["column"][rows]] * (WIDTH // 128), 1)
        mean = stats[0:1] / TOKENS + s["normed_rows"][rows] * (stats[1:2] / TOKENS)
        grad = s["region_info"][2:3] * (table_sum - counts * mean)
        return jnp.where(group < 16, grad, 0.0)

    def start_stats(self):
        self.outs["stats"][...] = jnp.zeros((8, WIDTH), WIDE)
        self.outs["region"][...] = jnp.zeros((1, 1, 4, 4, 8, WIDTH), WIDE)

    def end_stats(self):
        region, stats = self.outs["region"][0, 0].reshape(REGIONS, WIDTH), self.outs["stats"]
        stats[0:1] = jnp.sum(region, 0, keepdims=True)
        stats[1:2] = jnp.sum(region * self.s["normed_rows"][...], 0, keepdims=True)

    def each(self, action):
        lax.fori_loop(0, 2, lambda micro, _: (action(micro), 0)[1], 0)

    def finish(self):
        def run(micro):
            @pl.when(self.pipe < 3)
            def _():
                self.hop(0, micro).wait_send()

            @pl.when(self.pipe > 0)
            def _():
                self.hop(1, micro).wait_send()

        self.each(run)


ARGS = ("tokens", "doc_ids", "region_ids", "ln_gain", "ln_bias", "bn_gain", "bn_bias", "table", "out_cot")
def pack_proj(proj_ref, gather):
    for block in range(2):
        parts = []
        for turn in range(3):
            rows = slice(8 * turn, 8 * turn + 8)
            for side in range(2):
                parts.append(proj_ref[0, rows, cols(2 * side + block)].astype(WIDE))
        gather.own(block)[...] = jnp.concatenate(parts, 0).astype(LOW)


def own_counts(region_ids_ref):
    rank = lax.broadcasted_iota(jnp.int32, (REGIONS, SEQ), 0)
    total = jnp.zeros((8, REGIONS), WIDE)
    for micro in range(2):
        marks = jnp.where(rank == region_ids_ref[micro : micro + 1, :], 1.0, 0.0).astype(LOW)
        total = total + dot_nt(jnp.ones((8, SEQ), LOW), marks)
    return total


FAR = ("region_ids", "proj", "down", "table", "bn_gain", "bn_bias", "doc_ids", "ln_gain", "ln_bias", "tokens", "out_cot")


def whole_kernel(*refs):
    refs = list(refs)

    def take(count):
        taken = refs[:count]
        del refs[:count]
        return taken

    given = dict(zip(ARGS + ("proj", "down"), take(len(ARGS) + 2)))
    acts_out, dins_out, proj_out, down_out, table_out, shares_out = take(6)
    local_sem, cross_send, cross_recv = take(3)
    s = dict(zip(chain_scratch(), take(len(chain_scratch()))))
    near = dict(zip(FAR, take(len(FAR))))
    full = take(1)[0]
    gather = Gather(full, take(4), take(4))
    counted = Total(*take(5))
    held, region_held, stats = take(3)
    main = Scatter(held, take(4), take(4), take(4))
    region = Scatter(region_held, take(4), take(4), take(4), single=True)
    total = Total(*take(5))

    pipe = gather.pipe
    ffn = lax.rem(pipe, 2) == 1
    pairs = lax.rem(pipe, 2) + 1
    sibling = pipe + 1 - 2 * lax.rem(pipe, 2)
    fetches = [
        pltpu.make_async_copy(
            given[name].at[:REGIONS] if name == "table" else given[name], near[name], local_sem.at[index]
        )
        for index, name in enumerate(FAR)
    ]
    for fetch in fetches:
        fetch.start()
    others = all_dp_devices() + [{"pipe": lax.rem(pipe + 1, 4)}, {"pipe": lax.rem(pipe + 3, 4)}]
    greet(others)
    for fetch in fetches[:3]:
        fetch.wait()
    pack_proj(near["proj"], gather)
    gather.own(3)[...] = near["down"][0]
    meet(others)
    for route in range(2):
        gather.start(route, route)
    cross = pltpu.make_async_remote_copy(
        src_ref=gather.own(3), dst_ref=gather.own(2), send_sem=cross_send.at[0], recv_sem=cross_recv.at[0],
        device_id={"pipe": sibling}, device_id_type=MESH,
    )

    @pl.when(jnp.logical_not(ffn))
    def _():
        cross.start()

    @pl.when(ffn)
    def _():
        gather.start(1, 3)
        cross.wait_recv()
        gather.start(0, 2)

    counted.send(0, own_counts(near["region_ids"]))

    def each(action):
        def run(pair, _):
            for route in range(2):
                action(route, 2 * pair + route)
            return 0

        lax.fori_loop(0, pairs, run, 0)

    for index, step in enumerate(gather.steps()):
        each(step)
        if index in (1, 2):
            counted.send(index, counted.receive(index - 1))
    for fetch in fetches[3:]:
        fetch.wait()
    outs = dict(stats=stats, region=region_held)

    def await_down():
        for route in range(2):
            gather.last(route, 2 + route)

    def send_down(chain):
        for route in range(2):
            chain.down_gradients(2 + route)
            main.start(route, 2 + route)

    def send_proj(chain):
        for block in range(2):
            chain.weight_gradients(block)
            main.start(block, block)

    chain = Chain(near, full, counted.receive(2), outs, held, s, await_down, send_down, send_proj)
    chain.start_stats()
    for route in range(2):
        gather.last(route, route)
    unpack_proj(full, s["proj"])

    def turn():
        for route in range(2):
            gather.finish(route, route)
        chain.turn_proj()
        pl.when(pipe == 3)(await_down)
        pl.when(ffn)(chain.turn_down)

    pl.when(pipe >= 2)(turn)
    chain.each(chain.forward)
    pl.when(pipe < 2)(turn)
    put_acts = pltpu.make_async_copy(s["acts"], acts_out, local_sem.at[len(FAR)])
    put_dins = pltpu.make_async_copy(s["dins"], dins_out, local_sem.at[len(FAR) + 1])
    put_acts.start()
    chain.each(chain.backward)
    put_dins.start()
    pl.when(pipe > 0)(lambda: send_proj(chain))
    chain.end_stats()
    total.send(0, stats[...])

    def regions(action):
        for route in range(2):
            pl.when(lax.rem(pipe, 2) == route)(lambda route=route: action(route, 0))

    regions(region.start)

    @pl.when(pipe == 3)
    def _():
        send_down(chain)

    def each_late(action):
        def run(pair, _):
            for route in range(2):
                action(route, 2 * (pairs - 1 - pair) + route)
            return 0

        lax.fori_loop(0, pairs, run, 0)

    for index, (step, region_step) in enumerate(zip(main.steps(), region.steps())):
        each_late(step)
        regions(region_step)
        if index in (1, 2):
            total.send(index, total.receive(index - 1))
    back = pltpu.make_async_remote_copy(
        src_ref=main.own(2), dst_ref=down_out, send_sem=cross_send.at[1], recv_sem=cross_recv.at[1],
        device_id={"pipe": sibling}, device_id_type=MESH,
    )

    @pl.when(ffn)
    def _():
        back.start()
        down_out[...] = main.own(3)[...]

    for block in range(2):
        proj_out[block] = main.own(block)[...]
    summed = total.receive(2)
    table_out[...] = chain.table_gradient(region_held[0, 0, main.depth, main.column], summed)
    shift = lax.rem(WIDTH - 24 * gather.group, WIDTH)
    shares_out[...] = pltpu.roll(summed, shift, 1)[:, :128]

    @pl.when(ffn)
    def _():
        for route in range(2):
            gather.finish(route, 2 + route)

    each(main.finish)
    regions(region.finish)
    counted.finish()
    total.finish()
    chain.finish()
    put_acts.wait()
    put_dins.wait()

    @pl.when(ffn)
    def _():
        back.wait_send()

    @pl.when(jnp.logical_not(ffn))
    def _():
        cross.wait_send()
        back.wait_recv()


def run_whole(args, proj, down):
    micro = (2, SEQ, WIDTH)
    vmem, far = pl.BlockSpec(memory_space=pltpu.VMEM), pl.BlockSpec(memory_space=pl.ANY)
    out_shape = [
        jax.ShapeDtypeStruct(micro, LOW),
        jax.ShapeDtypeStruct(micro, LOW),
        jax.ShapeDtypeStruct((2, ROWS, WIDTH), LOW),
        jax.ShapeDtypeStruct((ROWS, WIDTH), LOW),
        jax.ShapeDtypeStruct((8, WIDTH), WIDE),
        jax.ShapeDtypeStruct((8, 128), WIDE),
    ]
    blocks = (BLOCKS, 2, 4, 4, ROWS, WIDTH)
    given = dict(args, proj=proj, down=down)
    scratch = [DMA((len(FAR) + 2,)), DMA((2,)), DMA((2,))]
    scratch += list(chain_scratch().values())
    scratch += [
        pltpu.VMEM((REGIONS, WIDTH) if name == "table" else given[name].shape, given[name].dtype)
        for name in FAR
    ]
    scratch += [pltpu.VMEM(blocks, LOW)] + gather_sems() + gather_sems()
    scratch += total_scratch((8, REGIONS))
    scratch += [pltpu.VMEM(blocks, LOW), pltpu.VMEM((1, 1, 4, 4, 8, WIDTH), WIDE), pltpu.VMEM((8, WIDTH), WIDE)]
    scratch += scatter_buffers(BLOCKS, ROWS, LOW) + scatter_sems(BLOCKS) + scatter_sems(BLOCKS)
    scratch += scatter_buffers(1, 8, WIDE) + scatter_sems(1) + scatter_sems(1)
    scratch += total_scratch((8, WIDTH))
    return pl.pallas_call(
        whole_kernel,
        out_shape=out_shape,
        in_specs=[far] * len(given),
        out_specs=[far] * 2 + [vmem] * (len(out_shape) - 2),
        scratch_shapes=scratch,
        compiler_params=pltpu.CompilerParams(
            collective_id=0, has_side_effects=True, vmem_limit_bytes=62 * 2**20
        ),
    )(*[args[name] for name in ARGS], proj, down)


def finish_kernel(acts, dins, proj, down, table, shares, *outs):
    outs[0][...] = acts[...].reshape(1, 2 * SEQ, WIDTH)
    outs[1][...] = dins[...].reshape(1, 2 * SEQ, WIDTH)
    for block in range(2):
        rows = proj[block].astype(WIDE)
        for turn in range(3):
            for side in range(2):
                start = 16 * turn + 8 * side
                outs[2][0, 8 * turn : 8 * turn + 8, cols(2 * side + block)] = rows[start : start + 8]
    outs[3][0] = down[...].astype(WIDE)
    for out, row in zip(outs[4:8], (2, 3, 1, 0)):
        out[...] = shares[row : row + 1, :24]
    outs[8][0] = table[...]


def finish(*arrays):
    vmem = pl.BlockSpec(memory_space=pltpu.VMEM)
    share = jax.ShapeDtypeStruct((1, 24), WIDE)
    out_shape = [
        jax.ShapeDtypeStruct((1, 2 * SEQ, WIDTH), LOW),
        jax.ShapeDtypeStruct((1, 2 * SEQ, WIDTH), LOW),
        jax.ShapeDtypeStruct((1, 24, FF), WIDE),
        jax.ShapeDtypeStruct((1, ROWS, WIDTH), WIDE),
        share, share, share, share,
        jax.ShapeDtypeStruct((1, 8, WIDTH), WIDE),
    ]
    return pl.pallas_call(
        finish_kernel, out_shape=out_shape, in_specs=[vmem] * 6, out_specs=[vmem] * 9,
        compiler_params=pltpu.CompilerParams(vmem_limit_bytes=62 * 2**20),
    )(*arrays)


def body(
    tokens, doc_ids, region_ids, proj, down, ln_gain, ln_bias, bn_gain, bn_bias, region_table, out_cot
):
    args = dict(
        tokens=tokens.reshape(2, SEQ, WIDTH), doc_ids=doc_ids, region_ids=region_ids, ln_gain=ln_gain,
        ln_bias=ln_bias, bn_gain=bn_gain, bn_bias=bn_bias, table=region_table[0],
        out_cot=out_cot.reshape(2, SEQ, WIDTH),
    )
    return tuple(finish(*run_whole(args, proj, down)))


def solution(mesh):
    in_specs = (
        P("dp", None),
        P("dp", None),
        P("dp", None),
        P("pipe", "dp", None),
        P("pipe", "dp", None),
        P("pipe", None),
        P("pipe", None),
        P("pipe", None),
        P("pipe", None),
        P("pipe", None, None),
        P("dp", None),
    )
    out_specs = (
        P("pipe", "dp", None),
        P("pipe", "dp", None),
        P("pipe", "dp", None),
        P("pipe", "dp", None),
        P("pipe", "dp"),
        P("pipe", "dp"),
        P("pipe", "dp"),
        P("pipe", "dp"),
        P("pipe", "dp", None),
    )
    return jax.shard_map(body, mesh=mesh, in_specs=in_specs, out_specs=out_specs, check_vma=False)
```

```python
from functools import partial

import jax
import jax.numpy as jnp
from jax import lax
from jax.experimental import pallas as pl
from jax.experimental.pallas import tpu as pltpu
from jax.sharding import PartitionSpec as P

HEADS = 12
FF = 3072
EPSILON = 1e-05
LOW = jnp.bfloat16
WIDE = jnp.float32
MESH = pl.DeviceIdType.MESH
DMA = pltpu.SemaphoreType.DMA
BLOCKS = 4
ROWS = 48
WIDTH = 768


def place():
    group = lax.axis_index("dp")
    pipe = lax.axis_index("pipe")
    half = lax.div(group, 16)
    rest = lax.rem(group, 16)
    return group, pipe, half, lax.div(rest, 4), lax.rem(rest, 4)


def around(position, distance):
    return lax.rem(position + distance + 4, 4)


def group_of(half, depth, column):
    return half * 16 + depth * 4 + column


def along(route, first, second):
    return (second, first) if route == 0 else (first, second)


def to_group(src, dst, send, recv, group):
    return pltpu.make_async_remote_copy(
        src_ref=src,
        dst_ref=dst,
        send_sem=send,
        recv_sem=recv,
        device_id={"dp": group},
        device_id_type=MESH,
    )


def arrived(dst, recv):
    pltpu.make_async_copy(dst, dst, recv).wait()


def narrow(ref, route, block, half, first, second):
    depth, column = along(route, first, second)
    return ref.at[block, half, depth, column]


def wide(ref, route, block, half, second):
    if route == 0:
        return ref.at[block, half, second]
    return ref.at[block, half, :, second]


def greet(others):
    barrier = pltpu.get_barrier_semaphore()
    for device in others:
        pl.semaphore_signal(barrier, inc=1, device_id=device, device_id_type=MESH)


def meet(others):
    pl.semaphore_wait(pltpu.get_barrier_semaphore(), len(others))


def ring_devices():
    group, pipe, half, depth, column = place()
    return [
        {"dp": group_of(1 - half, depth, column)},
        {"dp": group_of(half, around(depth, 1), column)},
        {"dp": group_of(half, around(depth, -1), column)},
        {"dp": group_of(half, depth, around(column, 1))},
        {"dp": group_of(half, depth, around(column, -1))},
    ]


def gather_sems():
    return [DMA((BLOCKS,)), DMA((BLOCKS, 3)), DMA((BLOCKS, 2, 2)), DMA((BLOCKS, 2, 2))]


def part(ref, way):
    return ref.at[pl.ds(2 * way, 2)]


class Rings:
    def __init__(self, ref, sends, recvs):
        self.ref, self.sends, self.recvs = ref, sends, recvs
        self.group, self.pipe, self.half, self.depth, self.column = place()
        self.partner = group_of(1 - self.half, self.depth, self.column)

    def axes(self, route):
        return (self.column, self.depth) if route == 0 else (self.depth, self.column)

    def small_peer(self, route, distance):
        if route == 0:
            return group_of(self.half, self.depth, around(self.column, distance))
        return group_of(self.half, around(self.depth, distance), self.column)

    def large_peer(self, route, distance):
        return self.small_peer(1 - route, distance)

    def own(self, block):
        return self.ref.at[block, self.half, self.depth, self.column]

    def send(self, kind, index, src, dst, group):
        return to_group(src, dst, self.sends[kind].at[index], self.recvs[kind].at[index], group)


class Gather(Rings):
    def swap(self, route, block, half, position=None):
        second = self.axes(route)[1]
        slot = wide(self.ref, route, block, half, second)
        if position is not None:
            slot = narrow(self.ref, route, block, half, position, second)
        return self.send(0, (block,), slot, slot, self.partner)

    def small(self, route, block, distance):
        slot = self.own(block)
        return self.send(1, (block, distance - 1), slot, slot, self.small_peer(route, distance))

    def large(self, route, block, half, way, position=None):
        second = self.axes(route)[1]
        slot = wide(self.ref, route, block, half, second)
        if position is not None:
            slot = narrow(self.ref, route, block, half, position, second)
        return self.send(2, (block, half, way), slot, slot, self.large_peer(route, 1 - 2 * way))

    def large_relay(self, route, block, half, way):
        second = self.axes(route)[1]
        distance = 1 - 2 * way
        slot = part(wide(self.ref, route, block, half, around(second, -distance)), way)
        return self.send(3, (block, half, way), slot, slot, self.large_peer(route, distance))

    def pass_on(self, route, block, position):
        for way in range(2):
            self.large(route, block, self.half, way, position).start()
        self.swap(route, block, self.half, position).start()

    def start(self, route, block):
        for distance in range(1, 4):
            self.small(route, block, distance).start()
        self.pass_on(route, block, self.axes(route)[0])

    def end_small(self, route, block):
        for distance in (1, 3, 2):
            self.small(route, block, distance).wait_recv()
            self.pass_on(route, block, around(self.axes(route)[0], -distance))

    def relay_large(self, route, block, half):
        for way in range(2):
            self.large(route, block, half, way).wait_recv()
            self.large_relay(route, block, half, way).start()

    def swap_in(self, route, block):
        self.swap(route, block, 1 - self.half).wait_recv()
        for way in range(2):
            self.large(route, block, 1 - self.half, way).start()

    def last(self, route, block):
        for half in range(2):
            for way in range(2):
                self.large_relay(route, block, half, way).wait_recv()

    def steps(self):
        return [
            self.end_small,
            lambda route, block: self.relay_large(route, block, self.half),
            self.swap_in,
            lambda route, block: self.relay_large(route, block, 1 - self.half),
        ]

    def finish(self, route, block):
        self.swap(route, block, self.half).wait_send()
        for distance in range(1, 4):
            self.small(route, block, distance).wait_send()
        for half in range(2):
            for way in range(2):
                self.large(route, block, half, way).wait_send()
                self.large_relay(route, block, half, way).wait_send()


def scatter_buffers(blocks, rows, dtype):
    return [
        pltpu.VMEM((blocks, 2, 4, rows, WIDTH), dtype),
        pltpu.VMEM((blocks, 2, 2, 4, rows, WIDTH), dtype),
        pltpu.VMEM((blocks, 4, rows, WIDTH), dtype),
        pltpu.VMEM((blocks, 3, rows, WIDTH), dtype),
    ]


def scatter_sems(blocks):
    return [DMA((blocks, 2, 2)), DMA((blocks, 2, 2)), DMA((blocks,)), DMA((blocks, 3))]


def accumulate(target, others):
    total = target[...].astype(WIDE)
    for other in others:
        total = total + other[...].astype(WIDE)
    target[...] = total.astype(target.dtype)


class Scatter(Rings):
    def __init__(self, ref, buffers, sends, recvs, single=False):
        super().__init__(ref, sends, recvs)
        self.buffers, self.single = buffers, single

    def large_early(self, route, block, half, way):
        second = self.axes(route)[1]
        return self.send(
            0, (block, half, way), part(wide(self.ref, route, block, half, around(second, 2)), way),
            part(self.buffers[0].at[block, half], way), self.large_peer(route, 1 - 2 * way),
        )

    def large(self, route, block, half, way, side=None):
        second = self.axes(route)[1]
        distance = 1 - 2 * way
        src = wide(self.ref, route, block, half, around(second, distance))
        dst = self.buffers[1].at[block, way, half]
        if side is not None:
            src, dst = part(src, side), part(dst, side)
        return self.send(1, (block, way, half), src, dst, self.large_peer(route, distance))

    def swap(self, route, block, half):
        second = self.axes(route)[1]
        return self.send(
            2, (block,), wide(self.ref, route, block, half, second), self.buffers[2].at[block], self.partner
        )

    def target(self, route, block, distance):
        first, second = self.axes(route)
        half = 0 if self.single else self.half
        return narrow(self.ref, route, block, half, around(first, distance), second)

    def small(self, route, block, distance):
        return self.send(
            3, (block, distance - 1), self.target(route, block, distance), self.buffers[3].at[block, distance - 1],
            self.small_peer(route, distance),
        )

    def where(self, half, action):
        if self.single:
            pl.when(half == 0)(lambda: action(0))
        else:
            action(half)

    def begin(self, route, block, half):
        def run(half):
            for way in range(2):
                self.large_early(route, block, half, way).start()
                self.large(route, block, half, way, 1 - way).start()

        self.where(half, run)

    def middle(self, route, block, half):
        def run(half):
            second = self.axes(route)[1]
            for way in range(2):
                self.large_early(route, block, half, way).wait_recv()
                accumulate(
                    part(wide(self.ref, route, block, half, around(second, 1 - 2 * way)), way),
                    [part(self.buffers[0].at[block, half], way)],
                )
                self.large(route, block, half, way, way).start()

        self.where(half, run)

    def sum_large(self, route, block, half, others):
        for way in range(2):
            self.large(route, block, half, way).wait_recv()
        arrivals = [self.buffers[1].at[block, way, half] for way in range(2)]
        accumulate(wide(self.ref, route, block, half, self.axes(route)[1]), arrivals + others)

    def start(self, route, block):
        self.begin(route, block, 1 - self.half)

    def turn(self, route, block):
        self.middle(route, block, 1 - self.half)
        self.begin(route, block, self.half)

    def sum_other(self, route, block):
        def run(half):
            self.sum_large(route, block, half, [])
            self.swap(route, block, half).start()

        self.where(1 - self.half, run)

    def swap_begin(self, route, block):
        self.sum_other(route, block)
        self.begin(route, block, self.half)

    def sum_own(self, route, block):
        def run(half):
            self.swap(route, block, half).wait_recv()
            self.sum_large(route, block, half, [self.buffers[2].at[block]])
            for distance in range(1, 4):
                self.small(route, block, distance).start()

        self.where(self.half, run)

    def last(self, route, block):
        def run(half):
            for distance in range(1, 4):
                self.small(route, block, distance).wait_recv()
            arrivals = [self.buffers[3].at[block, index] for index in range(3)]
            accumulate(self.target(route, block, 0), arrivals)

        self.where(self.half, run)

    def steps(self):
        return [
            lambda route, block: self.middle(route, block, 1 - self.half),
            self.swap_begin,
            lambda route, block: self.middle(route, block, self.half),
            self.sum_own,
            self.last,
        ]

    def finish(self, route, block):
        def large(half):
            for way in range(2):
                self.large_early(route, block, half, way).wait_send()
                self.large(route, block, half, way).wait_send()

        def other(half):
            large(half)
            self.swap(route, block, half).wait_send()

        def own(half):
            large(half)
            for distance in range(1, 4):
                self.small(route, block, distance).wait_send()

        self.where(1 - self.half, other)
        self.where(self.half, own)


class Total:
    def __init__(self, first, second, third, sends, recvs):
        self.stages, self.sends, self.recvs = (first, second, third), sends, recvs
        self.group, self.pipe, self.half, self.depth, self.column = place()
        self.where = (self.column, self.depth, self.half)

    def copy(self, stage, distance):
        here, buffer = self.where[stage], self.stages[stage]
        if stage == 0:
            peer = group_of(self.half, self.depth, around(here, distance))
        elif stage == 1:
            peer = group_of(self.half, around(here, distance), self.column)
        else:
            peer = group_of(1 - here, self.depth, self.column)
        return to_group(
            buffer.at[here], buffer.at[here],
            self.sends.at[stage, distance - 1], self.recvs.at[stage, distance - 1], peer,
        )

    def distances(self, stage):
        return range(1, 4) if stage < 2 else range(1, 2)

    def send(self, stage, value):
        self.stages[stage][self.where[stage]] = value
        for distance in self.distances(stage):
            self.copy(stage, distance).start()

    def receive(self, stage):
        for distance in self.distances(stage):
            self.copy(stage, distance).wait_recv()
        total = self.stages[stage][0]
        for index in range(1, 4 if stage < 2 else 2):
            total = total + self.stages[stage][index]
        return total

    def finish(self):
        for stage in range(3):
            for distance in self.distances(stage):
                self.copy(stage, distance).wait_send()


def total_scratch(shape):
    return [
        pltpu.VMEM((4,) + shape, WIDE),
        pltpu.VMEM((4,) + shape, WIDE),
        pltpu.VMEM((2,) + shape, WIDE),
        DMA((3, 3)),
        DMA((3, 3)),
    ]


def all_dp_devices():
    group, pipe, half, depth, column = place()
    return ring_devices() + [
        {"dp": group_of(half, around(depth, 2), column)},
        {"dp": group_of(half, depth, around(column, 2))},
    ]


PAIRS = HEADS // 2
SEQ = 128
REGIONS = 128
TOKENS = 8192
CHUNKS = 4


def dot(left, right):
    return lax.dot_general(left, right, (((1,), (0,)), ((), ())), preferred_element_type=WIDE)


def dot_nt(left, right):
    return lax.dot_general(left, right, (((1,), (1,)), ((), ())), preferred_element_type=WIDE)


def dot_tn(left, right):
    return lax.dot_general(left, right, (((0,), (0,)), ((), ())), preferred_element_type=WIDE)


def cols(index, width=WIDTH):
    return slice(index * width, (index + 1) * width)


def two_heads(pair):
    lane = lax.broadcasted_iota(jnp.int32, pair.shape, 1)
    zero = jnp.zeros_like(pair)
    return jnp.concatenate([jnp.where(lane < 64, pair, zero), jnp.where(lane < 64, zero, pair)], 0)


def side_by_side(stacked):
    return jnp.concatenate([stacked[:SEQ], stacked[SEQ:]], 1)


def row_mean(value):
    return jnp.mean(value, -1, keepdims=True)


def chain_scratch():
    return dict(
        proj=pltpu.VMEM((CHUNKS, WIDTH, WIDTH), LOW),
        fin=pltpu.VMEM((2, SEQ, WIDTH), LOW),
        bin=pltpu.VMEM((2, SEQ, WIDTH), LOW),
        lowered=pltpu.VMEM((2, SEQ, WIDTH), LOW),
        acts=pltpu.VMEM((2, SEQ, WIDTH), LOW),
        dins=pltpu.VMEM((2, SEQ, WIDTH), LOW),
        extra=pltpu.VMEM((2, SEQ, WIDTH), WIDE),
        resid=pltpu.VMEM((2, SEQ, WIDTH), WIDE),
        normed=pltpu.VMEM((2, SEQ, WIDTH), WIDE),
        inverse=pltpu.VMEM((2, SEQ, 128), WIDE),
        normed_rows=pltpu.VMEM((REGIONS, WIDTH), WIDE),
        region_info=pltpu.VMEM((8, WIDTH), WIDE),
        column=pltpu.VMEM((REGIONS, 128), WIDE),
        qkv=pltpu.VMEM((2, SEQ, 3 * WIDTH), LOW),
        probs=pltpu.VMEM((2, PAIRS, 2 * SEQ, SEQ), WIDE),
        mixed=pltpu.VMEM((2, SEQ, WIDTH), LOW),
        dbranch=pltpu.VMEM((2, SEQ, WIDTH), LOW),
        dwide=pltpu.VMEM((2, SEQ, FF), LOW),
        act=pltpu.VMEM((2, SEQ, FF), LOW),
        slope=pltpu.VMEM((2, SEQ, FF), WIDE),
        dweight=pltpu.VMEM((2, WIDTH, WIDTH), WIDE),
        send=DMA((2, 2)),
        recv=DMA((2, 2)),
    )


def unpack_proj(full_ref, proj_ref):
    def run(index, _):
        half, depth = lax.div(index, 4), lax.rem(index, 4)
        rows = pl.ds(pl.multiple_of(index * 96, 96), 96)
        for block in range(2):
            value = full_ref[block, half, depth].astype(WIDE).reshape(12, 2, 8, WIDTH)
            for side in range(2):
                proj_ref[2 * side + block, rows] = value[:, side].reshape(96, WIDTH).astype(LOW)
        return 0

    lax.fori_loop(0, 8, run, 0)


class Chain:
    def __init__(self, args, full_ref, counts, outs, grads, s, await_down, send_down, send_proj):
        self.await_down, self.send_down, self.send_proj = await_down, send_down, send_proj
        self.args, self.full, self.outs, self.grads, self.s = args, full_ref, outs, grads, s
        self.pipe = lax.axis_index("pipe")
        self.attention = lax.rem(self.pipe, 2) == 0
        self.region_statistics(counts)
        self.each(self.region_terms)

    def region_statistics(self, counts):
        table_ref, s = self.args["table"], self.s
        column = jnp.transpose(jnp.broadcast_to(counts[0:1], (SEQ, REGIONS)))
        s["column"][...] = column
        for index in range(WIDTH // 128):
            lanes = cols(index, 128)
            table = table_ref[:, lanes].astype(WIDE)
            mean = jnp.sum(table * column, 0, keepdims=True) / TOKENS
            second = jnp.sum(table * table * column, 0, keepdims=True) / TOKENS
            inverse = lax.rsqrt(second - mean * mean + EPSILON)
            s["normed_rows"][:, lanes] = (table - mean) * inverse
            s["region_info"][0:1, lanes] = mean
            s["region_info"][1:2, lanes] = inverse
            s["region_info"][2:3, lanes] = inverse * self.args["bn_gain"][0:1, lanes]

    def region_terms(self, micro):
        embedded = dot_tn(self.marks(micro), self.args["table"][...])
        info = self.s["region_info"]
        self.s["extra"][micro] = (embedded - info[0:1]) * info[2:3] + self.args["bn_bias"][...]

    def marks(self, micro):
        ids = self.args["region_ids"][pl.ds(micro, 1), :]
        rank = lax.broadcasted_iota(jnp.int32, (REGIONS, SEQ), 0)
        return jnp.where(rank == ids, 1.0, 0.0).astype(LOW)

    def same_document(self, micro):
        ids = jnp.broadcast_to(self.args["doc_ids"][pl.ds(micro, 1), :].astype(WIDE), (SEQ, SEQ))
        same = jnp.where(ids == jnp.transpose(ids), 1.0, 0.0)
        return jnp.concatenate([same, same], 0) > 0.5

    def down(self, index):
        return self.full[2 + index // 2, index % 2].reshape(WIDTH, WIDTH)

    def turned_proj(self, index):
        return self.full[index // 2, index % 2].reshape(WIDTH, WIDTH)

    def turned_down(self, index):
        return self.grads[index // 2, index % 2].reshape(WIDTH, WIDTH)

    def turn_proj(self):
        for index in range(CHUNKS):
            turned = jnp.transpose(self.s["proj"][index])
            self.full[index // 2, index % 2] = turned.reshape(4, 4, ROWS, WIDTH)

    def turn_down(self):
        for index in range(CHUNKS):
            turned = jnp.transpose(self.down(index))
            self.grads[index // 2, index % 2] = turned.reshape(4, 4, ROWS, WIDTH)

    def hop(self, direction, micro):
        names = ("acts", "fin") if direction == 0 else ("dins", "bin")
        source, target = self.s[names[0]], self.s[names[1]]
        return pltpu.make_async_remote_copy(
            src_ref=source.at[micro], dst_ref=target.at[micro],
            send_sem=self.s["send"].at[direction, micro], recv_sem=self.s["recv"].at[direction, micro],
            device_id={"pipe": lax.rem(self.pipe + 1 + 2 * direction, 4)}, device_id_type=MESH,
        )

    def forward(self, micro):
        s, args = self.s, self.args

        @pl.when(self.pipe == 0)
        def _():
            s["fin"][micro] = args["tokens"][micro]

        @pl.when(self.pipe > 0)
        def _():
            self.hop(0, micro).wait_recv()

        summed = s["fin"][micro].astype(WIDE) + s["extra"][micro]
        lowered = summed.astype(LOW)
        s["lowered"][micro] = lowered
        s["resid"][micro] = summed

        @pl.when(self.attention)
        def _():
            self.attention_forward(micro, lowered)

        @pl.when(jnp.logical_not(self.attention))
        def _():
            self.feed_forward(micro, lowered)

        residual = s["resid"][micro]
        centered = residual - row_mean(residual)
        inverse = lax.rsqrt(row_mean(centered * centered) + EPSILON)
        normed = centered * inverse
        s["normed"][micro] = normed
        s["inverse"][micro] = jnp.broadcast_to(inverse, (SEQ, 128))
        s["acts"][micro] = (normed * args["ln_gain"][...] + args["ln_bias"][...]).astype(LOW)

        @pl.when(self.pipe < 3)
        def _():
            self.hop(0, micro).start()

    def attention_forward(self, micro, lowered):
        s = self.s
        for index in range(3):
            s["qkv"][micro, :, cols(index)] = dot(lowered, s["proj"][index]).astype(LOW)
        same = self.same_document(micro)
        scores, probs, mixed = [], [], []
        for pair in range(PAIRS):
            queries = two_heads(s["qkv"][micro, :, cols(pair, 128)])
            scores.append(dot_nt(queries, s["qkv"][micro, :, cols(PAIRS + pair, 128)]))
        scores = [jnp.where(same, score * 0.125, -1e30) for score in scores]
        tops = [jnp.max(score, -1, keepdims=True) for score in scores]
        powers = [jnp.exp(score - top) for score, top in zip(scores, tops)]
        totals = [jnp.sum(power, -1, keepdims=True) for power in powers]
        for pair in range(PAIRS):
            probs.append(powers[pair] / totals[pair])
            s["probs"][micro, pair] = probs[pair]
        for pair in range(PAIRS):
            values = two_heads(s["qkv"][micro, :, cols(2 * PAIRS + pair, 128)])
            mixed.append(dot(side_by_side(probs[pair].astype(LOW)), values))
        for pair in range(PAIRS):
            s["mixed"][micro, :, cols(pair, 128)] = mixed[pair].astype(LOW)
        s["resid"][micro] = s["resid"][micro] + dot(s["mixed"][micro], s["proj"][3])

    def feed_forward(self, micro, lowered):
        s = self.s
        branch = s["resid"][micro]
        for index in range(CHUNKS):
            hidden = dot(lowered, s["proj"][index])
            cumulative = 0.5 * (1.0 + lax.erf(hidden * (0.5 ** 0.5)))
            density = jnp.exp(hidden * hidden * -0.5) * 0.3989422804014327
            s["act"][micro, :, cols(index)] = (hidden * cumulative).astype(LOW)
            s["slope"][micro, :, cols(index)] = cumulative + hidden * density

        @pl.when((micro == 0) & (self.pipe == 1))
        def _():
            self.await_down()

        for index in range(CHUNKS):
            branch = branch + dot(s["act"][micro, :, cols(index)], self.down(index))
        s["resid"][micro] = branch

    def backward(self, micro):
        s, args = self.s, self.args

        @pl.when(self.pipe == 3)
        def _():
            s["bin"][micro] = args["out_cot"][micro]

        @pl.when(self.pipe < 3)
        def _():
            self.hop(1, micro).wait_recv()

        gout = s["bin"][micro].astype(WIDE)
        normed = s["normed"][micro]
        dnormed = gout * args["ln_gain"][...]
        dres = s["inverse"][micro][:, 0:1] * (
            dnormed - row_mean(dnormed) - normed * row_mean(dnormed * normed)
        )
        s["resid"][micro] = dres
        s["dbranch"][micro] = dres.astype(LOW)

        @pl.when(self.attention)
        def _():
            self.attention_backward(micro)

        @pl.when((self.pipe == 0) & (micro == 1))
        def _():
            self.send_proj(self)

        @pl.when(self.attention)
        def _():
            total = s["resid"][micro]
            for index in range(3):
                total = total + dot(s["dwide"][micro, :, cols(index)], self.turned_proj(index))
            self.input_gradient(micro, total)

        @pl.when((self.pipe == 1) & (micro == 1))
        def _():
            self.send_down(self)

        @pl.when(jnp.logical_not(self.attention))
        def _():
            self.hidden_gradient(micro)

        @pl.when((self.pipe == 1) & (micro == 1))
        def _():
            self.send_proj(self)

        @pl.when(jnp.logical_not(self.attention))
        def _():
            total = s["resid"][micro]
            for index in range(CHUNKS):
                total = total + dot(s["dwide"][micro, :, cols(index)], self.turned_proj(index))
            self.input_gradient(micro, total)

        @pl.when(self.pipe > 0)
        def _():
            self.hop(1, micro).start()

    def sums(self, micro):
        s = self.s
        stats = self.outs["stats"]
        gout = s["bin"][micro].astype(WIDE)
        stats[2:3] = stats[2:3] + jnp.sum(gout * s["normed"][micro], 0, keepdims=True)
        stats[3:4] = stats[3:4] + jnp.sum(gout, 0, keepdims=True)
        marks = self.marks(micro)
        dsum = s["resid"][micro]
        high = s["dins"][micro]
        rest = (dsum - high.astype(WIDE)).astype(LOW)
        region = self.outs["region"]
        added = dot(marks, high) + dot(marks, rest)
        region[0, 0] = region[0, 0] + added.reshape(4, 4, 8, WIDTH)

    def input_gradient(self, micro, dsum):
        self.s["resid"][micro] = dsum
        self.s["dins"][micro] = dsum.astype(LOW)

    def attention_backward(self, micro):
        s, pairs = self.s, range(PAIRS)
        dmixed = dot(s["dbranch"][micro], self.turned_proj(3)).astype(LOW)
        pieces = [[s["qkv"][micro, :, cols(part * PAIRS + pair, 128)] for part in range(3)] for pair in pairs]
        grads = [two_heads(dmixed[:, cols(pair, 128)]) for pair in pairs]
        dprobs = [dot_nt(grads[pair], pieces[pair][2]) for pair in pairs]
        probs = [s["probs"][micro, pair] for pair in pairs]
        dvalues = [dot_tn(probs[pair].astype(LOW), grads[pair]) for pair in pairs]
        sums = [jnp.sum(dprobs[pair] * probs[pair], -1, keepdims=True) for pair in pairs]
        dscores = [(probs[pair] * (dprobs[pair] - sums[pair])).astype(LOW) for pair in pairs]
        dkeys = [dot_tn(dscores[pair], two_heads(pieces[pair][0])) * 0.125 for pair in pairs]
        dqueries = [dot(side_by_side(dscores[pair]), two_heads(pieces[pair][1])) * 0.125 for pair in pairs]
        for pair in pairs:
            for part, value in enumerate((dqueries[pair], dkeys[pair], dvalues[pair])):
                s["dwide"][micro, :, cols(part * PAIRS + pair, 128)] = value.astype(LOW)

    def hidden_gradient(self, micro):
        s = self.s
        dbranch = s["dbranch"][micro]
        for index in range(CHUNKS):
            dact = dot(dbranch, self.turned_down(index))
            s["dwide"][micro, :, cols(index)] = (dact * s["slope"][micro, :, cols(index)]).astype(LOW)

    def weight_gradients(self, block):
        s = self.s
        lowered = s["lowered"][...].reshape(2 * SEQ, WIDTH)
        for side in range(2):
            quarter = 2 * side + block
            if quarter == 3:
                @pl.when(self.attention)
                def _():
                    left = s["mixed"][...].reshape(2 * SEQ, WIDTH)
                    s["dweight"][1] = dot_tn(left, s["dbranch"][...].reshape(2 * SEQ, WIDTH))

                @pl.when(jnp.logical_not(self.attention))
                def _():
                    right = s["dwide"][:, :, cols(3)].reshape(2 * SEQ, WIDTH)
                    s["dweight"][1] = dot_tn(lowered, right)
            else:
                right = s["dwide"][:, :, cols(quarter)].reshape(2 * SEQ, WIDTH)
                s["dweight"][side] = dot_tn(lowered, right)

        def run(index, _):
            half, depth = lax.div(index, 4), lax.rem(index, 4)
            rows = pl.ds(pl.multiple_of(index * 96, 96), 96)
            sides = [s["dweight"][side, rows].reshape(12, 1, 8, WIDTH) for side in range(2)]
            value = jnp.concatenate(sides, 1).reshape(4, ROWS, WIDTH)
            self.grads[block, half, depth] = value.astype(LOW)
            return 0

        lax.fori_loop(0, 8, run, 0)

    def down_gradients(self, block):
        s = self.s
        dbranch = s["dbranch"][...].reshape(2 * SEQ, WIDTH)
        for half in range(2):
            act = s["act"][:, :, cols(2 * (block - 2) + half)].reshape(2 * SEQ, WIDTH)
            self.grads[block, half] = dot_tn(act, dbranch).astype(LOW).reshape(4, 4, ROWS, WIDTH)

    def table_gradient(self, table_sum, stats):
        s = self.s
        group = lax.axis_index("dp")
        rows = pl.ds(pl.multiple_of(lax.rem(group, 16) * 8, 8), 8)
        counts = jnp.concatenate([s["column"][rows]] * (WIDTH // 128), 1)
        mean = stats[0:1] / TOKENS + s["normed_rows"][rows] * (stats[1:2] / TOKENS)
        grad = s["region_info"][2:3] * (table_sum - counts * mean)
        return jnp.where(group < 16, grad, 0.0)

    def start_stats(self):
        self.outs["stats"][...] = jnp.zeros((8, WIDTH), WIDE)
        self.outs["region"][...] = jnp.zeros((1, 1, 4, 4, 8, WIDTH), WIDE)

    def end_stats(self):
        region, stats = self.outs["region"][0, 0].reshape(REGIONS, WIDTH), self.outs["stats"]
        stats[0:1] = jnp.sum(region, 0, keepdims=True)
        stats[1:2] = jnp.sum(region * self.s["normed_rows"][...], 0, keepdims=True)

    def each(self, action):
        lax.fori_loop(0, 2, lambda micro, _: (action(micro), 0)[1], 0)

    def finish(self):
        def run(micro):
            @pl.when(self.pipe < 3)
            def _():
                self.hop(0, micro).wait_send()

            @pl.when(self.pipe > 0)
            def _():
                self.hop(1, micro).wait_send()

        self.each(run)


ARGS = ("tokens", "doc_ids", "region_ids", "ln_gain", "ln_bias", "bn_gain", "bn_bias", "table", "out_cot")
def pack_proj(proj_ref, gather):
    for block in range(2):
        parts = []
        for turn in range(3):
            rows = slice(8 * turn, 8 * turn + 8)
            for side in range(2):
                parts.append(proj_ref[0, rows, cols(2 * side + block)].astype(WIDE))
        gather.own(block)[...] = jnp.concatenate(parts, 0).astype(LOW)


def own_counts(region_ids_ref):
    rank = lax.broadcasted_iota(jnp.int32, (REGIONS, SEQ), 0)
    total = jnp.zeros((8, REGIONS), WIDE)
    for micro in range(2):
        marks = jnp.where(rank == region_ids_ref[micro : micro + 1, :], 1.0, 0.0).astype(LOW)
        total = total + dot_nt(jnp.ones((8, SEQ), LOW), marks)
    return total


FAR = ("region_ids", "proj", "down", "table", "bn_gain", "bn_bias", "doc_ids", "ln_gain", "ln_bias", "tokens", "out_cot")


def whole_kernel(*refs):
    refs = list(refs)

    def take(count):
        taken = refs[:count]
        del refs[:count]
        return taken

    given = dict(zip(ARGS + ("proj", "down"), take(len(ARGS) + 2)))
    acts_out, dins_out, proj_out, down_out, table_out, shares_out = take(6)
    local_sem, cross_send, cross_recv = take(3)
    s = dict(zip(chain_scratch(), take(len(chain_scratch()))))
    near = dict(zip(FAR, take(len(FAR))))
    full = take(1)[0]
    gather = Gather(full, take(4), take(4))
    counted = Total(*take(5))
    held, region_held, stats = take(3)
    main = Scatter(held, take(4), take(4), take(4))
    region = Scatter(region_held, take(4), take(4), take(4), single=True)
    total = Total(*take(5))

    pipe = gather.pipe
    ffn = lax.rem(pipe, 2) == 1
    pairs = lax.rem(pipe, 2) + 1
    sibling = pipe + 1 - 2 * lax.rem(pipe, 2)
    fetches = [
        pltpu.make_async_copy(
            given[name].at[:REGIONS] if name == "table" else given[name], near[name], local_sem.at[index]
        )
        for index, name in enumerate(FAR)
    ]
    for fetch in fetches:
        fetch.start()
    others = all_dp_devices() + [{"pipe": lax.rem(pipe + 1, 4)}, {"pipe": lax.rem(pipe + 3, 4)}]
    greet(others)
    for fetch in fetches[:3]:
        fetch.wait()
    pack_proj(near["proj"], gather)
    gather.own(3)[...] = near["down"][0]
    meet(others)
    for route in range(2):
        gather.start(route, route)
    cross = pltpu.make_async_remote_copy(
        src_ref=gather.own(3), dst_ref=gather.own(2), send_sem=cross_send.at[0], recv_sem=cross_recv.at[0],
        device_id={"pipe": sibling}, device_id_type=MESH,
    )

    @pl.when(jnp.logical_not(ffn))
    def _():
        cross.start()

    @pl.when(ffn)
    def _():
        gather.start(1, 3)
        cross.wait_recv()
        gather.start(0, 2)

    counted.send(0, own_counts(near["region_ids"]))

    def each(action):
        def run(pair, _):
            for route in range(2):
                action(route, 2 * pair + route)
            return 0

        lax.fori_loop(0, pairs, run, 0)

    for index, step in enumerate(gather.steps()):
        each(step)
        if index in (1, 2):
            counted.send(index, counted.receive(index - 1))
    for fetch in fetches[3:]:
        fetch.wait()
    outs = dict(stats=stats, region=region_held)

    def await_down():
        for route in range(2):
            gather.last(route, 2 + route)

    def send_down(chain):
        for route in range(2):
            chain.down_gradients(2 + route)
            main.start(route, 2 + route)

    def send_proj(chain):
        for block in range(2):
            chain.weight_gradients(block)
            main.start(block, block)

    chain = Chain(near, full, counted.receive(2), outs, held, s, await_down, send_down, send_proj)
    chain.start_stats()
    for route in range(2):
        gather.last(route, route)
    unpack_proj(full, s["proj"])

    def turn():
        for route in range(2):
            gather.finish(route, route)
        chain.turn_proj()
        pl.when(pipe == 3)(await_down)
        pl.when(ffn)(chain.turn_down)

    pl.when(pipe >= 2)(turn)

    def tick(index, _):
        back = jnp.where(pipe == 3, lax.rem(index, 2), lax.div(index, 2))
        micro = jnp.where(pipe == 3, lax.div(index, 2), lax.rem(index, 2))
        pl.when((index == 2) & (pipe < 2))(turn)
        pl.when(back == 0)(lambda: chain.forward(micro))
        pl.when(back == 1)(lambda: chain.backward(micro))
        return 0

    lax.fori_loop(0, 4, tick, 0)
    put_acts = pltpu.make_async_copy(s["acts"], acts_out, local_sem.at[len(FAR)])
    put_dins = pltpu.make_async_copy(s["dins"], dins_out, local_sem.at[len(FAR) + 1])
    put_acts.start()
    put_dins.start()
    pl.when(pipe > 1)(lambda: send_proj(chain))
    chain.each(chain.sums)
    chain.end_stats()
    total.send(0, stats[...])

    def regions(action):
        for route in range(2):
            pl.when(lax.rem(pipe, 2) == route)(lambda route=route: action(route, 0))

    regions(region.start)

    @pl.when(pipe == 3)
    def _():
        send_down(chain)

    def each_late(action):
        def run(pair, _):
            for route in range(2):
                action(route, 2 * (pairs - 1 - pair) + route)
            return 0

        lax.fori_loop(0, pairs, run, 0)

    for index, (step, region_step) in enumerate(zip(main.steps(), region.steps())):
        each_late(step)
        regions(region_step)
        if index in (1, 2):
            total.send(index, total.receive(index - 1))
    back = pltpu.make_async_remote_copy(
        src_ref=main.own(2), dst_ref=down_out, send_sem=cross_send.at[1], recv_sem=cross_recv.at[1],
        device_id={"pipe": sibling}, device_id_type=MESH,
    )

    @pl.when(ffn)
    def _():
        back.start()
        down_out[...] = main.own(3)[...]

    for block in range(2):
        proj_out[block] = main.own(block)[...]
    summed = total.receive(2)
    table_out[...] = chain.table_gradient(region_held[0, 0, main.depth, main.column], summed)
    shift = lax.rem(WIDTH - 24 * gather.group, WIDTH)
    shares_out[...] = pltpu.roll(summed, shift, 1)[:, :128]

    @pl.when(ffn)
    def _():
        for route in range(2):
            gather.finish(route, 2 + route)

    each(main.finish)
    regions(region.finish)
    counted.finish()
    total.finish()
    chain.finish()
    put_acts.wait()
    put_dins.wait()

    @pl.when(ffn)
    def _():
        back.wait_send()

    @pl.when(jnp.logical_not(ffn))
    def _():
        cross.wait_send()
        back.wait_recv()


def run_whole(args, proj, down):
    micro = (2, SEQ, WIDTH)
    vmem, far = pl.BlockSpec(memory_space=pltpu.VMEM), pl.BlockSpec(memory_space=pl.ANY)
    out_shape = [
        jax.ShapeDtypeStruct(micro, LOW),
        jax.ShapeDtypeStruct(micro, LOW),
        jax.ShapeDtypeStruct((2, ROWS, WIDTH), LOW),
        jax.ShapeDtypeStruct((ROWS, WIDTH), LOW),
        jax.ShapeDtypeStruct((8, WIDTH), WIDE),
        jax.ShapeDtypeStruct((8, 128), WIDE),
    ]
    blocks = (BLOCKS, 2, 4, 4, ROWS, WIDTH)
    given = dict(args, proj=proj, down=down)
    scratch = [DMA((len(FAR) + 2,)), DMA((2,)), DMA((2,))]
    scratch += list(chain_scratch().values())
    scratch += [
        pltpu.VMEM((REGIONS, WIDTH) if name == "table" else given[name].shape, given[name].dtype)
        for name in FAR
    ]
    scratch += [pltpu.VMEM(blocks, LOW)] + gather_sems() + gather_sems()
    scratch += total_scratch((8, REGIONS))
    scratch += [pltpu.VMEM(blocks, LOW), pltpu.VMEM((1, 1, 4, 4, 8, WIDTH), WIDE), pltpu.VMEM((8, WIDTH), WIDE)]
    scratch += scatter_buffers(BLOCKS, ROWS, LOW) + scatter_sems(BLOCKS) + scatter_sems(BLOCKS)
    scratch += scatter_buffers(1, 8, WIDE) + scatter_sems(1) + scatter_sems(1)
    scratch += total_scratch((8, WIDTH))
    return pl.pallas_call(
        whole_kernel,
        out_shape=out_shape,
        in_specs=[far] * len(given),
        out_specs=[far] * 2 + [vmem] * (len(out_shape) - 2),
        scratch_shapes=scratch,
        compiler_params=pltpu.CompilerParams(
            collective_id=0, has_side_effects=True, vmem_limit_bytes=62 * 2**20
        ),
    )(*[args[name] for name in ARGS], proj, down)


def finish_kernel(acts, dins, proj, down, table, shares, *outs):
    outs[0][...] = acts[...].reshape(1, 2 * SEQ, WIDTH)
    outs[1][...] = dins[...].reshape(1, 2 * SEQ, WIDTH)
    for block in range(2):
        rows = proj[block].astype(WIDE)
        for turn in range(3):
            for side in range(2):
                start = 16 * turn + 8 * side
                outs[2][0, 8 * turn : 8 * turn + 8, cols(2 * side + block)] = rows[start : start + 8]
    outs[3][0] = down[...].astype(WIDE)
    for out, row in zip(outs[4:8], (2, 3, 1, 0)):
        out[...] = shares[row : row + 1, :24]
    outs[8][0] = table[...]


def finish(*arrays):
    vmem = pl.BlockSpec(memory_space=pltpu.VMEM)
    share = jax.ShapeDtypeStruct((1, 24), WIDE)
    out_shape = [
        jax.ShapeDtypeStruct((1, 2 * SEQ, WIDTH), LOW),
        jax.ShapeDtypeStruct((1, 2 * SEQ, WIDTH), LOW),
        jax.ShapeDtypeStruct((1, 24, FF), WIDE),
        jax.ShapeDtypeStruct((1, ROWS, WIDTH), WIDE),
        share, share, share, share,
        jax.ShapeDtypeStruct((1, 8, WIDTH), WIDE),
    ]
    return pl.pallas_call(
        finish_kernel, out_shape=out_shape, in_specs=[vmem] * 6, out_specs=[vmem] * 9,
        compiler_params=pltpu.CompilerParams(vmem_limit_bytes=62 * 2**20),
    )(*arrays)


def body(
    tokens, doc_ids, region_ids, proj, down, ln_gain, ln_bias, bn_gain, bn_bias, region_table, out_cot
):
    args = dict(
        tokens=tokens.reshape(2, SEQ, WIDTH), doc_ids=doc_ids, region_ids=region_ids, ln_gain=ln_gain,
        ln_bias=ln_bias, bn_gain=bn_gain, bn_bias=bn_bias, table=region_table[0],
        out_cot=out_cot.reshape(2, SEQ, WIDTH),
    )
    return tuple(finish(*run_whole(args, proj, down)))


def solution(mesh):
    in_specs = (
        P("dp", None),
        P("dp", None),
        P("dp", None),
        P("pipe", "dp", None),
        P("pipe", "dp", None),
        P("pipe", None),
        P("pipe", None),
        P("pipe", None),
        P("pipe", None),
        P("pipe", None, None),
        P("dp", None),
    )
    out_specs = (
        P("pipe", "dp", None),
        P("pipe", "dp", None),
        P("pipe", "dp", None),
        P("pipe", "dp", None),
        P("pipe", "dp"),
        P("pipe", "dp"),
        P("pipe", "dp"),
        P("pipe", "dp"),
        P("pipe", "dp", None),
    )
    return jax.shard_map(body, mesh=mesh, in_specs=in_specs, out_specs=out_specs, check_vma=False)
```

```python
from functools import partial

import jax
import jax.numpy as jnp
from jax import lax
from jax.experimental import pallas as pl
from jax.experimental.pallas import tpu as pltpu
from jax.sharding import PartitionSpec as P

HEADS = 12
FF = 3072
EPSILON = 1e-05
LOW = jnp.bfloat16
WIDE = jnp.float32
MESH = pl.DeviceIdType.MESH
DMA = pltpu.SemaphoreType.DMA
BLOCKS = 4
ROWS = 48
WIDTH = 768


def place():
    group = lax.axis_index("dp")
    pipe = lax.axis_index("pipe")
    half = lax.div(group, 16)
    rest = lax.rem(group, 16)
    return group, pipe, half, lax.div(rest, 4), lax.rem(rest, 4)


def around(position, distance):
    return lax.rem(position + distance + 4, 4)


def group_of(half, depth, column):
    return half * 16 + depth * 4 + column


def along(route, first, second):
    return (second, first) if route == 0 else (first, second)


def to_group(src, dst, send, recv, group):
    return pltpu.make_async_remote_copy(
        src_ref=src,
        dst_ref=dst,
        send_sem=send,
        recv_sem=recv,
        device_id={"dp": group},
        device_id_type=MESH,
    )


def arrived(dst, recv):
    pltpu.make_async_copy(dst, dst, recv).wait()


def narrow(ref, route, block, half, first, second):
    depth, column = along(route, first, second)
    return ref.at[block, half, depth, column]


def wide(ref, route, block, half, second):
    if route == 0:
        return ref.at[block, half, second]
    return ref.at[block, half, :, second]


def greet(others):
    barrier = pltpu.get_barrier_semaphore()
    for device in others:
        pl.semaphore_signal(barrier, inc=1, device_id=device, device_id_type=MESH)


def meet(others):
    pl.semaphore_wait(pltpu.get_barrier_semaphore(), len(others))


def ring_devices():
    group, pipe, half, depth, column = place()
    return [
        {"dp": group_of(1 - half, depth, column)},
        {"dp": group_of(half, around(depth, 1), column)},
        {"dp": group_of(half, around(depth, -1), column)},
        {"dp": group_of(half, depth, around(column, 1))},
        {"dp": group_of(half, depth, around(column, -1))},
    ]


def gather_sems():
    return [DMA((BLOCKS,)), DMA((BLOCKS, 3)), DMA((BLOCKS, 2, 2)), DMA((BLOCKS, 2, 2))]


def part(ref, way):
    return ref.at[pl.ds(2 * way, 2)]


class Rings:
    def __init__(self, ref, sends, recvs):
        self.ref, self.sends, self.recvs = ref, sends, recvs
        self.group, self.pipe, self.half, self.depth, self.column = place()
        self.partner = group_of(1 - self.half, self.depth, self.column)

    def axes(self, route):
        return (self.column, self.depth) if route == 0 else (self.depth, self.column)

    def small_peer(self, route, distance):
        if route == 0:
            return group_of(self.half, self.depth, around(self.column, distance))
        return group_of(self.half, around(self.depth, distance), self.column)

    def large_peer(self, route, distance):
        return self.small_peer(1 - route, distance)

    def own(self, block):
        return self.ref.at[block, self.half, self.depth, self.column]

    def send(self, kind, index, src, dst, group):
        return to_group(src, dst, self.sends[kind].at[index], self.recvs[kind].at[index], group)


class Gather(Rings):
    def swap(self, route, block, half, position=None):
        second = self.axes(route)[1]
        slot = wide(self.ref, route, block, half, second)
        if position is not None:
            slot = narrow(self.ref, route, block, half, position, second)
        return self.send(0, (block,), slot, slot, self.partner)

    def small(self, route, block, distance):
        slot = self.own(block)
        return self.send(1, (block, distance - 1), slot, slot, self.small_peer(route, distance))

    def large(self, route, block, half, way, position=None):
        second = self.axes(route)[1]
        slot = wide(self.ref, route, block, half, second)
        if position is not None:
            slot = narrow(self.ref, route, block, half, position, second)
        return self.send(2, (block, half, way), slot, slot, self.large_peer(route, 1 - 2 * way))

    def large_relay(self, route, block, half, way):
        second = self.axes(route)[1]
        distance = 1 - 2 * way
        slot = part(wide(self.ref, route, block, half, around(second, -distance)), way)
        return self.send(3, (block, half, way), slot, slot, self.large_peer(route, distance))

    def pass_on(self, route, block, position):
        for way in range(2):
            self.large(route, block, self.half, way, position).start()
        self.swap(route, block, self.half, position).start()

    def start(self, route, block):
        for distance in range(1, 4):
            self.small(route, block, distance).start()
        self.pass_on(route, block, self.axes(route)[0])

    def end_small(self, route, block):
        for distance in (1, 3, 2):
            self.small(route, block, distance).wait_recv()
            self.pass_on(route, block, around(self.axes(route)[0], -distance))

    def relay_large(self, route, block, half):
        for way in range(2):
            self.large(route, block, half, way).wait_recv()
            self.large_relay(route, block, half, way).start()

    def swap_in(self, route, block):
        self.swap(route, block, 1 - self.half).wait_recv()
        for way in range(2):
            self.large(route, block, 1 - self.half, way).start()

    def last(self, route, block, half):
        for way in range(2):
            self.large_relay(route, block, half, way).wait_recv()

    def steps(self):
        return [
            self.end_small,
            lambda route, block: self.relay_large(route, block, self.half),
            self.swap_in,
            lambda route, block: self.relay_large(route, block, 1 - self.half),
        ]

    def finish(self, route, block):
        self.swap(route, block, self.half).wait_send()
        for distance in range(1, 4):
            self.small(route, block, distance).wait_send()
        for half in range(2):
            for way in range(2):
                self.large(route, block, half, way).wait_send()
                self.large_relay(route, block, half, way).wait_send()


def scatter_buffers(blocks, rows, dtype):
    return [
        pltpu.VMEM((blocks, 2, 4, rows, WIDTH), dtype),
        pltpu.VMEM((blocks, 2, 2, 4, rows, WIDTH), dtype),
        pltpu.VMEM((blocks, 4, rows, WIDTH), dtype),
        pltpu.VMEM((blocks, 3, rows, WIDTH), dtype),
    ]


def scatter_sems(blocks):
    return [DMA((blocks, 2, 2)), DMA((blocks, 2, 2)), DMA((blocks,)), DMA((blocks, 3))]


def accumulate(target, others):
    total = target[...].astype(WIDE)
    for other in others:
        total = total + other[...].astype(WIDE)
    target[...] = total.astype(target.dtype)


class Scatter(Rings):
    def __init__(self, ref, buffers, sends, recvs, single=False):
        super().__init__(ref, sends, recvs)
        self.buffers, self.single = buffers, single

    def large_early(self, route, block, half, way):
        second = self.axes(route)[1]
        return self.send(
            0, (block, half, way), part(wide(self.ref, route, block, half, around(second, 2)), way),
            part(self.buffers[0].at[block, half], way), self.large_peer(route, 1 - 2 * way),
        )

    def large(self, route, block, half, way, side=None):
        second = self.axes(route)[1]
        distance = 1 - 2 * way
        src = wide(self.ref, route, block, half, around(second, distance))
        dst = self.buffers[1].at[block, way, half]
        if side is not None:
            src, dst = part(src, side), part(dst, side)
        return self.send(1, (block, way, half), src, dst, self.large_peer(route, distance))

    def swap(self, route, block, half):
        second = self.axes(route)[1]
        return self.send(
            2, (block,), wide(self.ref, route, block, half, second), self.buffers[2].at[block], self.partner
        )

    def target(self, route, block, distance):
        first, second = self.axes(route)
        half = 0 if self.single else self.half
        return narrow(self.ref, route, block, half, around(first, distance), second)

    def small(self, route, block, distance):
        return self.send(
            3, (block, distance - 1), self.target(route, block, distance), self.buffers[3].at[block, distance - 1],
            self.small_peer(route, distance),
        )

    def where(self, half, action):
        if self.single:
            pl.when(half == 0)(lambda: action(0))
        else:
            action(half)

    def begin(self, route, block, half):
        def run(half):
            for way in range(2):
                self.large_early(route, block, half, way).start()
                self.large(route, block, half, way, 1 - way).start()

        self.where(half, run)

    def middle(self, route, block, half):
        def run(half):
            second = self.axes(route)[1]
            for way in range(2):
                self.large_early(route, block, half, way).wait_recv()
                accumulate(
                    part(wide(self.ref, route, block, half, around(second, 1 - 2 * way)), way),
                    [part(self.buffers[0].at[block, half], way)],
                )
                self.large(route, block, half, way, way).start()

        self.where(half, run)

    def sum_large(self, route, block, half, others):
        for way in range(2):
            self.large(route, block, half, way).wait_recv()
        arrivals = [self.buffers[1].at[block, way, half] for way in range(2)]
        accumulate(wide(self.ref, route, block, half, self.axes(route)[1]), arrivals + others)

    def start(self, route, block):
        self.begin(route, block, 1 - self.half)

    def turn(self, route, block):
        self.middle(route, block, 1 - self.half)
        self.begin(route, block, self.half)

    def sum_other(self, route, block):
        def run(half):
            self.sum_large(route, block, half, [])
            self.swap(route, block, half).start()

        self.where(1 - self.half, run)

    def swap_begin(self, route, block):
        self.sum_other(route, block)
        self.begin(route, block, self.half)

    def sum_own(self, route, block):
        def run(half):
            self.swap(route, block, half).wait_recv()
            self.sum_large(route, block, half, [self.buffers[2].at[block]])
            for distance in range(1, 4):
                self.small(route, block, distance).start()

        self.where(self.half, run)

    def last(self, route, block):
        def run(half):
            for distance in range(1, 4):
                self.small(route, block, distance).wait_recv()
            arrivals = [self.buffers[3].at[block, index] for index in range(3)]
            accumulate(self.target(route, block, 0), arrivals)

        self.where(self.half, run)

    def steps(self):
        return [
            lambda route, block: self.middle(route, block, 1 - self.half),
            self.swap_begin,
            lambda route, block: self.middle(route, block, self.half),
            self.sum_own,
            self.last,
        ]

    def finish(self, route, block):
        def large(half):
            for way in range(2):
                self.large_early(route, block, half, way).wait_send()
                self.large(route, block, half, way).wait_send()

        def other(half):
            large(half)
            self.swap(route, block, half).wait_send()

        def own(half):
            large(half)
            for distance in range(1, 4):
                self.small(route, block, distance).wait_send()

        self.where(1 - self.half, other)
        self.where(self.half, own)


class Total:
    def __init__(self, first, second, third, sends, recvs):
        self.stages, self.sends, self.recvs = (first, second, third), sends, recvs
        self.group, self.pipe, self.half, self.depth, self.column = place()
        self.where = (self.column, self.depth, self.half)

    def copy(self, stage, distance):
        here, buffer = self.where[stage], self.stages[stage]
        if stage == 0:
            peer = group_of(self.half, self.depth, around(here, distance))
        elif stage == 1:
            peer = group_of(self.half, around(here, distance), self.column)
        else:
            peer = group_of(1 - here, self.depth, self.column)
        return to_group(
            buffer.at[here], buffer.at[here],
            self.sends.at[stage, distance - 1], self.recvs.at[stage, distance - 1], peer,
        )

    def distances(self, stage):
        return range(1, 4) if stage < 2 else range(1, 2)

    def send(self, stage, value):
        self.stages[stage][self.where[stage]] = value
        for distance in self.distances(stage):
            self.copy(stage, distance).start()

    def receive(self, stage):
        for distance in self.distances(stage):
            self.copy(stage, distance).wait_recv()
        total = self.stages[stage][0]
        for index in range(1, 4 if stage < 2 else 2):
            total = total + self.stages[stage][index]
        return total

    def finish(self):
        for stage in range(3):
            for distance in self.distances(stage):
                self.copy(stage, distance).wait_send()


def total_scratch(shape):
    return [
        pltpu.VMEM((4,) + shape, WIDE),
        pltpu.VMEM((4,) + shape, WIDE),
        pltpu.VMEM((2,) + shape, WIDE),
        DMA((3, 3)),
        DMA((3, 3)),
    ]


def all_dp_devices():
    group, pipe, half, depth, column = place()
    return ring_devices() + [
        {"dp": group_of(half, around(depth, 2), column)},
        {"dp": group_of(half, depth, around(column, 2))},
    ]


PAIRS = HEADS // 2
SEQ = 128
REGIONS = 128
TOKENS = 8192
CHUNKS = 4


def dot(left, right):
    return lax.dot_general(left, right, (((1,), (0,)), ((), ())), preferred_element_type=WIDE)


def dot_nt(left, right):
    return lax.dot_general(left, right, (((1,), (1,)), ((), ())), preferred_element_type=WIDE)


def dot_tn(left, right):
    return lax.dot_general(left, right, (((0,), (0,)), ((), ())), preferred_element_type=WIDE)


def cols(index, width=WIDTH):
    return slice(index * width, (index + 1) * width)


def two_heads(pair):
    lane = lax.broadcasted_iota(jnp.int32, pair.shape, 1)
    zero = jnp.zeros_like(pair)
    return jnp.concatenate([jnp.where(lane < 64, pair, zero), jnp.where(lane < 64, zero, pair)], 0)


def side_by_side(stacked):
    return jnp.concatenate([stacked[:SEQ], stacked[SEQ:]], 1)


def row_mean(value):
    return jnp.mean(value, -1, keepdims=True)


def chain_scratch():
    return dict(
        proj=pltpu.VMEM((CHUNKS, WIDTH, WIDTH), LOW),
        fin=pltpu.VMEM((2, SEQ, WIDTH), LOW),
        bin=pltpu.VMEM((2, SEQ, WIDTH), LOW),
        lowered=pltpu.VMEM((2, SEQ, WIDTH), LOW),
        acts=pltpu.VMEM((2, SEQ, WIDTH), LOW),
        dins=pltpu.VMEM((2, SEQ, WIDTH), LOW),
        extra=pltpu.VMEM((2, SEQ, WIDTH), WIDE),
        resid=pltpu.VMEM((2, SEQ, WIDTH), WIDE),
        normed=pltpu.VMEM((2, SEQ, WIDTH), WIDE),
        inverse=pltpu.VMEM((2, SEQ, 128), WIDE),
        normed_rows=pltpu.VMEM((REGIONS, WIDTH), WIDE),
        region_info=pltpu.VMEM((8, WIDTH), WIDE),
        column=pltpu.VMEM((REGIONS, 128), WIDE),
        qkv=pltpu.VMEM((2, SEQ, 3 * WIDTH), LOW),
        probs=pltpu.VMEM((2, PAIRS, 2 * SEQ, SEQ), WIDE),
        mixed=pltpu.VMEM((2, SEQ, WIDTH), LOW),
        dbranch=pltpu.VMEM((2, SEQ, WIDTH), LOW),
        dwide=pltpu.VMEM((2, SEQ, FF), LOW),
        act=pltpu.VMEM((2, SEQ, FF), LOW),
        slope=pltpu.VMEM((2, SEQ, FF), WIDE),
        dweight=pltpu.VMEM((2, WIDTH, WIDTH), WIDE),
        send=DMA((2, 2)),
        recv=DMA((2, 2)),
    )


def unpack_proj(full_ref, proj_ref, half):
    def run(depth, _):
        rows = pl.ds(pl.multiple_of((half * 4 + depth) * 96, 96), 96)
        for block in range(2):
            value = full_ref[block, half, depth].astype(WIDE).reshape(12, 2, 8, WIDTH)
            for side in range(2):
                proj_ref[2 * side + block, rows] = value[:, side].reshape(96, WIDTH).astype(LOW)
        return 0

    lax.fori_loop(0, 4, run, 0)


class Chain:
    def __init__(self, args, full_ref, counts, outs, grads, s, await_down, send_down, send_proj):
        self.await_down, self.send_down, self.send_proj = await_down, send_down, send_proj
        self.args, self.full, self.outs, self.grads, self.s = args, full_ref, outs, grads, s
        self.pipe = lax.axis_index("pipe")
        self.attention = lax.rem(self.pipe, 2) == 0
        self.region_statistics(counts)
        self.each(self.region_terms)

    def region_statistics(self, counts):
        table_ref, s = self.args["table"], self.s
        column = jnp.transpose(jnp.broadcast_to(counts[0:1], (SEQ, REGIONS)))
        s["column"][...] = column
        for index in range(WIDTH // 128):
            lanes = cols(index, 128)
            table = table_ref[:, lanes].astype(WIDE)
            mean = jnp.sum(table * column, 0, keepdims=True) / TOKENS
            second = jnp.sum(table * table * column, 0, keepdims=True) / TOKENS
            inverse = lax.rsqrt(second - mean * mean + EPSILON)
            s["normed_rows"][:, lanes] = (table - mean) * inverse
            s["region_info"][0:1, lanes] = mean
            s["region_info"][1:2, lanes] = inverse
            s["region_info"][2:3, lanes] = inverse * self.args["bn_gain"][0:1, lanes]

    def region_terms(self, micro):
        embedded = dot_tn(self.marks(micro), self.args["table"][...])
        info = self.s["region_info"]
        self.s["extra"][micro] = (embedded - info[0:1]) * info[2:3] + self.args["bn_bias"][...]

    def marks(self, micro):
        ids = self.args["region_ids"][pl.ds(micro, 1), :]
        rank = lax.broadcasted_iota(jnp.int32, (REGIONS, SEQ), 0)
        return jnp.where(rank == ids, 1.0, 0.0).astype(LOW)

    def same_document(self, micro):
        ids = jnp.broadcast_to(self.args["doc_ids"][pl.ds(micro, 1), :].astype(WIDE), (SEQ, SEQ))
        same = jnp.where(ids == jnp.transpose(ids), 1.0, 0.0)
        return jnp.concatenate([same, same], 0) > 0.5

    def down(self, index):
        return self.full[2 + index // 2, index % 2].reshape(WIDTH, WIDTH)

    def turned_proj(self, index):
        return self.full[index // 2, index % 2].reshape(WIDTH, WIDTH)

    def turned_down(self, index):
        return self.grads[index // 2, index % 2].reshape(WIDTH, WIDTH)

    def turn_proj(self):
        for index in range(CHUNKS):
            turned = jnp.transpose(self.s["proj"][index])
            self.full[index // 2, index % 2] = turned.reshape(4, 4, ROWS, WIDTH)

    def turn_down(self):
        for index in range(CHUNKS):
            turned = jnp.transpose(self.down(index))
            self.grads[index // 2, index % 2] = turned.reshape(4, 4, ROWS, WIDTH)

    def hop(self, direction, micro):
        names = ("acts", "fin") if direction == 0 else ("dins", "bin")
        source, target = self.s[names[0]], self.s[names[1]]
        return pltpu.make_async_remote_copy(
            src_ref=source.at[micro], dst_ref=target.at[micro],
            send_sem=self.s["send"].at[direction, micro], recv_sem=self.s["recv"].at[direction, micro],
            device_id={"pipe": lax.rem(self.pipe + 1 + 2 * direction, 4)}, device_id_type=MESH,
        )

    def forward(self, micro):
        s, args = self.s, self.args

        @pl.when(self.pipe == 0)
        def _():
            s["fin"][micro] = args["tokens"][micro]

        @pl.when(self.pipe > 0)
        def _():
            self.hop(0, micro).wait_recv()

        summed = s["fin"][micro].astype(WIDE) + s["extra"][micro]
        lowered = summed.astype(LOW)
        s["lowered"][micro] = lowered
        s["resid"][micro] = summed

        @pl.when(self.attention)
        def _():
            self.attention_forward(micro, lowered)

        @pl.when(jnp.logical_not(self.attention))
        def _():
            self.feed_forward(micro, lowered)

        residual = s["resid"][micro]
        centered = residual - row_mean(residual)
        inverse = lax.rsqrt(row_mean(centered * centered) + EPSILON)
        normed = centered * inverse
        s["normed"][micro] = normed
        s["inverse"][micro] = jnp.broadcast_to(inverse, (SEQ, 128))
        s["acts"][micro] = (normed * args["ln_gain"][...] + args["ln_bias"][...]).astype(LOW)

        @pl.when(self.pipe < 3)
        def _():
            self.hop(0, micro).start()

    def attention_forward(self, micro, lowered):
        s = self.s
        for index in range(3):
            s["qkv"][micro, :, cols(index)] = dot(lowered, s["proj"][index]).astype(LOW)
        same = self.same_document(micro)
        scores, probs, mixed = [], [], []
        for pair in range(PAIRS):
            queries = two_heads(s["qkv"][micro, :, cols(pair, 128)])
            scores.append(dot_nt(queries, s["qkv"][micro, :, cols(PAIRS + pair, 128)]))
        scores = [jnp.where(same, score * 0.125, -1e30) for score in scores]
        tops = [jnp.max(score, -1, keepdims=True) for score in scores]
        powers = [jnp.exp(score - top) for score, top in zip(scores, tops)]
        totals = [jnp.sum(power, -1, keepdims=True) for power in powers]
        for pair in range(PAIRS):
            probs.append(powers[pair] / totals[pair])
            s["probs"][micro, pair] = probs[pair]
        for pair in range(PAIRS):
            values = two_heads(s["qkv"][micro, :, cols(2 * PAIRS + pair, 128)])
            mixed.append(dot(side_by_side(probs[pair].astype(LOW)), values))
        for pair in range(PAIRS):
            s["mixed"][micro, :, cols(pair, 128)] = mixed[pair].astype(LOW)
        s["resid"][micro] = s["resid"][micro] + dot(s["mixed"][micro], s["proj"][3])

    def feed_forward(self, micro, lowered):
        s = self.s
        branch = s["resid"][micro]
        for index in range(CHUNKS):
            hidden = dot(lowered, s["proj"][index])
            cumulative = 0.5 * (1.0 + lax.erf(hidden * (0.5 ** 0.5)))
            density = jnp.exp(hidden * hidden * -0.5) * 0.3989422804014327
            s["act"][micro, :, cols(index)] = (hidden * cumulative).astype(LOW)
            s["slope"][micro, :, cols(index)] = cumulative + hidden * density

        @pl.when((micro == 0) & (self.pipe == 1))
        def _():
            self.await_down()

        for index in range(CHUNKS):
            branch = branch + dot(s["act"][micro, :, cols(index)], self.down(index))
        s["resid"][micro] = branch

    def backward(self, micro):
        s, args = self.s, self.args

        @pl.when(self.pipe == 3)
        def _():
            s["bin"][micro] = args["out_cot"][micro]

        @pl.when(self.pipe < 3)
        def _():
            self.hop(1, micro).wait_recv()

        gout = s["bin"][micro].astype(WIDE)
        normed = s["normed"][micro]
        dnormed = gout * args["ln_gain"][...]
        dres = s["inverse"][micro][:, 0:1] * (
            dnormed - row_mean(dnormed) - normed * row_mean(dnormed * normed)
        )
        s["resid"][micro] = dres
        s["dbranch"][micro] = dres.astype(LOW)

        @pl.when(self.attention)
        def _():
            self.attention_backward(micro)

        @pl.when((self.pipe == 0) & (micro == 1))
        def _():
            self.send_proj(self)

        @pl.when(self.attention)
        def _():
            total = s["resid"][micro]
            for index in range(3):
                total = total + dot(s["dwide"][micro, :, cols(index)], self.turned_proj(index))
            self.input_gradient(micro, total)

        @pl.when((self.pipe == 1) & (micro == 1))
        def _():
            self.send_down(self)

        @pl.when(jnp.logical_not(self.attention))
        def _():
            self.hidden_gradient(micro)

        @pl.when((self.pipe == 1) & (micro == 1))
        def _():
            self.send_proj(self)

        @pl.when(jnp.logical_not(self.attention))
        def _():
            total = s["resid"][micro]
            for index in range(CHUNKS):
                total = total + dot(s["dwide"][micro, :, cols(index)], self.turned_proj(index))
            self.input_gradient(micro, total)

        @pl.when(self.pipe > 0)
        def _():
            self.hop(1, micro).start()

    def sums(self, micro):
        s = self.s
        stats = self.outs["stats"]
        gout = s["bin"][micro].astype(WIDE)
        stats[2:3] = stats[2:3] + jnp.sum(gout * s["normed"][micro], 0, keepdims=True)
        stats[3:4] = stats[3:4] + jnp.sum(gout, 0, keepdims=True)
        marks = self.marks(micro)
        dsum = s["resid"][micro]
        high = s["dins"][micro]
        rest = (dsum - high.astype(WIDE)).astype(LOW)
        region = self.outs["region"]
        added = dot(marks, high) + dot(marks, rest)
        region[0, 0] = region[0, 0] + added.reshape(4, 4, 8, WIDTH)

    def input_gradient(self, micro, dsum):
        self.s["resid"][micro] = dsum
        self.s["dins"][micro] = dsum.astype(LOW)

    def attention_backward(self, micro):
        s, pairs = self.s, range(PAIRS)
        dmixed = dot(s["dbranch"][micro], self.turned_proj(3)).astype(LOW)
        pieces = [[s["qkv"][micro, :, cols(part * PAIRS + pair, 128)] for part in range(3)] for pair in pairs]
        grads = [two_heads(dmixed[:, cols(pair, 128)]) for pair in pairs]
        dprobs = [dot_nt(grads[pair], pieces[pair][2]) for pair in pairs]
        probs = [s["probs"][micro, pair] for pair in pairs]
        dvalues = [dot_tn(probs[pair].astype(LOW), grads[pair]) for pair in pairs]
        sums = [jnp.sum(dprobs[pair] * probs[pair], -1, keepdims=True) for pair in pairs]
        dscores = [(probs[pair] * (dprobs[pair] - sums[pair])).astype(LOW) for pair in pairs]
        dkeys = [dot_tn(dscores[pair], two_heads(pieces[pair][0])) * 0.125 for pair in pairs]
        dqueries = [dot(side_by_side(dscores[pair]), two_heads(pieces[pair][1])) * 0.125 for pair in pairs]
        for pair in pairs:
            for part, value in enumerate((dqueries[pair], dkeys[pair], dvalues[pair])):
                s["dwide"][micro, :, cols(part * PAIRS + pair, 128)] = value.astype(LOW)

    def hidden_gradient(self, micro):
        s = self.s
        dbranch = s["dbranch"][micro]
        for index in range(CHUNKS):
            dact = dot(dbranch, self.turned_down(index))
            s["dwide"][micro, :, cols(index)] = (dact * s["slope"][micro, :, cols(index)]).astype(LOW)

    def weight_gradients(self, block):
        s = self.s
        lowered = s["lowered"][...].reshape(2 * SEQ, WIDTH)
        for side in range(2):
            quarter = 2 * side + block
            if quarter == 3:
                @pl.when(self.attention)
                def _():
                    left = s["mixed"][...].reshape(2 * SEQ, WIDTH)
                    s["dweight"][1] = dot_tn(left, s["dbranch"][...].reshape(2 * SEQ, WIDTH))

                @pl.when(jnp.logical_not(self.attention))
                def _():
                    right = s["dwide"][:, :, cols(3)].reshape(2 * SEQ, WIDTH)
                    s["dweight"][1] = dot_tn(lowered, right)
            else:
                right = s["dwide"][:, :, cols(quarter)].reshape(2 * SEQ, WIDTH)
                s["dweight"][side] = dot_tn(lowered, right)

        def run(index, _):
            half, depth = lax.div(index, 4), lax.rem(index, 4)
            rows = pl.ds(pl.multiple_of(index * 96, 96), 96)
            sides = [s["dweight"][side, rows].reshape(12, 1, 8, WIDTH) for side in range(2)]
            value = jnp.concatenate(sides, 1).reshape(4, ROWS, WIDTH)
            self.grads[block, half, depth] = value.astype(LOW)
            return 0

        lax.fori_loop(0, 8, run, 0)

    def down_gradients(self, block):
        s = self.s
        dbranch = s["dbranch"][...].reshape(2 * SEQ, WIDTH)
        for half in range(2):
            act = s["act"][:, :, cols(2 * (block - 2) + half)].reshape(2 * SEQ, WIDTH)
            self.grads[block, half] = dot_tn(act, dbranch).astype(LOW).reshape(4, 4, ROWS, WIDTH)

    def table_gradient(self, table_sum, stats):
        s = self.s
        group = lax.axis_index("dp")
        rows = pl.ds(pl.multiple_of(lax.rem(group, 16) * 8, 8), 8)
        counts = jnp.concatenate([s["column"][rows]] * (WIDTH // 128), 1)
        mean = stats[0:1] / TOKENS + s["normed_rows"][rows] * (stats[1:2] / TOKENS)
        grad = s["region_info"][2:3] * (table_sum - counts * mean)
        return jnp.where(group < 16, grad, 0.0)

    def start_stats(self):
        self.outs["stats"][...] = jnp.zeros((8, WIDTH), WIDE)
        self.outs["region"][...] = jnp.zeros((1, 1, 4, 4, 8, WIDTH), WIDE)

    def end_stats(self):
        region, stats = self.outs["region"][0, 0].reshape(REGIONS, WIDTH), self.outs["stats"]
        stats[0:1] = jnp.sum(region, 0, keepdims=True)
        stats[1:2] = jnp.sum(region * self.s["normed_rows"][...], 0, keepdims=True)

    def each(self, action):
        lax.fori_loop(0, 2, lambda micro, _: (action(micro), 0)[1], 0)

    def finish(self):
        def run(micro):
            @pl.when(self.pipe < 3)
            def _():
                self.hop(0, micro).wait_send()

            @pl.when(self.pipe > 0)
            def _():
                self.hop(1, micro).wait_send()

        self.each(run)


ARGS = ("tokens", "doc_ids", "region_ids", "ln_gain", "ln_bias", "bn_gain", "bn_bias", "table", "out_cot")
def pack_proj(proj_ref, gather):
    for block in range(2):
        parts = []
        for turn in range(3):
            rows = slice(8 * turn, 8 * turn + 8)
            for side in range(2):
                parts.append(proj_ref[0, rows, cols(2 * side + block)].astype(WIDE))
        gather.own(block)[...] = jnp.concatenate(parts, 0).astype(LOW)


def own_counts(region_ids_ref):
    rank = lax.broadcasted_iota(jnp.int32, (REGIONS, SEQ), 0)
    total = jnp.zeros((8, REGIONS), WIDE)
    for micro in range(2):
        marks = jnp.where(rank == region_ids_ref[micro : micro + 1, :], 1.0, 0.0).astype(LOW)
        total = total + dot_nt(jnp.ones((8, SEQ), LOW), marks)
    return total


FAR = ("region_ids", "proj", "down", "table", "bn_gain", "bn_bias", "doc_ids", "ln_gain", "ln_bias", "tokens", "out_cot")


def whole_kernel(*refs):
    refs = list(refs)

    def take(count):
        taken = refs[:count]
        del refs[:count]
        return taken

    given = dict(zip(ARGS + ("proj", "down"), take(len(ARGS) + 2)))
    acts_out, dins_out, proj_out, down_out, table_out, shares_out = take(6)
    local_sem, cross_send, cross_recv = take(3)
    s = dict(zip(chain_scratch(), take(len(chain_scratch()))))
    near = dict(zip(FAR, take(len(FAR))))
    full = take(1)[0]
    gather = Gather(full, take(4), take(4))
    counted = Total(*take(5))
    held, region_held, stats = take(3)
    main = Scatter(held, take(4), take(4), take(4))
    region = Scatter(region_held, take(4), take(4), take(4), single=True)
    total = Total(*take(5))

    pipe, half = gather.pipe, gather.half
    ffn = lax.rem(pipe, 2) == 1
    pairs = lax.rem(pipe, 2) + 1
    sibling = pipe + 1 - 2 * lax.rem(pipe, 2)
    fetches = [
        pltpu.make_async_copy(
            given[name].at[:REGIONS] if name == "table" else given[name], near[name], local_sem.at[index]
        )
        for index, name in enumerate(FAR)
    ]
    for fetch in fetches:
        fetch.start()
    others = all_dp_devices() + [{"pipe": lax.rem(pipe + 1, 4)}, {"pipe": lax.rem(pipe + 3, 4)}]
    greet(others)
    for fetch in fetches[:3]:
        fetch.wait()
    pack_proj(near["proj"], gather)
    gather.own(3)[...] = near["down"][0]
    meet(others)
    for route in range(2):
        gather.start(route, route)
    cross = pltpu.make_async_remote_copy(
        src_ref=gather.own(3), dst_ref=gather.own(2), send_sem=cross_send.at[0], recv_sem=cross_recv.at[0],
        device_id={"pipe": sibling}, device_id_type=MESH,
    )

    @pl.when(jnp.logical_not(ffn))
    def _():
        cross.start()

    @pl.when(ffn)
    def _():
        gather.start(1, 3)
        cross.wait_recv()
        gather.start(0, 2)

    counted.send(0, own_counts(near["region_ids"]))

    def each(action):
        def run(pair, _):
            for route in range(2):
                action(route, 2 * pair + route)
            return 0

        lax.fori_loop(0, pairs, run, 0)

    for index, step in enumerate(gather.steps()):
        each(step)
        if index in (1, 2):
            counted.send(index, counted.receive(index - 1))
    for fetch in fetches[3:]:
        fetch.wait()
    outs = dict(stats=stats, region=region_held)

    def await_down():
        for route in range(2):
            for arriving in range(2):
                gather.last(route, 2 + route, arriving)

    def send_down(chain):
        for route in range(2):
            chain.down_gradients(2 + route)
            main.start(route, 2 + route)

    def send_proj(chain):
        for block in range(2):
            chain.weight_gradients(block)
            main.start(block, block)

    chain = Chain(near, full, counted.receive(2), outs, held, s, await_down, send_down, send_proj)
    chain.start_stats()
    for arriving in (half, 1 - half):
        for route in range(2):
            gather.last(route, route, arriving)
        unpack_proj(full, s["proj"], arriving)

    def turn():
        for route in range(2):
            gather.finish(route, route)
        chain.turn_proj()
        pl.when(pipe == 3)(await_down)
        pl.when(ffn)(chain.turn_down)

    pl.when(pipe >= 2)(turn)

    def tick(index, _):
        back = lax.div(index, 2)
        micro = lax.rem(index, 2)
        pl.when((index == 2) & (pipe < 2))(turn)
        pl.when(back == 0)(lambda: chain.forward(micro))
        pl.when(back == 1)(lambda: chain.backward(micro))
        return 0

    lax.fori_loop(0, 4, tick, 0)
    put_acts = pltpu.make_async_copy(s["acts"], acts_out, local_sem.at[len(FAR)])
    put_dins = pltpu.make_async_copy(s["dins"], dins_out, local_sem.at[len(FAR) + 1])
    put_acts.start()
    put_dins.start()
    pl.when(pipe > 1)(lambda: send_proj(chain))
    chain.each(chain.sums)
    chain.end_stats()
    total.send(0, jnp.concatenate([stats[0:4, : WIDTH // 2], stats[0:4, WIDTH // 2 :]], 0))

    def regions(action):
        for route in range(2):
            pl.when(lax.rem(pipe, 2) == route)(lambda route=route: action(route, 0))

    regions(region.start)

    @pl.when(pipe == 3)
    def _():
        send_down(chain)

    def each_late(action):
        def run(pair, _):
            for route in range(2):
                action(route, 2 * (pairs - 1 - pair) + route)
            return 0

        lax.fori_loop(0, pairs, run, 0)

    for index, (step, region_step) in enumerate(zip(main.steps(), region.steps())):
        each_late(step)
        regions(region_step)
        if index in (1, 2):
            total.send(index, total.receive(index - 1))
    back = pltpu.make_async_remote_copy(
        src_ref=main.own(2), dst_ref=down_out, send_sem=cross_send.at[1], recv_sem=cross_recv.at[1],
        device_id={"pipe": sibling}, device_id_type=MESH,
    )

    @pl.when(ffn)
    def _():
        back.start()
        down_out[...] = main.own(3)[...]

    for block in range(2):
        proj_out[block] = main.own(block)[...]
    summed = total.receive(2)
    summed = jnp.concatenate([summed[0:4], summed[4:8]], 1)
    summed = jnp.concatenate([summed, summed], 0)
    table_out[...] = chain.table_gradient(region_held[0, 0, main.depth, main.column], summed)
    shift = lax.rem(WIDTH - 24 * gather.group, WIDTH)
    shares_out[...] = pltpu.roll(summed, shift, 1)[:, :128]

    @pl.when(ffn)
    def _():
        for route in range(2):
            gather.finish(route, 2 + route)

    each(main.finish)
    regions(region.finish)
    counted.finish()
    total.finish()
    chain.finish()
    put_acts.wait()
    put_dins.wait()

    @pl.when(ffn)
    def _():
        back.wait_send()

    @pl.when(jnp.logical_not(ffn))
    def _():
        cross.wait_send()
        back.wait_recv()


def run_whole(args, proj, down):
    micro = (2, SEQ, WIDTH)
    vmem, far = pl.BlockSpec(memory_space=pltpu.VMEM), pl.BlockSpec(memory_space=pl.ANY)
    out_shape = [
        jax.ShapeDtypeStruct(micro, LOW),
        jax.ShapeDtypeStruct(micro, LOW),
        jax.ShapeDtypeStruct((2, ROWS, WIDTH), LOW),
        jax.ShapeDtypeStruct((ROWS, WIDTH), LOW),
        jax.ShapeDtypeStruct((8, WIDTH), WIDE),
        jax.ShapeDtypeStruct((8, 128), WIDE),
    ]
    blocks = (BLOCKS, 2, 4, 4, ROWS, WIDTH)
    given = dict(args, proj=proj, down=down)
    scratch = [DMA((len(FAR) + 2,)), DMA((2,)), DMA((2,))]
    scratch += list(chain_scratch().values())
    scratch += [
        pltpu.VMEM((REGIONS, WIDTH) if name == "table" else given[name].shape, given[name].dtype)
        for name in FAR
    ]
    scratch += [pltpu.VMEM(blocks, LOW)] + gather_sems() + gather_sems()
    scratch += total_scratch((8, REGIONS))
    scratch += [pltpu.VMEM(blocks, LOW), pltpu.VMEM((1, 1, 4, 4, 8, WIDTH), WIDE), pltpu.VMEM((8, WIDTH), WIDE)]
    scratch += scatter_buffers(BLOCKS, ROWS, LOW) + scatter_sems(BLOCKS) + scatter_sems(BLOCKS)
    scratch += scatter_buffers(1, 8, WIDE) + scatter_sems(1) + scatter_sems(1)
    scratch += total_scratch((8, WIDTH // 2))
    return pl.pallas_call(
        whole_kernel,
        out_shape=out_shape,
        in_specs=[far] * len(given),
        out_specs=[far] * 2 + [vmem] * (len(out_shape) - 2),
        scratch_shapes=scratch,
        compiler_params=pltpu.CompilerParams(
            collective_id=0, has_side_effects=True, vmem_limit_bytes=62 * 2**20
        ),
    )(*[args[name] for name in ARGS], proj, down)


def finish_kernel(acts, dins, proj, down, table, shares, *outs):
    outs[0][...] = acts[...].reshape(1, 2 * SEQ, WIDTH)
    outs[1][...] = dins[...].reshape(1, 2 * SEQ, WIDTH)
    for block in range(2):
        rows = proj[block].astype(WIDE)
        for turn in range(3):
            for side in range(2):
                start = 16 * turn + 8 * side
                outs[2][0, 8 * turn : 8 * turn + 8, cols(2 * side + block)] = rows[start : start + 8]
    outs[3][0] = down[...].astype(WIDE)
    for out, row in zip(outs[4:8], (2, 3, 1, 0)):
        out[...] = shares[row : row + 1, :24]
    outs[8][0] = table[...]


def finish(*arrays):
    vmem = pl.BlockSpec(memory_space=pltpu.VMEM)
    share = jax.ShapeDtypeStruct((1, 24), WIDE)
    out_shape = [
        jax.ShapeDtypeStruct((1, 2 * SEQ, WIDTH), LOW),
        jax.ShapeDtypeStruct((1, 2 * SEQ, WIDTH), LOW),
        jax.ShapeDtypeStruct((1, 24, FF), WIDE),
        jax.ShapeDtypeStruct((1, ROWS, WIDTH), WIDE),
        share, share, share, share,
        jax.ShapeDtypeStruct((1, 8, WIDTH), WIDE),
    ]
    return pl.pallas_call(
        finish_kernel, out_shape=out_shape, in_specs=[vmem] * 6, out_specs=[vmem] * 9,
        compiler_params=pltpu.CompilerParams(vmem_limit_bytes=62 * 2**20),
    )(*arrays)


def body(
    tokens, doc_ids, region_ids, proj, down, ln_gain, ln_bias, bn_gain, bn_bias, region_table, out_cot
):
    args = dict(
        tokens=tokens.reshape(2, SEQ, WIDTH), doc_ids=doc_ids, region_ids=region_ids, ln_gain=ln_gain,
        ln_bias=ln_bias, bn_gain=bn_gain, bn_bias=bn_bias, table=region_table[0],
        out_cot=out_cot.reshape(2, SEQ, WIDTH),
    )
    return tuple(finish(*run_whole(args, proj, down)))


def solution(mesh):
    in_specs = (
        P("dp", None),
        P("dp", None),
        P("dp", None),
        P("pipe", "dp", None),
        P("pipe", "dp", None),
        P("pipe", None),
        P("pipe", None),
        P("pipe", None),
        P("pipe", None),
        P("pipe", None, None),
        P("dp", None),
    )
    out_specs = (
        P("pipe", "dp", None),
        P("pipe", "dp", None),
        P("pipe", "dp", None),
        P("pipe", "dp", None),
        P("pipe", "dp"),
        P("pipe", "dp"),
        P("pipe", "dp"),
        P("pipe", "dp"),
        P("pipe", "dp", None),
    )
    return jax.shard_map(body, mesh=mesh, in_specs=in_specs, out_specs=out_specs, check_vma=False)
```

```python
from functools import partial

import jax
import jax.numpy as jnp
from jax import lax
from jax.experimental import pallas as pl
from jax.experimental.pallas import tpu as pltpu
from jax.sharding import PartitionSpec as P

HEADS = 12
FF = 3072
EPSILON = 1e-05
LOW = jnp.bfloat16
WIDE = jnp.float32
MESH = pl.DeviceIdType.MESH
DMA = pltpu.SemaphoreType.DMA
BLOCKS = 4
ROWS = 48
WIDTH = 768


def place():
    group = lax.axis_index("dp")
    pipe = lax.axis_index("pipe")
    half = lax.div(group, 16)
    rest = lax.rem(group, 16)
    return group, pipe, half, lax.div(rest, 4), lax.rem(rest, 4)


def around(position, distance):
    return lax.rem(position + distance + 4, 4)


def group_of(half, depth, column):
    return half * 16 + depth * 4 + column


def along(route, first, second):
    return (second, first) if route == 0 else (first, second)


def to_group(src, dst, send, recv, group):
    return pltpu.make_async_remote_copy(
        src_ref=src,
        dst_ref=dst,
        send_sem=send,
        recv_sem=recv,
        device_id={"dp": group},
        device_id_type=MESH,
    )


def arrived(dst, recv):
    pltpu.make_async_copy(dst, dst, recv).wait()


def narrow(ref, route, block, half, first, second):
    depth, column = along(route, first, second)
    return ref.at[block, half, depth, column]


def wide(ref, route, block, half, second):
    if route == 0:
        return ref.at[block, half, second]
    return ref.at[block, half, :, second]


def greet(others):
    barrier = pltpu.get_barrier_semaphore()
    for device in others:
        pl.semaphore_signal(barrier, inc=1, device_id=device, device_id_type=MESH)


def meet(others):
    pl.semaphore_wait(pltpu.get_barrier_semaphore(), len(others))


def ring_devices():
    group, pipe, half, depth, column = place()
    return [
        {"dp": group_of(1 - half, depth, column)},
        {"dp": group_of(half, around(depth, 1), column)},
        {"dp": group_of(half, around(depth, -1), column)},
        {"dp": group_of(half, depth, around(column, 1))},
        {"dp": group_of(half, depth, around(column, -1))},
    ]


def gather_sems():
    return [DMA((BLOCKS,)), DMA((BLOCKS, 3)), DMA((BLOCKS, 2, 2)), DMA((BLOCKS, 2, 2))]


def part(ref, way):
    return ref.at[pl.ds(2 * way, 2)]


class Rings:
    def __init__(self, ref, sends, recvs):
        self.ref, self.sends, self.recvs = ref, sends, recvs
        self.group, self.pipe, self.half, self.depth, self.column = place()
        self.partner = group_of(1 - self.half, self.depth, self.column)

    def axes(self, route):
        return (self.column, self.depth) if route == 0 else (self.depth, self.column)

    def small_peer(self, route, distance):
        if route == 0:
            return group_of(self.half, self.depth, around(self.column, distance))
        return group_of(self.half, around(self.depth, distance), self.column)

    def large_peer(self, route, distance):
        return self.small_peer(1 - route, distance)

    def own(self, block):
        return self.ref.at[block, self.half, self.depth, self.column]

    def send(self, kind, index, src, dst, group):
        return to_group(src, dst, self.sends[kind].at[index], self.recvs[kind].at[index], group)


class Gather(Rings):
    def swap(self, route, block, half, position=None):
        second = self.axes(route)[1]
        slot = wide(self.ref, route, block, half, second)
        if position is not None:
            slot = narrow(self.ref, route, block, half, position, second)
        return self.send(0, (block,), slot, slot, self.partner)

    def small(self, route, block, distance):
        slot = self.own(block)
        return self.send(1, (block, distance - 1), slot, slot, self.small_peer(route, distance))

    def large(self, route, block, half, way, position=None):
        second = self.axes(route)[1]
        slot = wide(self.ref, route, block, half, second)
        if position is not None:
            slot = narrow(self.ref, route, block, half, position, second)
        return self.send(2, (block, half, way), slot, slot, self.large_peer(route, 1 - 2 * way))

    def large_relay(self, route, block, half, way):
        second = self.axes(route)[1]
        distance = 1 - 2 * way
        slot = part(wide(self.ref, route, block, half, around(second, -distance)), way)
        return self.send(3, (block, half, way), slot, slot, self.large_peer(route, distance))

    def pass_on(self, route, block, position):
        for way in range(2):
            self.large(route, block, self.half, way, position).start()
        self.swap(route, block, self.half, position).start()

    def start(self, route, block):
        for distance in range(1, 4):
            self.small(route, block, distance).start()
        self.pass_on(route, block, self.axes(route)[0])

    def end_small(self, route, block):
        for distance in (1, 3, 2):
            self.small(route, block, distance).wait_recv()
            self.pass_on(route, block, around(self.axes(route)[0], -distance))

    def relay_large(self, route, block, half):
        for way in range(2):
            self.large(route, block, half, way).wait_recv()
            self.large_relay(route, block, half, way).start()

    def swap_in(self, route, block):
        self.swap(route, block, 1 - self.half).wait_recv()
        for way in range(2):
            self.large(route, block, 1 - self.half, way).start()

    def last(self, route, block, half):
        for way in range(2):
            self.large_relay(route, block, half, way).wait_recv()

    def steps(self):
        return [
            self.end_small,
            lambda route, block: self.relay_large(route, block, self.half),
            self.swap_in,
            lambda route, block: self.relay_large(route, block, 1 - self.half),
        ]

    def finish(self, route, block):
        self.swap(route, block, self.half).wait_send()
        for distance in range(1, 4):
            self.small(route, block, distance).wait_send()
        for half in range(2):
            for way in range(2):
                self.large(route, block, half, way).wait_send()
                self.large_relay(route, block, half, way).wait_send()


def scatter_buffers(blocks, rows, dtype):
    return [
        pltpu.VMEM((blocks, 2, 4, rows, WIDTH), dtype),
        pltpu.VMEM((blocks, 2, 2, 4, rows, WIDTH), dtype),
        pltpu.VMEM((blocks, 4, rows, WIDTH), dtype),
        pltpu.VMEM((blocks, 3, rows, WIDTH), dtype),
    ]


def scatter_sems(blocks):
    return [DMA((blocks, 2, 2)), DMA((blocks, 2, 2)), DMA((blocks,)), DMA((blocks, 3))]


def accumulate(target, others):
    total = target[...].astype(WIDE)
    for other in others:
        total = total + other[...].astype(WIDE)
    target[...] = total.astype(target.dtype)


class Scatter(Rings):
    def __init__(self, ref, buffers, sends, recvs, single=False):
        super().__init__(ref, sends, recvs)
        self.buffers, self.single = buffers, single

    def large_early(self, route, block, half, way):
        second = self.axes(route)[1]
        return self.send(
            0, (block, half, way), part(wide(self.ref, route, block, half, around(second, 2)), way),
            part(self.buffers[0].at[block, half], way), self.large_peer(route, 1 - 2 * way),
        )

    def large(self, route, block, half, way, side=None):
        second = self.axes(route)[1]
        distance = 1 - 2 * way
        src = wide(self.ref, route, block, half, around(second, distance))
        dst = self.buffers[1].at[block, way, half]
        if side is not None:
            src, dst = part(src, side), part(dst, side)
        return self.send(1, (block, way, half), src, dst, self.large_peer(route, distance))

    def swap(self, route, block, half):
        second = self.axes(route)[1]
        return self.send(
            2, (block,), wide(self.ref, route, block, half, second), self.buffers[2].at[block], self.partner
        )

    def target(self, route, block, distance):
        first, second = self.axes(route)
        half = 0 if self.single else self.half
        return narrow(self.ref, route, block, half, around(first, distance), second)

    def small(self, route, block, distance):
        return self.send(
            3, (block, distance - 1), self.target(route, block, distance), self.buffers[3].at[block, distance - 1],
            self.small_peer(route, distance),
        )

    def where(self, half, action):
        if self.single:
            pl.when(half == 0)(lambda: action(0))
        else:
            action(half)

    def begin(self, route, block, half):
        def run(half):
            for way in range(2):
                self.large_early(route, block, half, way).start()
                self.large(route, block, half, way, 1 - way).start()

        self.where(half, run)

    def middle(self, route, block, half):
        def run(half):
            second = self.axes(route)[1]
            for way in range(2):
                self.large_early(route, block, half, way).wait_recv()
                accumulate(
                    part(wide(self.ref, route, block, half, around(second, 1 - 2 * way)), way),
                    [part(self.buffers[0].at[block, half], way)],
                )
                self.large(route, block, half, way, way).start()

        self.where(half, run)

    def sum_large(self, route, block, half, others):
        for way in range(2):
            self.large(route, block, half, way).wait_recv()
        arrivals = [self.buffers[1].at[block, way, half] for way in range(2)]
        accumulate(wide(self.ref, route, block, half, self.axes(route)[1]), arrivals + others)

    def start(self, route, block):
        self.begin(route, block, 1 - self.half)

    def turn(self, route, block):
        self.middle(route, block, 1 - self.half)
        self.begin(route, block, self.half)

    def sum_other(self, route, block):
        def run(half):
            self.sum_large(route, block, half, [])
            self.swap(route, block, half).start()

        self.where(1 - self.half, run)

    def swap_begin(self, route, block):
        self.sum_other(route, block)
        self.begin(route, block, self.half)

    def sum_own(self, route, block):
        def run(half):
            self.swap(route, block, half).wait_recv()
            self.sum_large(route, block, half, [self.buffers[2].at[block]])
            for distance in range(1, 4):
                self.small(route, block, distance).start()

        self.where(self.half, run)

    def last(self, route, block):
        def run(half):
            for distance in range(1, 4):
                self.small(route, block, distance).wait_recv()
            arrivals = [self.buffers[3].at[block, index] for index in range(3)]
            accumulate(self.target(route, block, 0), arrivals)

        self.where(self.half, run)

    def steps(self):
        return [
            lambda route, block: self.middle(route, block, 1 - self.half),
            self.swap_begin,
            lambda route, block: self.middle(route, block, self.half),
            self.sum_own,
            self.last,
        ]

    def finish(self, route, block):
        def large(half):
            for way in range(2):
                self.large_early(route, block, half, way).wait_send()
                self.large(route, block, half, way).wait_send()

        def other(half):
            large(half)
            self.swap(route, block, half).wait_send()

        def own(half):
            large(half)
            for distance in range(1, 4):
                self.small(route, block, distance).wait_send()

        self.where(1 - self.half, other)
        self.where(self.half, own)


class Total:
    def __init__(self, first, second, third, sends, recvs):
        self.stages, self.sends, self.recvs = (first, second, third), sends, recvs
        self.group, self.pipe, self.half, self.depth, self.column = place()
        self.where = (self.column, self.depth, self.half)

    def copy(self, stage, distance):
        here, buffer = self.where[stage], self.stages[stage]
        if stage == 0:
            peer = group_of(self.half, self.depth, around(here, distance))
        elif stage == 1:
            peer = group_of(self.half, around(here, distance), self.column)
        else:
            peer = group_of(1 - here, self.depth, self.column)
        return to_group(
            buffer.at[here], buffer.at[here],
            self.sends.at[stage, distance - 1], self.recvs.at[stage, distance - 1], peer,
        )

    def distances(self, stage):
        return range(1, 4) if stage < 2 else range(1, 2)

    def send(self, stage, value):
        self.stages[stage][self.where[stage]] = value
        for distance in self.distances(stage):
            self.copy(stage, distance).start()

    def receive(self, stage):
        for distance in self.distances(stage):
            self.copy(stage, distance).wait_recv()
        total = self.stages[stage][0]
        for index in range(1, 4 if stage < 2 else 2):
            total = total + self.stages[stage][index]
        return total

    def finish(self):
        for stage in range(3):
            for distance in self.distances(stage):
                self.copy(stage, distance).wait_send()


def total_scratch(shape):
    return [
        pltpu.VMEM((4,) + shape, WIDE),
        pltpu.VMEM((4,) + shape, WIDE),
        pltpu.VMEM((2,) + shape, WIDE),
        DMA((3, 3)),
        DMA((3, 3)),
    ]


def all_dp_devices():
    group, pipe, half, depth, column = place()
    return ring_devices() + [
        {"dp": group_of(half, around(depth, 2), column)},
        {"dp": group_of(half, depth, around(column, 2))},
    ]


PAIRS = HEADS // 2
SEQ = 128
REGIONS = 128
TOKENS = 8192
CHUNKS = 4


def dot(left, right):
    return lax.dot_general(left, right, (((1,), (0,)), ((), ())), preferred_element_type=WIDE)


def dot_nt(left, right):
    return lax.dot_general(left, right, (((1,), (1,)), ((), ())), preferred_element_type=WIDE)


def dot_tn(left, right):
    return lax.dot_general(left, right, (((0,), (0,)), ((), ())), preferred_element_type=WIDE)


def cols(index, width=WIDTH):
    return slice(index * width, (index + 1) * width)


def two_heads(pair):
    lane = lax.broadcasted_iota(jnp.int32, pair.shape, 1)
    zero = jnp.zeros_like(pair)
    return jnp.concatenate([jnp.where(lane < 64, pair, zero), jnp.where(lane < 64, zero, pair)], 0)


def side_by_side(stacked):
    return jnp.concatenate([stacked[:SEQ], stacked[SEQ:]], 1)


def row_mean(value):
    return jnp.mean(value, -1, keepdims=True)


def chain_scratch():
    return dict(
        proj=pltpu.VMEM((CHUNKS, WIDTH, WIDTH), LOW),
        fin=pltpu.VMEM((2, SEQ, WIDTH), LOW),
        bin=pltpu.VMEM((2, SEQ, WIDTH), LOW),
        lowered=pltpu.VMEM((2, SEQ, WIDTH), LOW),
        acts=pltpu.VMEM((2, SEQ, WIDTH), LOW),
        dins=pltpu.VMEM((2, SEQ, WIDTH), LOW),
        extra=pltpu.VMEM((2, SEQ, WIDTH), WIDE),
        resid=pltpu.VMEM((2, SEQ, WIDTH), WIDE),
        normed=pltpu.VMEM((2, SEQ, WIDTH), WIDE),
        inverse=pltpu.VMEM((2, SEQ, 128), WIDE),
        normed_rows=pltpu.VMEM((REGIONS, WIDTH), WIDE),
        region_info=pltpu.VMEM((8, WIDTH), WIDE),
        column=pltpu.VMEM((REGIONS, 128), WIDE),
        qkv=pltpu.VMEM((2, SEQ, 3 * WIDTH), LOW),
        probs=pltpu.VMEM((2, PAIRS, 2 * SEQ, SEQ), WIDE),
        mixed=pltpu.VMEM((2, SEQ, WIDTH), LOW),
        dbranch=pltpu.VMEM((2, SEQ, WIDTH), LOW),
        dwide=pltpu.VMEM((2, SEQ, FF), LOW),
        act=pltpu.VMEM((2, SEQ, FF), LOW),
        slope=pltpu.VMEM((2, SEQ, FF), WIDE),
        dweight=pltpu.VMEM((2, WIDTH, WIDTH), WIDE),
        send=DMA((2, 2)),
        recv=DMA((2, 2)),
    )


def unpack_proj(full_ref, proj_ref, half):
    def run(depth, _):
        rows = pl.ds(pl.multiple_of((half * 4 + depth) * 96, 96), 96)
        for block in range(2):
            value = full_ref[block, half, depth].astype(WIDE).reshape(12, 2, 8, WIDTH)
            for side in range(2):
                proj_ref[2 * side + block, rows] = value[:, side].reshape(96, WIDTH).astype(LOW)
        return 0

    lax.fori_loop(0, 4, run, 0)


class Chain:
    def __init__(self, args, full_ref, counts, outs, grads, s, await_down, send_down, send_proj):
        self.await_down, self.send_down, self.send_proj = await_down, send_down, send_proj
        self.args, self.full, self.outs, self.grads, self.s = args, full_ref, outs, grads, s
        self.pipe = lax.axis_index("pipe")
        self.attention = lax.rem(self.pipe, 2) == 0
        self.region_statistics(counts)
        self.each(self.region_terms)

    def region_statistics(self, counts):
        table_ref, s = self.args["table"], self.s
        column = jnp.transpose(jnp.broadcast_to(counts[0:1], (SEQ, REGIONS)))
        s["column"][...] = column
        for index in range(WIDTH // 128):
            lanes = cols(index, 128)
            table = table_ref[:, lanes].astype(WIDE)
            mean = jnp.sum(table * column, 0, keepdims=True) / TOKENS
            second = jnp.sum(table * table * column, 0, keepdims=True) / TOKENS
            inverse = lax.rsqrt(second - mean * mean + EPSILON)
            s["normed_rows"][:, lanes] = (table - mean) * inverse
            s["region_info"][0:1, lanes] = mean
            s["region_info"][1:2, lanes] = inverse
            s["region_info"][2:3, lanes] = inverse * self.args["bn_gain"][0:1, lanes]

    def region_terms(self, micro):
        embedded = dot_tn(self.marks(micro), self.args["table"][...])
        info = self.s["region_info"]
        self.s["extra"][micro] = (embedded - info[0:1]) * info[2:3] + self.args["bn_bias"][...]

    def marks(self, micro):
        ids = self.args["region_ids"][pl.ds(micro, 1), :]
        rank = lax.broadcasted_iota(jnp.int32, (REGIONS, SEQ), 0)
        return jnp.where(rank == ids, 1.0, 0.0).astype(LOW)

    def same_document(self, micro):
        ids = jnp.broadcast_to(self.args["doc_ids"][pl.ds(micro, 1), :].astype(WIDE), (SEQ, SEQ))
        same = jnp.where(ids == jnp.transpose(ids), 1.0, 0.0)
        return jnp.concatenate([same, same], 0) > 0.5

    def down(self, index):
        return self.full[2 + index // 2, index % 2].reshape(WIDTH, WIDTH)

    def turned_proj(self, index):
        return self.full[index // 2, index % 2].reshape(WIDTH, WIDTH)

    def turned_down(self, index):
        return self.grads[index // 2, index % 2].reshape(WIDTH, WIDTH)

    def turn_proj(self):
        for index in range(CHUNKS):
            turned = jnp.transpose(self.s["proj"][index])
            self.full[index // 2, index % 2] = turned.reshape(4, 4, ROWS, WIDTH)

    def turn_down(self):
        for index in range(CHUNKS):
            turned = jnp.transpose(self.down(index))
            self.grads[index // 2, index % 2] = turned.reshape(4, 4, ROWS, WIDTH)

    def hop(self, direction, micro):
        names = ("acts", "fin") if direction == 0 else ("dins", "bin")
        source, target = self.s[names[0]], self.s[names[1]]
        return pltpu.make_async_remote_copy(
            src_ref=source.at[micro], dst_ref=target.at[micro],
            send_sem=self.s["send"].at[direction, micro], recv_sem=self.s["recv"].at[direction, micro],
            device_id={"pipe": lax.rem(self.pipe + 1 + 2 * direction, 4)}, device_id_type=MESH,
        )

    def forward(self, micro):
        s, args = self.s, self.args

        @pl.when(self.pipe == 0)
        def _():
            s["fin"][micro] = args["tokens"][micro]

        @pl.when(self.pipe > 0)
        def _():
            self.hop(0, micro).wait_recv()

        summed = s["fin"][micro].astype(WIDE) + s["extra"][micro]
        lowered = summed.astype(LOW)
        s["lowered"][micro] = lowered
        s["resid"][micro] = summed

        @pl.when(self.attention)
        def _():
            self.attention_forward(micro, lowered)

        @pl.when(jnp.logical_not(self.attention))
        def _():
            self.feed_forward(micro, lowered)

        residual = s["resid"][micro]
        centered = residual - row_mean(residual)
        inverse = lax.rsqrt(row_mean(centered * centered) + EPSILON)
        normed = centered * inverse
        s["normed"][micro] = normed
        s["inverse"][micro] = jnp.broadcast_to(inverse, (SEQ, 128))
        s["acts"][micro] = (normed * args["ln_gain"][...] + args["ln_bias"][...]).astype(LOW)

        @pl.when(self.pipe < 3)
        def _():
            self.hop(0, micro).start()

    def attention_forward(self, micro, lowered):
        s = self.s
        for index in range(3):
            s["qkv"][micro, :, cols(index)] = dot(lowered, s["proj"][index]).astype(LOW)
        same = self.same_document(micro)
        scores, probs, mixed = [], [], []
        for pair in range(PAIRS):
            queries = two_heads(s["qkv"][micro, :, cols(pair, 128)])
            scores.append(dot_nt(queries, s["qkv"][micro, :, cols(PAIRS + pair, 128)]))
        scores = [jnp.where(same, score * 0.125, -1e30) for score in scores]
        tops = [jnp.max(score, -1, keepdims=True) for score in scores]
        powers = [jnp.exp(score - top) for score, top in zip(scores, tops)]
        totals = [jnp.sum(power, -1, keepdims=True) for power in powers]
        for pair in range(PAIRS):
            probs.append(powers[pair] / totals[pair])
            s["probs"][micro, pair] = probs[pair]
        for pair in range(PAIRS):
            values = two_heads(s["qkv"][micro, :, cols(2 * PAIRS + pair, 128)])
            mixed.append(dot(side_by_side(probs[pair].astype(LOW)), values))
        for pair in range(PAIRS):
            s["mixed"][micro, :, cols(pair, 128)] = mixed[pair].astype(LOW)
        s["resid"][micro] = s["resid"][micro] + dot(s["mixed"][micro], s["proj"][3])

    def feed_forward(self, micro, lowered):
        s = self.s
        branch = s["resid"][micro]
        for index in range(CHUNKS):
            hidden = dot(lowered, s["proj"][index])
            cumulative = 0.5 * (1.0 + lax.erf(hidden * (0.5 ** 0.5)))
            density = jnp.exp(hidden * hidden * -0.5) * 0.3989422804014327
            s["act"][micro, :, cols(index)] = (hidden * cumulative).astype(LOW)
            s["slope"][micro, :, cols(index)] = cumulative + hidden * density

        @pl.when((micro == 0) & (self.pipe == 1))
        def _():
            self.await_down()

        for index in range(CHUNKS):
            branch = branch + dot(s["act"][micro, :, cols(index)], self.down(index))
        s["resid"][micro] = branch

    def backward(self, micro):
        s, args = self.s, self.args

        @pl.when(self.pipe == 3)
        def _():
            s["bin"][micro] = args["out_cot"][micro]

        @pl.when(self.pipe < 3)
        def _():
            self.hop(1, micro).wait_recv()

        gout = s["bin"][micro].astype(WIDE)
        normed = s["normed"][micro]
        dnormed = gout * args["ln_gain"][...]
        dres = s["inverse"][micro][:, 0:1] * (
            dnormed - row_mean(dnormed) - normed * row_mean(dnormed * normed)
        )
        s["resid"][micro] = dres
        s["dbranch"][micro] = dres.astype(LOW)

        @pl.when(self.attention)
        def _():
            self.attention_backward(micro)

        @pl.when((self.pipe == 0) & (micro == 1))
        def _():
            self.send_proj(self)

        @pl.when(self.attention)
        def _():
            total = s["resid"][micro]
            for index in range(3):
                total = total + dot(s["dwide"][micro, :, cols(index)], self.turned_proj(index))
            self.input_gradient(micro, total)

        @pl.when((self.pipe == 1) & (micro == 1))
        def _():
            self.send_down(self)

        @pl.when(jnp.logical_not(self.attention))
        def _():
            self.hidden_gradient(micro)

        @pl.when((self.pipe == 1) & (micro == 1))
        def _():
            self.send_proj(self)

        @pl.when(jnp.logical_not(self.attention))
        def _():
            total = s["resid"][micro]
            for index in range(CHUNKS):
                total = total + dot(s["dwide"][micro, :, cols(index)], self.turned_proj(index))
            self.input_gradient(micro, total)

        @pl.when(self.pipe > 0)
        def _():
            self.hop(1, micro).start()

    def sums(self, micro):
        s = self.s
        stats = self.outs["stats"]
        gout = s["bin"][micro].astype(WIDE)
        stats[2:3] = stats[2:3] + jnp.sum(gout * s["normed"][micro], 0, keepdims=True)
        stats[3:4] = stats[3:4] + jnp.sum(gout, 0, keepdims=True)
        marks = self.marks(micro)
        dsum = s["resid"][micro]
        high = s["dins"][micro]
        rest = (dsum - high.astype(WIDE)).astype(LOW)
        region = self.outs["region"]
        added = dot(marks, high) + dot(marks, rest)
        region[0, 0] = region[0, 0] + added.reshape(4, 4, 8, WIDTH)

    def input_gradient(self, micro, dsum):
        self.s["resid"][micro] = dsum
        self.s["dins"][micro] = dsum.astype(LOW)

    def attention_backward(self, micro):
        s, pairs = self.s, range(PAIRS)
        dmixed = dot(s["dbranch"][micro], self.turned_proj(3)).astype(LOW)
        pieces = [[s["qkv"][micro, :, cols(part * PAIRS + pair, 128)] for part in range(3)] for pair in pairs]
        grads = [two_heads(dmixed[:, cols(pair, 128)]) for pair in pairs]
        dprobs = [dot_nt(grads[pair], pieces[pair][2]) for pair in pairs]
        probs = [s["probs"][micro, pair] for pair in pairs]
        dvalues = [dot_tn(probs[pair].astype(LOW), grads[pair]) for pair in pairs]
        sums = [jnp.sum(dprobs[pair] * probs[pair], -1, keepdims=True) for pair in pairs]
        dscores = [(probs[pair] * (dprobs[pair] - sums[pair])).astype(LOW) for pair in pairs]
        dkeys = [dot_tn(dscores[pair], two_heads(pieces[pair][0])) * 0.125 for pair in pairs]
        dqueries = [dot(side_by_side(dscores[pair]), two_heads(pieces[pair][1])) * 0.125 for pair in pairs]
        for pair in pairs:
            for part, value in enumerate((dqueries[pair], dkeys[pair], dvalues[pair])):
                s["dwide"][micro, :, cols(part * PAIRS + pair, 128)] = value.astype(LOW)

    def hidden_gradient(self, micro):
        s = self.s
        dbranch = s["dbranch"][micro]
        for index in range(CHUNKS):
            dact = dot(dbranch, self.turned_down(index))
            s["dwide"][micro, :, cols(index)] = (dact * s["slope"][micro, :, cols(index)]).astype(LOW)

    def weight_gradients(self, block):
        s = self.s
        lowered = s["lowered"][...].reshape(2 * SEQ, WIDTH)
        for side in range(2):
            quarter = 2 * side + block
            if quarter == 3:
                @pl.when(self.attention)
                def _():
                    left = s["mixed"][...].reshape(2 * SEQ, WIDTH)
                    s["dweight"][1] = dot_tn(left, s["dbranch"][...].reshape(2 * SEQ, WIDTH))

                @pl.when(jnp.logical_not(self.attention))
                def _():
                    right = s["dwide"][:, :, cols(3)].reshape(2 * SEQ, WIDTH)
                    s["dweight"][1] = dot_tn(lowered, right)
            else:
                right = s["dwide"][:, :, cols(quarter)].reshape(2 * SEQ, WIDTH)
                s["dweight"][side] = dot_tn(lowered, right)

        def run(index, _):
            half, depth = lax.div(index, 4), lax.rem(index, 4)
            rows = pl.ds(pl.multiple_of(index * 96, 96), 96)
            sides = [s["dweight"][side, rows].reshape(12, 1, 8, WIDTH) for side in range(2)]
            value = jnp.concatenate(sides, 1).reshape(4, ROWS, WIDTH)
            self.grads[block, half, depth] = value.astype(LOW)
            return 0

        lax.fori_loop(0, 8, run, 0)

    def down_gradients(self, block):
        s = self.s
        dbranch = s["dbranch"][...].reshape(2 * SEQ, WIDTH)
        for half in range(2):
            act = s["act"][:, :, cols(2 * (block - 2) + half)].reshape(2 * SEQ, WIDTH)
            self.grads[block, half] = dot_tn(act, dbranch).astype(LOW).reshape(4, 4, ROWS, WIDTH)

    def table_gradient(self, table_sum, stats):
        s = self.s
        group = lax.axis_index("dp")
        rows = pl.ds(pl.multiple_of(lax.rem(group, 16) * 8, 8), 8)
        counts = jnp.concatenate([s["column"][rows]] * (WIDTH // 128), 1)
        mean = stats[0:1] / TOKENS + s["normed_rows"][rows] * (stats[1:2] / TOKENS)
        grad = s["region_info"][2:3] * (table_sum - counts * mean)
        return jnp.where(group < 16, grad, 0.0)

    def start_stats(self):
        self.outs["stats"][...] = jnp.zeros((8, WIDTH), WIDE)
        self.outs["region"][...] = jnp.zeros((1, 1, 4, 4, 8, WIDTH), WIDE)

    def end_stats(self):
        region, stats = self.outs["region"][0, 0].reshape(REGIONS, WIDTH), self.outs["stats"]
        stats[0:1] = jnp.sum(region, 0, keepdims=True)
        stats[1:2] = jnp.sum(region * self.s["normed_rows"][...], 0, keepdims=True)

    def each(self, action):
        lax.fori_loop(0, 2, lambda micro, _: (action(micro), 0)[1], 0)

    def finish(self):
        def run(micro):
            @pl.when(self.pipe < 3)
            def _():
                self.hop(0, micro).wait_send()

            @pl.when(self.pipe > 0)
            def _():
                self.hop(1, micro).wait_send()

        self.each(run)


ARGS = ("tokens", "doc_ids", "region_ids", "ln_gain", "ln_bias", "bn_gain", "bn_bias", "table", "out_cot")
def pack_proj(proj_ref, gather):
    quarters = [proj_ref[0, :, cols(quarter)].astype(WIDE) for quarter in range(CHUNKS)]
    for block in range(2):
        parts = []
        for turn in range(3):
            for side in range(2):
                parts.append(quarters[2 * side + block][8 * turn : 8 * turn + 8])
        gather.own(block)[...] = jnp.concatenate(parts, 0).astype(LOW)


def own_counts(region_ids_ref):
    rank = lax.broadcasted_iota(jnp.int32, (REGIONS, SEQ), 0)
    total = jnp.zeros((8, REGIONS), WIDE)
    for micro in range(2):
        marks = jnp.where(rank == region_ids_ref[micro : micro + 1, :], 1.0, 0.0).astype(LOW)
        total = total + dot_nt(jnp.ones((8, SEQ), LOW), marks)
    return total


FAR = ("region_ids", "proj", "down", "table", "bn_gain", "bn_bias", "doc_ids", "ln_gain", "ln_bias", "tokens", "out_cot")


def whole_kernel(*refs):
    refs = list(refs)

    def take(count):
        taken = refs[:count]
        del refs[:count]
        return taken

    given = dict(zip(ARGS + ("proj", "down"), take(len(ARGS) + 2)))
    acts_out, dins_out, proj_out, down_out, table_out, shares_out = take(6)
    local_sem, cross_send, cross_recv = take(3)
    s = dict(zip(chain_scratch(), take(len(chain_scratch()))))
    near = dict(zip(FAR, take(len(FAR))))
    full = take(1)[0]
    gather = Gather(full, take(4), take(4))
    counted = Total(*take(5))
    held, region_held, stats = take(3)
    main = Scatter(held, take(4), take(4), take(4))
    region = Scatter(region_held, take(4), take(4), take(4), single=True)
    total = Total(*take(5))

    pipe, half = gather.pipe, gather.half
    ffn = lax.rem(pipe, 2) == 1
    pairs = lax.rem(pipe, 2) + 1
    sibling = pipe + 1 - 2 * lax.rem(pipe, 2)
    fetches = [
        pltpu.make_async_copy(
            given[name].at[:REGIONS] if name == "table" else given[name], near[name], local_sem.at[index]
        )
        for index, name in enumerate(FAR)
    ]
    for fetch in fetches:
        fetch.start()
    others = all_dp_devices() + [{"pipe": lax.rem(pipe + 1, 4)}, {"pipe": lax.rem(pipe + 3, 4)}]
    greet(others)
    for fetch in fetches[:3]:
        fetch.wait()
    pack_proj(near["proj"], gather)
    gather.own(3)[...] = near["down"][0]
    meet(others)
    for route in range(2):
        gather.start(route, route)
    cross = pltpu.make_async_remote_copy(
        src_ref=gather.own(3), dst_ref=gather.own(2), send_sem=cross_send.at[0], recv_sem=cross_recv.at[0],
        device_id={"pipe": sibling}, device_id_type=MESH,
    )

    @pl.when(jnp.logical_not(ffn))
    def _():
        cross.start()

    @pl.when(ffn)
    def _():
        gather.start(1, 3)
        cross.wait_recv()
        gather.start(0, 2)

    counted.send(0, own_counts(near["region_ids"]))

    def each(action):
        def run(pair, _):
            for route in range(2):
                action(route, 2 * pair + route)
            return 0

        lax.fori_loop(0, pairs, run, 0)

    for index, step in enumerate(gather.steps()):
        each(step)
        if index in (1, 2):
            counted.send(index, counted.receive(index - 1))
    for fetch in fetches[3:]:
        fetch.wait()
    outs = dict(stats=stats, region=region_held)

    def await_down():
        for route in range(2):
            for arriving in range(2):
                gather.last(route, 2 + route, arriving)

    def send_down(chain):
        for route in range(2):
            chain.down_gradients(2 + route)
            main.start(route, 2 + route)

    def send_proj(chain):
        for block in range(2):
            chain.weight_gradients(block)
            main.start(block, block)

    chain = Chain(near, full, counted.receive(2), outs, held, s, await_down, send_down, send_proj)
    chain.start_stats()
    for arriving in (half, 1 - half):
        for route in range(2):
            gather.last(route, route, arriving)
        unpack_proj(full, s["proj"], arriving)

    def turn():
        for route in range(2):
            gather.finish(route, route)
        chain.turn_proj()
        pl.when(pipe == 3)(await_down)
        pl.when(ffn)(chain.turn_down)

    pl.when(pipe >= 2)(turn)

    def tick(index, _):
        back = lax.div(index, 2)
        micro = lax.rem(index, 2)
        pl.when((index == 2) & (pipe < 2))(turn)
        pl.when(back == 0)(lambda: chain.forward(micro))
        pl.when(back == 1)(lambda: chain.backward(micro))
        return 0

    lax.fori_loop(0, 4, tick, 0)
    put_acts = pltpu.make_async_copy(s["acts"], acts_out, local_sem.at[len(FAR)])
    put_dins = pltpu.make_async_copy(s["dins"], dins_out, local_sem.at[len(FAR) + 1])
    put_acts.start()
    put_dins.start()
    pl.when(pipe > 1)(lambda: send_proj(chain))
    chain.each(chain.sums)
    chain.end_stats()
    total.send(0, jnp.concatenate([stats[0:4, : WIDTH // 2], stats[0:4, WIDTH // 2 :]], 0))

    def regions(action):
        for route in range(2):
            pl.when(lax.rem(pipe, 2) == route)(lambda route=route: action(route, 0))

    regions(region.start)

    @pl.when(pipe == 3)
    def _():
        send_down(chain)

    def each_late(action):
        def run(pair, _):
            for route in range(2):
                action(route, 2 * (pairs - 1 - pair) + route)
            return 0

        lax.fori_loop(0, pairs, run, 0)

    for index, (step, region_step) in enumerate(zip(main.steps(), region.steps())):
        each_late(step)
        regions(region_step)
        if index in (1, 2):
            total.send(index, total.receive(index - 1))
    back = pltpu.make_async_remote_copy(
        src_ref=main.own(2), dst_ref=down_out, send_sem=cross_send.at[1], recv_sem=cross_recv.at[1],
        device_id={"pipe": sibling}, device_id_type=MESH,
    )

    @pl.when(ffn)
    def _():
        back.start()
        down_out[...] = main.own(3)[...]

    for block in range(2):
        proj_out[block] = main.own(block)[...]
    summed = total.receive(2)
    summed = jnp.concatenate([summed[0:4], summed[4:8]], 1)
    summed = jnp.concatenate([summed, summed], 0)
    table_out[...] = chain.table_gradient(region_held[0, 0, main.depth, main.column], summed)
    shift = lax.rem(WIDTH - 24 * gather.group, WIDTH)
    shares_out[...] = pltpu.roll(summed, shift, 1)[:, :128]

    @pl.when(ffn)
    def _():
        for route in range(2):
            gather.finish(route, 2 + route)

    each(main.finish)
    regions(region.finish)
    counted.finish()
    total.finish()
    chain.finish()
    put_acts.wait()
    put_dins.wait()

    @pl.when(ffn)
    def _():
        back.wait_send()

    @pl.when(jnp.logical_not(ffn))
    def _():
        cross.wait_send()
        back.wait_recv()


def run_whole(args, proj, down):
    micro = (2, SEQ, WIDTH)
    vmem, far = pl.BlockSpec(memory_space=pltpu.VMEM), pl.BlockSpec(memory_space=pl.ANY)
    out_shape = [
        jax.ShapeDtypeStruct(micro, LOW),
        jax.ShapeDtypeStruct(micro, LOW),
        jax.ShapeDtypeStruct((2, ROWS, WIDTH), LOW),
        jax.ShapeDtypeStruct((ROWS, WIDTH), LOW),
        jax.ShapeDtypeStruct((8, WIDTH), WIDE),
        jax.ShapeDtypeStruct((8, 128), WIDE),
    ]
    blocks = (BLOCKS, 2, 4, 4, ROWS, WIDTH)
    given = dict(args, proj=proj, down=down)
    scratch = [DMA((len(FAR) + 2,)), DMA((2,)), DMA((2,))]
    scratch += list(chain_scratch().values())
    scratch += [
        pltpu.VMEM((REGIONS, WIDTH) if name == "table" else given[name].shape, given[name].dtype)
        for name in FAR
    ]
    scratch += [pltpu.VMEM(blocks, LOW)] + gather_sems() + gather_sems()
    scratch += total_scratch((8, REGIONS))
    scratch += [pltpu.VMEM(blocks, LOW), pltpu.VMEM((1, 1, 4, 4, 8, WIDTH), WIDE), pltpu.VMEM((8, WIDTH), WIDE)]
    scratch += scatter_buffers(BLOCKS, ROWS, LOW) + scatter_sems(BLOCKS) + scatter_sems(BLOCKS)
    scratch += scatter_buffers(1, 8, WIDE) + scatter_sems(1) + scatter_sems(1)
    scratch += total_scratch((8, WIDTH // 2))
    return pl.pallas_call(
        whole_kernel,
        out_shape=out_shape,
        in_specs=[far] * len(given),
        out_specs=[far] * 2 + [vmem] * (len(out_shape) - 2),
        scratch_shapes=scratch,
        compiler_params=pltpu.CompilerParams(
            collective_id=0, has_side_effects=True, vmem_limit_bytes=62 * 2**20
        ),
    )(*[args[name] for name in ARGS], proj, down)


def finish_kernel(acts, dins, proj, down, table, shares, *outs):
    outs[0][...] = acts[...].reshape(1, 2 * SEQ, WIDTH)
    outs[1][...] = dins[...].reshape(1, 2 * SEQ, WIDTH)
    for block in range(2):
        rows = proj[block].astype(WIDE)
        for turn in range(3):
            for side in range(2):
                start = 16 * turn + 8 * side
                outs[2][0, 8 * turn : 8 * turn + 8, cols(2 * side + block)] = rows[start : start + 8]
    outs[3][0] = down[...].astype(WIDE)
    for out, row in zip(outs[4:8], (2, 3, 1, 0)):
        out[...] = shares[row : row + 1, :24]
    outs[8][0] = table[...]


def finish(*arrays):
    vmem = pl.BlockSpec(memory_space=pltpu.VMEM)
    share = jax.ShapeDtypeStruct((1, 24), WIDE)
    out_shape = [
        jax.ShapeDtypeStruct((1, 2 * SEQ, WIDTH), LOW),
        jax.ShapeDtypeStruct((1, 2 * SEQ, WIDTH), LOW),
        jax.ShapeDtypeStruct((1, 24, FF), WIDE),
        jax.ShapeDtypeStruct((1, ROWS, WIDTH), WIDE),
        share, share, share, share,
        jax.ShapeDtypeStruct((1, 8, WIDTH), WIDE),
    ]
    return pl.pallas_call(
        finish_kernel, out_shape=out_shape, in_specs=[vmem] * 6, out_specs=[vmem] * 9,
        compiler_params=pltpu.CompilerParams(vmem_limit_bytes=62 * 2**20),
    )(*arrays)


def body(
    tokens, doc_ids, region_ids, proj, down, ln_gain, ln_bias, bn_gain, bn_bias, region_table, out_cot
):
    args = dict(
        tokens=tokens.reshape(2, SEQ, WIDTH), doc_ids=doc_ids, region_ids=region_ids, ln_gain=ln_gain,
        ln_bias=ln_bias, bn_gain=bn_gain, bn_bias=bn_bias, table=region_table[0],
        out_cot=out_cot.reshape(2, SEQ, WIDTH),
    )
    return tuple(finish(*run_whole(args, proj, down)))


def solution(mesh):
    in_specs = (
        P("dp", None),
        P("dp", None),
        P("dp", None),
        P("pipe", "dp", None),
        P("pipe", "dp", None),
        P("pipe", None),
        P("pipe", None),
        P("pipe", None),
        P("pipe", None),
        P("pipe", None, None),
        P("dp", None),
    )
    out_specs = (
        P("pipe", "dp", None),
        P("pipe", "dp", None),
        P("pipe", "dp", None),
        P("pipe", "dp", None),
        P("pipe", "dp"),
        P("pipe", "dp"),
        P("pipe", "dp"),
        P("pipe", "dp"),
        P("pipe", "dp", None),
    )
    return jax.shard_map(body, mesh=mesh, in_specs=in_specs, out_specs=out_specs, check_vma=False)
```

```python
from functools import partial

import jax
import jax.numpy as jnp
from jax import lax
from jax.experimental import pallas as pl
from jax.experimental.pallas import tpu as pltpu
from jax.sharding import PartitionSpec as P

HEADS = 12
FF = 3072
EPSILON = 1e-05
LOW = jnp.bfloat16
WIDE = jnp.float32
MESH = pl.DeviceIdType.MESH
DMA = pltpu.SemaphoreType.DMA
BLOCKS = 4
ROWS = 48
WIDTH = 768


def place():
    group = lax.axis_index("dp")
    pipe = lax.axis_index("pipe")
    half = lax.div(group, 16)
    rest = lax.rem(group, 16)
    return group, pipe, half, lax.div(rest, 4), lax.rem(rest, 4)


def around(position, distance):
    return lax.rem(position + distance + 4, 4)


def group_of(half, depth, column):
    return half * 16 + depth * 4 + column


def along(route, first, second):
    return (second, first) if route == 0 else (first, second)


def to_group(src, dst, send, recv, group):
    return pltpu.make_async_remote_copy(
        src_ref=src,
        dst_ref=dst,
        send_sem=send,
        recv_sem=recv,
        device_id={"dp": group},
        device_id_type=MESH,
    )


def arrived(dst, recv):
    pltpu.make_async_copy(dst, dst, recv).wait()


def narrow(ref, route, block, half, first, second):
    depth, column = along(route, first, second)
    return ref.at[block, half, depth, column]


def wide(ref, route, block, half, second):
    if route == 0:
        return ref.at[block, half, second]
    return ref.at[block, half, :, second]


def greet(others):
    barrier = pltpu.get_barrier_semaphore()
    for device in others:
        pl.semaphore_signal(barrier, inc=1, device_id=device, device_id_type=MESH)


def meet(others):
    pl.semaphore_wait(pltpu.get_barrier_semaphore(), len(others))


def ring_devices():
    group, pipe, half, depth, column = place()
    return [
        {"dp": group_of(1 - half, depth, column)},
        {"dp": group_of(half, around(depth, 1), column)},
        {"dp": group_of(half, around(depth, -1), column)},
        {"dp": group_of(half, depth, around(column, 1))},
        {"dp": group_of(half, depth, around(column, -1))},
    ]


def gather_sems():
    return [DMA((BLOCKS,)), DMA((BLOCKS, 3)), DMA((BLOCKS, 2, 2)), DMA((BLOCKS, 2, 2))]


def part(ref, way):
    return ref.at[pl.ds(2 * way, 2)]


class Rings:
    def __init__(self, ref, sends, recvs):
        self.ref, self.sends, self.recvs = ref, sends, recvs
        self.group, self.pipe, self.half, self.depth, self.column = place()
        self.partner = group_of(1 - self.half, self.depth, self.column)

    def axes(self, route):
        return (self.column, self.depth) if route == 0 else (self.depth, self.column)

    def small_peer(self, route, distance):
        if route == 0:
            return group_of(self.half, self.depth, around(self.column, distance))
        return group_of(self.half, around(self.depth, distance), self.column)

    def large_peer(self, route, distance):
        return self.small_peer(1 - route, distance)

    def own(self, block):
        return self.ref.at[block, self.half, self.depth, self.column]

    def send(self, kind, index, src, dst, group):
        return to_group(src, dst, self.sends[kind].at[index], self.recvs[kind].at[index], group)


class Gather(Rings):
    def swap(self, route, block, half, position=None):
        second = self.axes(route)[1]
        slot = wide(self.ref, route, block, half, second)
        if position is not None:
            slot = narrow(self.ref, route, block, half, position, second)
        return self.send(0, (block,), slot, slot, self.partner)

    def small(self, route, block, distance):
        slot = self.own(block)
        return self.send(1, (block, distance - 1), slot, slot, self.small_peer(route, distance))

    def large(self, route, block, half, way, position=None):
        second = self.axes(route)[1]
        slot = wide(self.ref, route, block, half, second)
        if position is not None:
            slot = narrow(self.ref, route, block, half, position, second)
        return self.send(2, (block, half, way), slot, slot, self.large_peer(route, 1 - 2 * way))

    def large_relay(self, route, block, half, way):
        second = self.axes(route)[1]
        distance = 1 - 2 * way
        slot = part(wide(self.ref, route, block, half, around(second, -distance)), way)
        return self.send(3, (block, half, way), slot, slot, self.large_peer(route, distance))

    def pass_on(self, route, block, position):
        for way in range(2):
            self.large(route, block, self.half, way, position).start()
        self.swap(route, block, self.half, position).start()

    def start(self, route, block):
        for distance in range(1, 4):
            self.small(route, block, distance).start()
        self.pass_on(route, block, self.axes(route)[0])

    def end_small(self, route, block):
        for distance in (1, 3, 2):
            self.small(route, block, distance).wait_recv()
            self.pass_on(route, block, around(self.axes(route)[0], -distance))

    def relay_large(self, route, block, half):
        for way in range(2):
            self.large(route, block, half, way).wait_recv()
            self.large_relay(route, block, half, way).start()

    def swap_in(self, route, block):
        self.swap(route, block, 1 - self.half).wait_recv()
        for way in range(2):
            self.large(route, block, 1 - self.half, way).start()

    def last(self, route, block, half):
        for way in range(2):
            self.large_relay(route, block, half, way).wait_recv()

    def steps(self):
        return [
            self.end_small,
            lambda route, block: self.relay_large(route, block, self.half),
            self.swap_in,
            lambda route, block: self.relay_large(route, block, 1 - self.half),
        ]

    def finish(self, route, block):
        self.swap(route, block, self.half).wait_send()
        for distance in range(1, 4):
            self.small(route, block, distance).wait_send()
        for half in range(2):
            for way in range(2):
                self.large(route, block, half, way).wait_send()
                self.large_relay(route, block, half, way).wait_send()


def scatter_buffers(blocks, rows, dtype):
    return [
        pltpu.VMEM((blocks, 2, 4, rows, WIDTH), dtype),
        pltpu.VMEM((blocks, 2, 2, 4, rows, WIDTH), dtype),
        pltpu.VMEM((blocks, 4, rows, WIDTH), dtype),
        pltpu.VMEM((blocks, 3, rows, WIDTH), dtype),
    ]


def scatter_sems(blocks):
    return [DMA((blocks, 2, 2)), DMA((blocks, 2, 2)), DMA((blocks,)), DMA((blocks, 3))]


def accumulate(target, others):
    total = target[...].astype(WIDE)
    for other in others:
        total = total + other[...].astype(WIDE)
    target[...] = total.astype(target.dtype)


class Scatter(Rings):
    def __init__(self, ref, buffers, sends, recvs, single=False):
        super().__init__(ref, sends, recvs)
        self.buffers, self.single = buffers, single

    def large_early(self, route, block, half, way):
        second = self.axes(route)[1]
        return self.send(
            0, (block, half, way), part(wide(self.ref, route, block, half, around(second, 2)), way),
            part(self.buffers[0].at[block, half], way), self.large_peer(route, 1 - 2 * way),
        )

    def large(self, route, block, half, way, side=None):
        second = self.axes(route)[1]
        distance = 1 - 2 * way
        src = wide(self.ref, route, block, half, around(second, distance))
        dst = self.buffers[1].at[block, way, half]
        if side is not None:
            src, dst = part(src, side), part(dst, side)
        return self.send(1, (block, way, half), src, dst, self.large_peer(route, distance))

    def swap(self, route, block, half):
        second = self.axes(route)[1]
        return self.send(
            2, (block,), wide(self.ref, route, block, half, second), self.buffers[2].at[block], self.partner
        )

    def target(self, route, block, distance):
        first, second = self.axes(route)
        half = 0 if self.single else self.half
        return narrow(self.ref, route, block, half, around(first, distance), second)

    def small(self, route, block, distance):
        return self.send(
            3, (block, distance - 1), self.target(route, block, distance), self.buffers[3].at[block, distance - 1],
            self.small_peer(route, distance),
        )

    def where(self, half, action):
        if self.single:
            pl.when(half == 0)(lambda: action(0))
        else:
            action(half)

    def begin(self, route, block, half):
        def run(half):
            for way in range(2):
                self.large_early(route, block, half, way).start()
                self.large(route, block, half, way, 1 - way).start()

        self.where(half, run)

    def middle(self, route, block, half):
        def run(half):
            second = self.axes(route)[1]
            for way in range(2):
                self.large_early(route, block, half, way).wait_recv()
                accumulate(
                    part(wide(self.ref, route, block, half, around(second, 1 - 2 * way)), way),
                    [part(self.buffers[0].at[block, half], way)],
                )
                self.large(route, block, half, way, way).start()

        self.where(half, run)

    def sum_large(self, route, block, half, others):
        for way in range(2):
            self.large(route, block, half, way).wait_recv()
        arrivals = [self.buffers[1].at[block, way, half] for way in range(2)]
        accumulate(wide(self.ref, route, block, half, self.axes(route)[1]), arrivals + others)

    def start(self, route, block):
        self.begin(route, block, 1 - self.half)

    def turn(self, route, block):
        self.middle(route, block, 1 - self.half)
        self.begin(route, block, self.half)

    def sum_other(self, route, block):
        def run(half):
            self.sum_large(route, block, half, [])
            self.swap(route, block, half).start()

        self.where(1 - self.half, run)

    def begin_swap(self, route, block):
        self.begin(route, block, self.half)
        self.sum_other(route, block)

    def swap_begin(self, route, block):
        self.sum_other(route, block)
        self.begin(route, block, self.half)

    def sum_own(self, route, block):
        def run(half):
            self.swap(route, block, half).wait_recv()
            self.sum_large(route, block, half, [self.buffers[2].at[block]])
            for distance in range(1, 4):
                self.small(route, block, distance).start()

        self.where(self.half, run)

    def last(self, route, block):
        def run(half):
            for distance in range(1, 4):
                self.small(route, block, distance).wait_recv()
            arrivals = [self.buffers[3].at[block, index] for index in range(3)]
            accumulate(self.target(route, block, 0), arrivals)

        self.where(self.half, run)

    def steps(self):
        return [
            lambda route, block: self.middle(route, block, 1 - self.half),
            self.begin_swap,
            lambda route, block: self.middle(route, block, self.half),
            self.sum_own,
            self.last,
        ]

    def finish(self, route, block):
        def large(half):
            for way in range(2):
                self.large_early(route, block, half, way).wait_send()
                self.large(route, block, half, way).wait_send()

        def other(half):
            large(half)
            self.swap(route, block, half).wait_send()

        def own(half):
            large(half)
            for distance in range(1, 4):
                self.small(route, block, distance).wait_send()

        self.where(1 - self.half, other)
        self.where(self.half, own)


class Total:
    def __init__(self, first, second, third, sends, recvs):
        self.stages, self.sends, self.recvs = (first, second, third), sends, recvs
        self.group, self.pipe, self.half, self.depth, self.column = place()
        self.where = (self.column, self.depth, self.half)

    def copy(self, stage, distance):
        here, buffer = self.where[stage], self.stages[stage]
        if stage == 0:
            peer = group_of(self.half, self.depth, around(here, distance))
        elif stage == 1:
            peer = group_of(self.half, around(here, distance), self.column)
        else:
            peer = group_of(1 - here, self.depth, self.column)
        return to_group(
            buffer.at[here], buffer.at[here],
            self.sends.at[stage, distance - 1], self.recvs.at[stage, distance - 1], peer,
        )

    def distances(self, stage):
        return range(1, 4) if stage < 2 else range(1, 2)

    def send(self, stage, value):
        self.stages[stage][self.where[stage]] = value
        for distance in self.distances(stage):
            self.copy(stage, distance).start()

    def receive(self, stage):
        for distance in self.distances(stage):
            self.copy(stage, distance).wait_recv()
        total = self.stages[stage][0]
        for index in range(1, 4 if stage < 2 else 2):
            total = total + self.stages[stage][index]
        return total

    def finish(self):
        for stage in range(3):
            for distance in self.distances(stage):
                self.copy(stage, distance).wait_send()


def total_scratch(shape):
    return [
        pltpu.VMEM((4,) + shape, WIDE),
        pltpu.VMEM((4,) + shape, WIDE),
        pltpu.VMEM((2,) + shape, WIDE),
        DMA((3, 3)),
        DMA((3, 3)),
    ]


def all_dp_devices():
    group, pipe, half, depth, column = place()
    return ring_devices() + [
        {"dp": group_of(half, around(depth, 2), column)},
        {"dp": group_of(half, depth, around(column, 2))},
    ]


PAIRS = HEADS // 2
SEQ = 128
REGIONS = 128
TOKENS = 8192
CHUNKS = 4


def dot(left, right):
    return lax.dot_general(left, right, (((1,), (0,)), ((), ())), preferred_element_type=WIDE)


def dot_nt(left, right):
    return lax.dot_general(left, right, (((1,), (1,)), ((), ())), preferred_element_type=WIDE)


def dot_tn(left, right):
    return lax.dot_general(left, right, (((0,), (0,)), ((), ())), preferred_element_type=WIDE)


def cols(index, width=WIDTH):
    return slice(index * width, (index + 1) * width)


def two_heads(pair):
    lane = lax.broadcasted_iota(jnp.int32, pair.shape, 1)
    zero = jnp.zeros_like(pair)
    return jnp.concatenate([jnp.where(lane < 64, pair, zero), jnp.where(lane < 64, zero, pair)], 0)


def side_by_side(stacked):
    return jnp.concatenate([stacked[:SEQ], stacked[SEQ:]], 1)


def row_mean(value):
    return jnp.mean(value, -1, keepdims=True)


def chain_scratch():
    return dict(
        proj=pltpu.VMEM((CHUNKS, WIDTH, WIDTH), LOW),
        fin=pltpu.VMEM((2, SEQ, WIDTH), LOW),
        bin=pltpu.VMEM((2, SEQ, WIDTH), LOW),
        lowered=pltpu.VMEM((2, SEQ, WIDTH), LOW),
        acts=pltpu.VMEM((2, SEQ, WIDTH), LOW),
        dins=pltpu.VMEM((2, SEQ, WIDTH), LOW),
        extra=pltpu.VMEM((2, SEQ, WIDTH), WIDE),
        resid=pltpu.VMEM((2, SEQ, WIDTH), WIDE),
        normed=pltpu.VMEM((2, SEQ, WIDTH), WIDE),
        inverse=pltpu.VMEM((2, SEQ, 128), WIDE),
        normed_rows=pltpu.VMEM((REGIONS, WIDTH), WIDE),
        region_info=pltpu.VMEM((8, WIDTH), WIDE),
        column=pltpu.VMEM((REGIONS, 128), WIDE),
        qkv=pltpu.VMEM((2, SEQ, 3 * WIDTH), LOW),
        probs=pltpu.VMEM((2, PAIRS, 2 * SEQ, SEQ), WIDE),
        mixed=pltpu.VMEM((2, SEQ, WIDTH), LOW),
        dbranch=pltpu.VMEM((2, SEQ, WIDTH), LOW),
        dwide=pltpu.VMEM((2, SEQ, FF), LOW),
        act=pltpu.VMEM((2, SEQ, FF), LOW),
        slope=pltpu.VMEM((2, SEQ, FF), WIDE),
        dweight=pltpu.VMEM((2, WIDTH, WIDTH), WIDE),
        send=DMA((2, 2)),
        recv=DMA((2, 2)),
    )


def unpack_proj(full_ref, proj_ref, half):
    def run(depth, _):
        rows = pl.ds(pl.multiple_of((half * 4 + depth) * 96, 96), 96)
        for block in range(2):
            value = full_ref[block, half, depth].astype(WIDE).reshape(12, 2, 8, WIDTH)
            for side in range(2):
                proj_ref[2 * side + block, rows] = value[:, side].reshape(96, WIDTH).astype(LOW)
        return 0

    lax.fori_loop(0, 4, run, 0)


class Chain:
    def __init__(self, args, full_ref, counts, outs, grads, s, await_down, send_down, send_proj):
        self.await_down, self.send_down, self.send_proj = await_down, send_down, send_proj
        self.args, self.full, self.outs, self.grads, self.s = args, full_ref, outs, grads, s
        self.pipe = lax.axis_index("pipe")
        self.attention = lax.rem(self.pipe, 2) == 0
        self.region_statistics(counts)
        self.each(self.region_terms)

    def region_statistics(self, counts):
        table_ref, s = self.args["table"], self.s
        column = jnp.transpose(jnp.broadcast_to(counts[0:1], (SEQ, REGIONS)))
        s["column"][...] = column
        for index in range(WIDTH // 128):
            lanes = cols(index, 128)
            table = table_ref[:, lanes].astype(WIDE)
            mean = jnp.sum(table * column, 0, keepdims=True) / TOKENS
            second = jnp.sum(table * table * column, 0, keepdims=True) / TOKENS
            inverse = lax.rsqrt(second - mean * mean + EPSILON)
            s["normed_rows"][:, lanes] = (table - mean) * inverse
            s["region_info"][0:1, lanes] = mean
            s["region_info"][1:2, lanes] = inverse
            s["region_info"][2:3, lanes] = inverse * self.args["bn_gain"][0:1, lanes]

    def region_terms(self, micro):
        embedded = dot_tn(self.marks(micro), self.args["table"][...])
        info = self.s["region_info"]
        self.s["extra"][micro] = (embedded - info[0:1]) * info[2:3] + self.args["bn_bias"][...]

    def marks(self, micro):
        ids = self.args["region_ids"][pl.ds(micro, 1), :]
        rank = lax.broadcasted_iota(jnp.int32, (REGIONS, SEQ), 0)
        return jnp.where(rank == ids, 1.0, 0.0).astype(LOW)

    def same_document(self, micro):
        ids = jnp.broadcast_to(self.args["doc_ids"][pl.ds(micro, 1), :].astype(WIDE), (SEQ, SEQ))
        same = jnp.where(ids == jnp.transpose(ids), 1.0, 0.0)
        return jnp.concatenate([same, same], 0) > 0.5

    def down(self, index):
        return self.full[2 + index // 2, index % 2].reshape(WIDTH, WIDTH)

    def turned_proj(self, index):
        return self.full[index // 2, index % 2].reshape(WIDTH, WIDTH)

    def turned_down(self, index):
        return self.grads[index // 2, index % 2].reshape(WIDTH, WIDTH)

    def turn_proj(self):
        for index in range(CHUNKS):
            turned = jnp.transpose(self.s["proj"][index])
            self.full[index // 2, index % 2] = turned.reshape(4, 4, ROWS, WIDTH)

    def turn_down(self):
        for index in range(CHUNKS):
            turned = jnp.transpose(self.down(index))
            self.grads[index // 2, index % 2] = turned.reshape(4, 4, ROWS, WIDTH)

    def hop(self, direction, micro):
        names = ("acts", "fin") if direction == 0 else ("dins", "bin")
        source, target = self.s[names[0]], self.s[names[1]]
        return pltpu.make_async_remote_copy(
            src_ref=source.at[micro], dst_ref=target.at[micro],
            send_sem=self.s["send"].at[direction, micro], recv_sem=self.s["recv"].at[direction, micro],
            device_id={"pipe": lax.rem(self.pipe + 1 + 2 * direction, 4)}, device_id_type=MESH,
        )

    def forward(self, micro):
        s, args = self.s, self.args

        @pl.when(self.pipe == 0)
        def _():
            s["fin"][micro] = args["tokens"][micro]

        @pl.when(self.pipe > 0)
        def _():
            self.hop(0, micro).wait_recv()

        summed = s["fin"][micro].astype(WIDE) + s["extra"][micro]
        lowered = summed.astype(LOW)
        s["lowered"][micro] = lowered
        s["resid"][micro] = summed

        @pl.when(self.attention)
        def _():
            self.attention_forward(micro, lowered)

        @pl.when(jnp.logical_not(self.attention))
        def _():
            self.feed_forward(micro, lowered)

        residual = s["resid"][micro]
        centered = residual - row_mean(residual)
        inverse = lax.rsqrt(row_mean(centered * centered) + EPSILON)
        normed = centered * inverse
        s["normed"][micro] = normed
        s["inverse"][micro] = jnp.broadcast_to(inverse, (SEQ, 128))
        s["acts"][micro] = (normed * args["ln_gain"][...] + args["ln_bias"][...]).astype(LOW)

        @pl.when(self.pipe < 3)
        def _():
            self.hop(0, micro).start()

    def attention_forward(self, micro, lowered):
        s = self.s
        for index in range(3):
            s["qkv"][micro, :, cols(index)] = dot(lowered, s["proj"][index]).astype(LOW)
        same = self.same_document(micro)
        scores, probs, mixed = [], [], []
        for pair in range(PAIRS):
            queries = two_heads(s["qkv"][micro, :, cols(pair, 128)])
            scores.append(dot_nt(queries, s["qkv"][micro, :, cols(PAIRS + pair, 128)]))
        scores = [jnp.where(same, score * 0.125, -1e30) for score in scores]
        tops = [jnp.max(score, -1, keepdims=True) for score in scores]
        powers = [jnp.exp(score - top) for score, top in zip(scores, tops)]
        totals = [jnp.sum(power, -1, keepdims=True) for power in powers]
        for pair in range(PAIRS):
            probs.append(powers[pair] / totals[pair])
            s["probs"][micro, pair] = probs[pair]
        for pair in range(PAIRS):
            values = two_heads(s["qkv"][micro, :, cols(2 * PAIRS + pair, 128)])
            mixed.append(dot(side_by_side(probs[pair].astype(LOW)), values))
        for pair in range(PAIRS):
            s["mixed"][micro, :, cols(pair, 128)] = mixed[pair].astype(LOW)
        s["resid"][micro] = s["resid"][micro] + dot(s["mixed"][micro], s["proj"][3])

    def feed_forward(self, micro, lowered):
        s = self.s
        branch = s["resid"][micro]
        for index in range(CHUNKS):
            hidden = dot(lowered, s["proj"][index])
            cumulative = 0.5 * (1.0 + lax.erf(hidden * (0.5 ** 0.5)))
            density = jnp.exp(hidden * hidden * -0.5) * 0.3989422804014327
            s["act"][micro, :, cols(index)] = (hidden * cumulative).astype(LOW)
            s["slope"][micro, :, cols(index)] = cumulative + hidden * density

        @pl.when((micro == 0) & (self.pipe == 1))
        def _():
            self.await_down()

        for index in range(CHUNKS):
            branch = branch + dot(s["act"][micro, :, cols(index)], self.down(index))
        s["resid"][micro] = branch

    def backward(self, micro):
        s, args = self.s, self.args

        @pl.when(self.pipe == 3)
        def _():
            s["bin"][micro] = args["out_cot"][micro]

        @pl.when(self.pipe < 3)
        def _():
            self.hop(1, micro).wait_recv()

        gout = s["bin"][micro].astype(WIDE)
        normed = s["normed"][micro]
        dnormed = gout * args["ln_gain"][...]
        dres = s["inverse"][micro][:, 0:1] * (
            dnormed - row_mean(dnormed) - normed * row_mean(dnormed * normed)
        )
        s["resid"][micro] = dres
        s["dbranch"][micro] = dres.astype(LOW)

        @pl.when(self.attention)
        def _():
            self.attention_backward(micro)

        @pl.when((self.pipe == 0) & (micro == 1))
        def _():
            self.send_proj(self)

        @pl.when(self.attention)
        def _():
            total = s["resid"][micro]
            for index in range(3):
                total = total + dot(s["dwide"][micro, :, cols(index)], self.turned_proj(index))
            self.input_gradient(micro, total)

        @pl.when((self.pipe == 1) & (micro == 1))
        def _():
            self.send_down(self)

        @pl.when(jnp.logical_not(self.attention))
        def _():
            self.hidden_gradient(micro)

        @pl.when((self.pipe == 1) & (micro == 1))
        def _():
            self.send_proj(self)

        @pl.when(jnp.logical_not(self.attention))
        def _():
            total = s["resid"][micro]
            for index in range(CHUNKS):
                total = total + dot(s["dwide"][micro, :, cols(index)], self.turned_proj(index))
            self.input_gradient(micro, total)

        @pl.when(self.pipe > 0)
        def _():
            self.hop(1, micro).start()

    def sums(self, micro):
        s = self.s
        stats = self.outs["stats"]
        gout = s["bin"][micro].astype(WIDE)
        stats[2:3] = stats[2:3] + jnp.sum(gout * s["normed"][micro], 0, keepdims=True)
        stats[3:4] = stats[3:4] + jnp.sum(gout, 0, keepdims=True)
        marks = self.marks(micro)
        dsum = s["resid"][micro]
        high = s["dins"][micro]
        rest = (dsum - high.astype(WIDE)).astype(LOW)
        region = self.outs["region"]
        added = dot(marks, high) + dot(marks, rest)
        region[0, 0] = region[0, 0] + added.reshape(4, 4, 8, WIDTH)

    def input_gradient(self, micro, dsum):
        self.s["resid"][micro] = dsum
        self.s["dins"][micro] = dsum.astype(LOW)

    def attention_backward(self, micro):
        s, pairs = self.s, range(PAIRS)
        dmixed = dot(s["dbranch"][micro], self.turned_proj(3)).astype(LOW)
        pieces = [[s["qkv"][micro, :, cols(part * PAIRS + pair, 128)] for part in range(3)] for pair in pairs]
        grads = [two_heads(dmixed[:, cols(pair, 128)]) for pair in pairs]
        dprobs = [dot_nt(grads[pair], pieces[pair][2]) for pair in pairs]
        probs = [s["probs"][micro, pair] for pair in pairs]
        dvalues = [dot_tn(probs[pair].astype(LOW), grads[pair]) for pair in pairs]
        sums = [jnp.sum(dprobs[pair] * probs[pair], -1, keepdims=True) for pair in pairs]
        dscores = [(probs[pair] * (dprobs[pair] - sums[pair])).astype(LOW) for pair in pairs]
        dkeys = [dot_tn(dscores[pair], two_heads(pieces[pair][0])) * 0.125 for pair in pairs]
        dqueries = [dot(side_by_side(dscores[pair]), two_heads(pieces[pair][1])) * 0.125 for pair in pairs]
        for pair in pairs:
            for part, value in enumerate((dqueries[pair], dkeys[pair], dvalues[pair])):
                s["dwide"][micro, :, cols(part * PAIRS + pair, 128)] = value.astype(LOW)

    def hidden_gradient(self, micro):
        s = self.s
        dbranch = s["dbranch"][micro]
        for index in range(CHUNKS):
            dact = dot(dbranch, self.turned_down(index))
            s["dwide"][micro, :, cols(index)] = (dact * s["slope"][micro, :, cols(index)]).astype(LOW)

    def weight_gradients(self, block):
        s = self.s
        lowered = s["lowered"][...].reshape(2 * SEQ, WIDTH)
        for side in range(2):
            quarter = 2 * side + block
            if quarter == 3:
                @pl.when(self.attention)
                def _():
                    left = s["mixed"][...].reshape(2 * SEQ, WIDTH)
                    s["dweight"][1] = dot_tn(left, s["dbranch"][...].reshape(2 * SEQ, WIDTH))

                @pl.when(jnp.logical_not(self.attention))
                def _():
                    right = s["dwide"][:, :, cols(3)].reshape(2 * SEQ, WIDTH)
                    s["dweight"][1] = dot_tn(lowered, right)
            else:
                right = s["dwide"][:, :, cols(quarter)].reshape(2 * SEQ, WIDTH)
                s["dweight"][side] = dot_tn(lowered, right)

        def run(index, _):
            half, depth = lax.div(index, 4), lax.rem(index, 4)
            rows = pl.ds(pl.multiple_of(index * 96, 96), 96)
            sides = [s["dweight"][side, rows].reshape(12, 1, 8, WIDTH) for side in range(2)]
            value = jnp.concatenate(sides, 1).reshape(4, ROWS, WIDTH)
            self.grads[block, half, depth] = value.astype(LOW)
            return 0

        lax.fori_loop(0, 8, run, 0)

    def down_gradients(self, block):
        s = self.s
        dbranch = s["dbranch"][...].reshape(2 * SEQ, WIDTH)
        for half in range(2):
            act = s["act"][:, :, cols(2 * (block - 2) + half)].reshape(2 * SEQ, WIDTH)
            self.grads[block, half] = dot_tn(act, dbranch).astype(LOW).reshape(4, 4, ROWS, WIDTH)

    def table_gradient(self, table_sum, stats):
        s = self.s
        group = lax.axis_index("dp")
        rows = pl.ds(pl.multiple_of(lax.rem(group, 16) * 8, 8), 8)
        counts = jnp.concatenate([s["column"][rows]] * (WIDTH // 128), 1)
        mean = stats[0:1] / TOKENS + s["normed_rows"][rows] * (stats[1:2] / TOKENS)
        grad = s["region_info"][2:3] * (table_sum - counts * mean)
        return jnp.where(group < 16, grad, 0.0)

    def start_stats(self):
        self.outs["stats"][...] = jnp.zeros((8, WIDTH), WIDE)
        self.outs["region"][...] = jnp.zeros((1, 1, 4, 4, 8, WIDTH), WIDE)

    def end_stats(self):
        region, stats = self.outs["region"][0, 0].reshape(REGIONS, WIDTH), self.outs["stats"]
        stats[0:1] = jnp.sum(region, 0, keepdims=True)
        stats[1:2] = jnp.sum(region * self.s["normed_rows"][...], 0, keepdims=True)

    def each(self, action):
        lax.fori_loop(0, 2, lambda micro, _: (action(micro), 0)[1], 0)

    def finish(self):
        def run(micro):
            @pl.when(self.pipe < 3)
            def _():
                self.hop(0, micro).wait_send()

            @pl.when(self.pipe > 0)
            def _():
                self.hop(1, micro).wait_send()

        self.each(run)


ARGS = ("tokens", "doc_ids", "region_ids", "ln_gain", "ln_bias", "bn_gain", "bn_bias", "table", "out_cot")
def pack_proj(proj_ref, gather):
    quarters = [proj_ref[0, :, cols(quarter)].astype(WIDE) for quarter in range(CHUNKS)]
    for block in range(2):
        parts = []
        for turn in range(3):
            for side in range(2):
                parts.append(quarters[2 * side + block][8 * turn : 8 * turn + 8])
        gather.own(block)[...] = jnp.concatenate(parts, 0).astype(LOW)


def own_counts(region_ids_ref):
    rank = lax.broadcasted_iota(jnp.int32, (REGIONS, SEQ), 0)
    total = jnp.zeros((8, REGIONS), WIDE)
    for micro in range(2):
        marks = jnp.where(rank == region_ids_ref[micro : micro + 1, :], 1.0, 0.0).astype(LOW)
        total = total + dot_nt(jnp.ones((8, SEQ), LOW), marks)
    return total


FAR = ("region_ids", "proj", "down", "table", "bn_gain", "bn_bias", "doc_ids", "ln_gain", "ln_bias", "tokens", "out_cot")


def whole_kernel(*refs):
    refs = list(refs)

    def take(count):
        taken = refs[:count]
        del refs[:count]
        return taken

    given = dict(zip(ARGS + ("proj", "down"), take(len(ARGS) + 2)))
    acts_out, dins_out, proj_out, down_out, table_out, shares_out = take(6)
    local_sem, cross_send, cross_recv = take(3)
    s = dict(zip(chain_scratch(), take(len(chain_scratch()))))
    near = dict(zip(FAR, take(len(FAR))))
    full = take(1)[0]
    gather = Gather(full, take(4), take(4))
    counted = Total(*take(5))
    held, region_held, stats = take(3)
    main = Scatter(held, take(4), take(4), take(4))
    region = Scatter(region_held, take(4), take(4), take(4), single=True)
    total = Total(*take(5))

    pipe, half = gather.pipe, gather.half
    ffn = lax.rem(pipe, 2) == 1
    pairs = lax.rem(pipe, 2) + 1
    sibling = pipe + 1 - 2 * lax.rem(pipe, 2)
    fetches = [
        pltpu.make_async_copy(
            given[name].at[:REGIONS] if name == "table" else given[name], near[name], local_sem.at[index]
        )
        for index, name in enumerate(FAR)
    ]
    for fetch in fetches:
        fetch.start()
    others = all_dp_devices() + [{"pipe": lax.rem(pipe + 1, 4)}, {"pipe": lax.rem(pipe + 3, 4)}]
    greet(others)
    for fetch in fetches[:3]:
        fetch.wait()
    pack_proj(near["proj"], gather)
    gather.own(3)[...] = near["down"][0]
    meet(others)
    for route in range(2):
        gather.start(route, route)
    cross = pltpu.make_async_remote_copy(
        src_ref=gather.own(3), dst_ref=gather.own(2), send_sem=cross_send.at[0], recv_sem=cross_recv.at[0],
        device_id={"pipe": sibling}, device_id_type=MESH,
    )

    @pl.when(jnp.logical_not(ffn))
    def _():
        cross.start()

    @pl.when(ffn)
    def _():
        gather.start(1, 3)
        cross.wait_recv()
        gather.start(0, 2)

    counted.send(0, own_counts(near["region_ids"]))

    def each(action):
        def run(pair, _):
            for route in range(2):
                action(route, 2 * pair + route)
            return 0

        lax.fori_loop(0, pairs, run, 0)

    for index, step in enumerate(gather.steps()):
        each(step)
        if index in (1, 2):
            counted.send(index, counted.receive(index - 1))
    for fetch in fetches[3:]:
        fetch.wait()
    outs = dict(stats=stats, region=region_held)

    def await_down():
        for route in range(2):
            for arriving in range(2):
                gather.last(route, 2 + route, arriving)

    def send_down(chain):
        for route in range(2):
            chain.down_gradients(2 + route)
            main.start(route, 2 + route)

    def send_proj(chain):
        for block in range(2):
            chain.weight_gradients(block)
            main.start(block, block)

    chain = Chain(near, full, counted.receive(2), outs, held, s, await_down, send_down, send_proj)
    chain.start_stats()
    for arriving in (half, 1 - half):
        for route in range(2):
            gather.last(route, route, arriving)
        unpack_proj(full, s["proj"], arriving)

    def turn():
        for route in range(2):
            gather.finish(route, route)
        chain.turn_proj()
        pl.when(pipe == 3)(await_down)
        pl.when(ffn)(chain.turn_down)

    pl.when(pipe >= 2)(turn)

    def tick(index, _):
        back = lax.div(index, 2)
        micro = lax.rem(index, 2)
        pl.when((index == 2) & (pipe < 2))(turn)
        pl.when(back == 0)(lambda: chain.forward(micro))
        pl.when(back == 1)(lambda: chain.backward(micro))
        return 0

    lax.fori_loop(0, 4, tick, 0)
    put_acts = pltpu.make_async_copy(s["acts"], acts_out, local_sem.at[len(FAR)])
    put_dins = pltpu.make_async_copy(s["dins"], dins_out, local_sem.at[len(FAR) + 1])
    put_acts.start()
    put_dins.start()
    pl.when(pipe > 1)(lambda: send_proj(chain))
    chain.each(chain.sums)
    chain.end_stats()
    total.send(0, jnp.concatenate([stats[0:4, : WIDTH // 2], stats[0:4, WIDTH // 2 :]], 0))

    def regions(action):
        for route in range(2):
            pl.when(lax.rem(pipe, 2) == route)(lambda route=route: action(route, 0))

    regions(region.start)

    @pl.when(pipe == 3)
    def _():
        send_down(chain)

    def each_late(action):
        def run(pair, _):
            for route in range(2):
                action(route, 2 * (pairs - 1 - pair) + route)
            return 0

        lax.fori_loop(0, pairs, run, 0)

    steps, region_steps = main.steps(), region.steps()
    for index in range(4):
        each_late(steps[index])
        regions(region_steps[index])
        if index in (1, 2):
            total.send(index, total.receive(index - 1))
    regions(region_steps[4])
    summed = total.receive(2)
    summed = jnp.concatenate([summed[0:4], summed[4:8]], 1)
    summed = jnp.concatenate([summed, summed], 0)
    table_out[...] = chain.table_gradient(region_held[0, 0, main.depth, main.column], summed)
    shift = lax.rem(WIDTH - 24 * gather.group, WIDTH)
    shares_out[...] = pltpu.roll(summed, shift, 1)[:, :128]
    each_late(steps[4])
    back = pltpu.make_async_remote_copy(
        src_ref=main.own(2), dst_ref=down_out, send_sem=cross_send.at[1], recv_sem=cross_recv.at[1],
        device_id={"pipe": sibling}, device_id_type=MESH,
    )

    @pl.when(ffn)
    def _():
        back.start()
        down_out[...] = main.own(3)[...]

    for block in range(2):
        proj_out[block] = main.own(block)[...]

    @pl.when(ffn)
    def _():
        for route in range(2):
            gather.finish(route, 2 + route)

    each(main.finish)
    regions(region.finish)
    counted.finish()
    total.finish()
    chain.finish()
    put_acts.wait()
    put_dins.wait()

    @pl.when(ffn)
    def _():
        back.wait_send()

    @pl.when(jnp.logical_not(ffn))
    def _():
        cross.wait_send()
        back.wait_recv()


def run_whole(args, proj, down):
    micro = (2, SEQ, WIDTH)
    vmem, far = pl.BlockSpec(memory_space=pltpu.VMEM), pl.BlockSpec(memory_space=pl.ANY)
    out_shape = [
        jax.ShapeDtypeStruct(micro, LOW),
        jax.ShapeDtypeStruct(micro, LOW),
        jax.ShapeDtypeStruct((2, ROWS, WIDTH), LOW),
        jax.ShapeDtypeStruct((ROWS, WIDTH), LOW),
        jax.ShapeDtypeStruct((8, WIDTH), WIDE),
        jax.ShapeDtypeStruct((8, 128), WIDE),
    ]
    blocks = (BLOCKS, 2, 4, 4, ROWS, WIDTH)
    given = dict(args, proj=proj, down=down)
    scratch = [DMA((len(FAR) + 2,)), DMA((2,)), DMA((2,))]
    scratch += list(chain_scratch().values())
    scratch += [
        pltpu.VMEM((REGIONS, WIDTH) if name == "table" else given[name].shape, given[name].dtype)
        for name in FAR
    ]
    scratch += [pltpu.VMEM(blocks, LOW)] + gather_sems() + gather_sems()
    scratch += total_scratch((8, REGIONS))
    scratch += [pltpu.VMEM(blocks, LOW), pltpu.VMEM((1, 1, 4, 4, 8, WIDTH), WIDE), pltpu.VMEM((8, WIDTH), WIDE)]
    scratch += scatter_buffers(BLOCKS, ROWS, LOW) + scatter_sems(BLOCKS) + scatter_sems(BLOCKS)
    scratch += scatter_buffers(1, 8, WIDE) + scatter_sems(1) + scatter_sems(1)
    scratch += total_scratch((8, WIDTH // 2))
    return pl.pallas_call(
        whole_kernel,
        out_shape=out_shape,
        in_specs=[far] * len(given),
        out_specs=[far] * 2 + [vmem] * (len(out_shape) - 2),
        scratch_shapes=scratch,
        compiler_params=pltpu.CompilerParams(
            collective_id=0, has_side_effects=True, vmem_limit_bytes=62 * 2**20
        ),
    )(*[args[name] for name in ARGS], proj, down)


def finish_kernel(acts, dins, proj, down, table, shares, *outs):
    outs[0][...] = acts[...].reshape(1, 2 * SEQ, WIDTH)
    outs[1][...] = dins[...].reshape(1, 2 * SEQ, WIDTH)
    for block in range(2):
        rows = proj[block].astype(WIDE)
        for turn in range(3):
            for side in range(2):
                start = 16 * turn + 8 * side
                outs[2][0, 8 * turn : 8 * turn + 8, cols(2 * side + block)] = rows[start : start + 8]
    outs[3][0] = down[...].astype(WIDE)
    for out, row in zip(outs[4:8], (2, 3, 1, 0)):
        out[...] = shares[row : row + 1, :24]
    outs[8][0] = table[...]


def finish(*arrays):
    vmem = pl.BlockSpec(memory_space=pltpu.VMEM)
    share = jax.ShapeDtypeStruct((1, 24), WIDE)
    out_shape = [
        jax.ShapeDtypeStruct((1, 2 * SEQ, WIDTH), LOW),
        jax.ShapeDtypeStruct((1, 2 * SEQ, WIDTH), LOW),
        jax.ShapeDtypeStruct((1, 24, FF), WIDE),
        jax.ShapeDtypeStruct((1, ROWS, WIDTH), WIDE),
        share, share, share, share,
        jax.ShapeDtypeStruct((1, 8, WIDTH), WIDE),
    ]
    return pl.pallas_call(
        finish_kernel, out_shape=out_shape, in_specs=[vmem] * 6, out_specs=[vmem] * 9,
        compiler_params=pltpu.CompilerParams(vmem_limit_bytes=62 * 2**20),
    )(*arrays)


def body(
    tokens, doc_ids, region_ids, proj, down, ln_gain, ln_bias, bn_gain, bn_bias, region_table, out_cot
):
    args = dict(
        tokens=tokens.reshape(2, SEQ, WIDTH), doc_ids=doc_ids, region_ids=region_ids, ln_gain=ln_gain,
        ln_bias=ln_bias, bn_gain=bn_gain, bn_bias=bn_bias, table=region_table[0],
        out_cot=out_cot.reshape(2, SEQ, WIDTH),
    )
    return tuple(finish(*run_whole(args, proj, down)))


def solution(mesh):
    in_specs = (
        P("dp", None),
        P("dp", None),
        P("dp", None),
        P("pipe", "dp", None),
        P("pipe", "dp", None),
        P("pipe", None),
        P("pipe", None),
        P("pipe", None),
        P("pipe", None),
        P("pipe", None, None),
        P("dp", None),
    )
    out_specs = (
        P("pipe", "dp", None),
        P("pipe", "dp", None),
        P("pipe", "dp", None),
        P("pipe", "dp", None),
        P("pipe", "dp"),
        P("pipe", "dp"),
        P("pipe", "dp"),
        P("pipe", "dp"),
        P("pipe", "dp", None),
    )
    return jax.shard_map(body, mesh=mesh, in_specs=in_specs, out_specs=out_specs, check_vma=False)
```
